32 devices in a mesh: section: 4 (over y, x), fsdp: 2 (over core), dp: 4 (over z).
Axes of the slice: x: 2, y: 2, z: 4, core: 2. Of those that a mesh axis runs over, the one named last changes fastest.
Arguments:
- inputs: bfloat16 [4, 256, 4096], P(None, ('fsdp', 'dp')), may hold values from -6 to 6
- cotangent: bfloat16 [4, 256, 4096], P(None, ('fsdp', 'dp')), may hold values from -0.09375 to 0.09375
- norm_gain: bfloat16 [4, 4096], P('section', 'fsdp'), may hold values from 0.25 to 1.75
- up_blocks: bfloat16 [4, 128, 128, 128], P('section', 'fsdp'), may hold values from -0.5 to 0.5
- down_blocks: bfloat16 [4, 128, 128, 128], P('section', 'fsdp'), may hold values from -0.25 to 0.25
- up_left: bfloat16 [4, 16, 4096], P('section', None, 'fsdp'), may hold values from -0.09375 to 0.09375
- up_right: bfloat16 [4, 16, 16384], P('section', None, 'fsdp'), may hold values from -1.5 to 1.5
- down_left: bfloat16 [4, 16, 16384], P('section', None, 'fsdp'), may hold values from -0.046875 to 0.046875
- down_right: bfloat16 [4, 16, 4096], P('section', None, 'fsdp'), may hold values from -1.5 to 1.5
- up_pattern: int32 [4, 128], P('section'), may hold values from 0 to 31, as said below
- down_pattern: int32 [4, 128], P('section'), may hold values from 0 to 127, as said below
Outputs:
- grad_norm_gain: float32 [4, 4096], P('section', 'fsdp')
- grad_up_blocks: float32 [4, 128, 128, 128], P('section', 'fsdp')
- grad_down_blocks: float32 [4, 128, 128, 128], P('section', 'fsdp')
- grad_up_left: float32 [4, 16, 4096], P('section', None, 'fsdp')
- grad_up_right: float32 [4, 16, 16384], P('section', None, 'fsdp')
- grad_down_left: float32 [4, 16, 16384], P('section', None, 'fsdp')
- grad_down_right: float32 [4, 16, 4096], P('section', None, 'fsdp')
The draws below stay inside these ranges and needn't reach their ends.
Inputs may be any that keep to these rules, and one draw needn't show every extreme that they name: Each row of up_pattern names every one of the 32 model blocks exactly 4 times. Each row of down_pattern names every one of the 128 hidden blocks exactly once.
All inputs are finite; a program needn't handle non-finite values.
Results may differ from the reference program's by a relative error of at most 0.023.
Values may be sent and summed in bfloat16 or wider, within the bound.
No kernel may reach another device: no remote copies, remote signals or barrier semaphores. Data moves between devices by JAX's collectives and lax.ppermute only.
A program may use at most 192 MiB of HBM per device.

```python
import jax
import jax.numpy as jnp
from jax import lax

D = 4096
FF = 16384
BLOCK = 128
RANK = 16
M = 4
TOK_MB = 32
LAYERS = 4
DB = 32
FB = 128
GROUP = 4
TOKENS = 256
N_FSDP = 2
N_DP = 4


def draw_up_pattern(key, part):
    layer_keys = jax.random.split(jax.random.fold_in(key, 11), LAYERS)
    orders = jax.vmap(lambda layer_key: jax.random.permutation(layer_key, FB))(layer_keys)
    return (orders % DB).astype(jnp.int32)


def draw_down_pattern(key, part):
    layer_keys = jax.random.split(jax.random.fold_in(key, 23), LAYERS)
    orders = jax.vmap(lambda layer_key: jax.random.permutation(layer_key, FB))(layer_keys)
    return orders.astype(jnp.int32)


def shard_levels(rng, dims, pieces, least, high):
    level = 1.0
    for position, blocks in pieces:
        steps = jax.random.uniform(jax.random.fold_in(jax.random.fold_in(rng, 6), position), (blocks,), jnp.float32, least / len(pieces), high / len(pieces))
        level = level * jnp.repeat(jnp.exp(steps), dims[position] // blocks).reshape((-1,) + (1,) * (len(dims) - 1 - position))
    return level


def centred(stream_key, dims, scale, bound, cuts=(), held_as=jnp.bfloat16):
    values = jax.random.normal(stream_key, dims, jnp.float32) * scale
    if len(cuts) > 0:
        values = shard_levels(stream_key, dims, cuts, -0.22, 0.18) * values
    return jnp.clip(values, min=-bound, max=bound).astype(held_as)


def setup_inputs(seed: int = 0) -> dict:
    arg_keys = jax.random.split(jax.random.key(seed), 12)
    inputs = centred(arg_keys[0], (M, TOKENS, D), 1.0, 6.0, ((1, 8),))
    cotangent = centred(arg_keys[1], (M, TOKENS, D), 0.015625, 0.09375, ((1, 8),))
    norm_gain = jnp.clip(1.0 + 0.15 * jax.random.normal(arg_keys[2], (LAYERS, D), jnp.float32), 0.25, 1.75).astype(jnp.bfloat16)
    up_blocks = centred(arg_keys[3], (LAYERS, FB, BLOCK, BLOCK), BLOCK ** -0.5, 0.5, ((0, 4), (1, 2)))
    down_blocks = centred(arg_keys[4], (LAYERS, FB, BLOCK, BLOCK), (GROUP * BLOCK) ** -0.5, 0.25, ((0, 4), (1, 2)))
    up_left = centred(arg_keys[5], (LAYERS, RANK, D), D ** -0.5, 0.09375, ((0, 4), (2, 2)))
    up_right = centred(arg_keys[6], (LAYERS, RANK, FF), RANK ** -0.5, 1.5, ((0, 4), (2, 2)))
    down_left = centred(arg_keys[7], (LAYERS, RANK, FF), FF ** -0.5, 0.046875, ((0, 4), (2, 2)))
    down_right = centred(arg_keys[8], (LAYERS, RANK, D), RANK ** -0.5, 1.5, ((0, 4), (2, 2)))
    up_pattern = draw_up_pattern(jax.random.fold_in(arg_keys[11], 71), 0)
    down_pattern = draw_down_pattern(jax.random.fold_in(arg_keys[11], 71), 0)
    return {"inputs": inputs, "cotangent": cotangent, "norm_gain": norm_gain, "up_blocks": up_blocks, "down_blocks": down_blocks, "up_left": up_left, "up_right": up_right, "down_left": down_left, "down_right": down_right, "up_pattern": up_pattern, "down_pattern": down_pattern}


EPSILON = 1e-05
ROOT_HALF = 0.7071067811865476
NORMAL_PEAK = 0.3989422804014327

def gelu_pair(pre_act):
    normal_cdf = 0.5 * (1.0 + lax.erf(pre_act * ROOT_HALF))
    normal_pdf = jnp.exp(-0.5 * pre_act * pre_act) * NORMAL_PEAK
    return (pre_act * normal_cdf, normal_cdf + pre_act * normal_pdf)

def inverse_order(order):
    positions = jnp.arange(order.shape[0], dtype=jnp.int32)
    matches = order[None, :] == positions[:, None]
    return lax.optimization_barrier(jnp.sum(jnp.where(matches, positions[None, :], 0), axis=1)).astype(jnp.int32)

def layer_forward(layer_in, gain, up_blocks, down_blocks, up_left, up_right, down_left, down_right, up_order, down_order):
    row_count = layer_in.shape[0]
    wide_in = layer_in.astype(jnp.float32)
    inv_rms = lax.rsqrt(lax.optimization_barrier(jnp.mean(wide_in * wide_in, axis=-1, keepdims=True)) + EPSILON)
    normed = (wide_in * inv_rms * gain.astype(jnp.float32)).astype(jnp.bfloat16)
    up_low = jnp.dot(normed, up_left.T, preferred_element_type=jnp.float32).astype(jnp.bfloat16)
    picked = jnp.take(normed.reshape(row_count, DB, BLOCK), up_order, axis=1)
    pre_act = jnp.einsum('rjb,jbe->rje', picked.astype(jnp.float32), up_blocks.astype(jnp.float32)).reshape(row_count, FF)
    pre_act = pre_act + jnp.dot(up_low, up_right, preferred_element_type=jnp.float32)
    hidden = gelu_pair(pre_act)[0].astype(jnp.bfloat16)
    down_low = jnp.dot(hidden, down_left.T, preferred_element_type=jnp.float32).astype(jnp.bfloat16)
    chosen = jnp.take(hidden.reshape(row_count, FB, BLOCK), down_order, axis=1).reshape(row_count, DB, GROUP, BLOCK)
    mixed = jnp.einsum('ricb,icbe->rie', chosen.astype(jnp.float32), down_blocks.reshape(DB, GROUP, BLOCK, BLOCK).astype(jnp.float32)).reshape(row_count, D)
    mixed = mixed + jnp.dot(down_low, down_right, preferred_element_type=jnp.float32)
    return ((wide_in + mixed).astype(jnp.bfloat16), (normed, up_low, pre_act, down_low))

def layer_backward(layer_in, pre_act, grad_out, gain, up_blocks, down_blocks, up_left, up_right, down_left, down_right, fold_map, inverse_down):
    row_count = layer_in.shape[0]
    wide_in = layer_in.astype(jnp.float32)
    inv_rms = lax.rsqrt(lax.optimization_barrier(jnp.mean(wide_in * wide_in, axis=-1, keepdims=True)) + EPSILON)
    hidden, gelu_slope = gelu_pair(pre_act)
    hidden = hidden.astype(jnp.bfloat16)
    grad_down_low = jnp.dot(grad_out, down_right.T, preferred_element_type=jnp.float32).astype(jnp.bfloat16)
    spread = jnp.einsum('rie,icbe->ricb', grad_out.reshape(row_count, DB, BLOCK).astype(jnp.float32), down_blocks.reshape(DB, GROUP, BLOCK, BLOCK).astype(jnp.float32)).reshape(row_count, FB, BLOCK)
    grad_hidden = jnp.take(spread, inverse_down, axis=1).reshape(row_count, FF)
    grad_hidden = grad_hidden + jnp.dot(grad_down_low, down_left, preferred_element_type=jnp.float32)
    grad_pre = (grad_hidden * gelu_slope).astype(jnp.bfloat16)
    grad_up_low = jnp.dot(grad_pre, up_right.T, preferred_element_type=jnp.float32).astype(jnp.bfloat16)
    sent_back = jnp.einsum('rje,jbe->rjb', grad_pre.reshape(row_count, FB, BLOCK).astype(jnp.float32), up_blocks.astype(jnp.float32))
    grad_normed = jnp.einsum('rjb,ji->rib', sent_back, fold_map, precision=lax.Precision.HIGHEST).reshape(row_count, D)
    grad_normed = grad_normed + jnp.dot(grad_up_low, up_left, preferred_element_type=jnp.float32)
    scaled = grad_normed * gain.astype(jnp.float32)
    grad_gain = lax.optimization_barrier(jnp.sum(grad_normed * wide_in * inv_rms, axis=0))
    grad_in = grad_out.astype(jnp.float32) + inv_rms * scaled - wide_in * inv_rms * inv_rms * inv_rms * lax.optimization_barrier(jnp.mean(wide_in * scaled, axis=-1, keepdims=True))
    return (grad_in.astype(jnp.bfloat16), grad_pre, grad_up_low, grad_down_low, hidden, grad_gain)

def weight_terms(normed, up_low, grad_pre, grad_up_low, hidden, down_low, grad_down_low, grad_out, up_order, down_order):
    row_count = normed.shape[0]
    picked = jnp.take(normed.reshape(row_count, DB, BLOCK), up_order, axis=1)
    grad_up = jnp.einsum('rjb,rje->jbe', picked.astype(jnp.float32), grad_pre.reshape(row_count, FB, BLOCK).astype(jnp.float32))
    chosen = jnp.take(hidden.reshape(row_count, FB, BLOCK), down_order, axis=1)
    owner = (jnp.arange(FB, dtype=jnp.int32) // GROUP).astype(jnp.int32)
    spread = jnp.take(grad_out.reshape(row_count, DB, BLOCK), owner, axis=1)
    grad_down = jnp.einsum('rkb,rke->kbe', chosen.astype(jnp.float32), spread.astype(jnp.float32))
    grad_up_left = jnp.dot(grad_up_low.T, normed, preferred_element_type=jnp.float32)
    grad_up_right = jnp.dot(up_low.T, grad_pre, preferred_element_type=jnp.float32)
    grad_down_left = jnp.dot(grad_down_low.T, hidden, preferred_element_type=jnp.float32)
    grad_down_right = jnp.dot(down_low.T, grad_out, preferred_element_type=jnp.float32)
    return (grad_up, grad_down, grad_up_left, grad_up_right, grad_down_left, grad_down_right)

def reference(inputs, cotangent, norm_gain, up_blocks, down_blocks, up_left, up_right, down_left, down_right, up_pattern, down_pattern):
    shard_count = N_FSDP * N_DP
    in_rows = inputs.reshape(M, shard_count, TOK_MB, D).transpose(1, 0, 2, 3).reshape(shard_count, M * TOK_MB, D)
    out_rows = cotangent.reshape(M, shard_count, TOK_MB, D).transpose(1, 0, 2, 3).reshape(shard_count, M * TOK_MB, D)
    block_ids = jnp.arange(DB, dtype=jnp.int32)
    fold_maps = [(up_pattern[layer_index][:, None] == block_ids[None, :]).astype(jnp.float32) for layer_index in range(LAYERS)]
    inverses = [inverse_order(down_pattern[layer_index]) for layer_index in range(LAYERS)]
    zero_totals = (jnp.zeros((LAYERS, FB, BLOCK, BLOCK), jnp.float32), jnp.zeros((LAYERS, FB, BLOCK, BLOCK), jnp.float32), jnp.zeros((LAYERS, RANK, D), jnp.float32), jnp.zeros((LAYERS, RANK, FF), jnp.float32), jnp.zeros((LAYERS, RANK, FF), jnp.float32), jnp.zeros((LAYERS, RANK, D), jnp.float32), jnp.zeros((LAYERS, D), jnp.float32))

    def one_shard(totals, shard_pair):
        layer_in, grad_out = shard_pair
        saved_acts = []
        for layer_index in range(LAYERS):
            layer_out, cache = layer_forward(layer_in, norm_gain[layer_index], up_blocks[layer_index], down_blocks[layer_index], up_left[layer_index], up_right[layer_index], down_left[layer_index], down_right[layer_index], up_pattern[layer_index], down_pattern[layer_index])
            saved_acts.append((layer_in, cache))
            layer_in = layer_out
        per_layer = [None] * LAYERS
        for layer_index in reversed(range(LAYERS)):
            stored_in, cache = saved_acts[layer_index]
            normed, up_low, pre_act, down_low = cache
            grad_in, grad_pre, grad_up_low, grad_down_low, hidden, grad_gain = layer_backward(stored_in, pre_act, grad_out, norm_gain[layer_index], up_blocks[layer_index], down_blocks[layer_index], up_left[layer_index], up_right[layer_index], down_left[layer_index], down_right[layer_index], fold_maps[layer_index], inverses[layer_index])
            layer_terms = weight_terms(normed, up_low, grad_pre, grad_up_low, hidden, down_low, grad_down_low, grad_out, up_pattern[layer_index], down_pattern[layer_index])
            per_layer[layer_index] = layer_terms + (grad_gain,)
            grad_out = grad_in
        stacked = tuple((jnp.stack([per_layer[layer_index][kind_index] for layer_index in range(LAYERS)]) for kind_index in range(7)))
        rounded = tuple((lax.optimization_barrier(term.astype(jnp.bfloat16)).astype(jnp.float32) for term in stacked))
        return (tuple((total_part + new_part for total_part, new_part in zip(totals, rounded))), None)
    totals, _ = lax.scan(one_shard, zero_totals, (in_rows, out_rows))
    return (totals[6], totals[0], totals[1], totals[2], totals[3], totals[4], totals[5])
```

```python
import functools

import jax
import jax.numpy as jnp
from jax import lax
from jax.experimental import pallas as pl
from jax.experimental.pallas import tpu as pltpu
from jax.sharding import PartitionSpec as P

EPSILON = 1e-05
NORMAL_PEAK = 0.3989422804014327
TAIL_SCALE = 0.3
TAIL = (
    0.11962930931947272,
    0.12075380294875883,
    0.09991439682547013,
    0.12855881360857063,
    -0.05367866289105895,
    0.20634847173237508,
    -0.15720038925639956,
    0.03567418525278745,
)
BLK = 128
RANK = 16
BF = jnp.bfloat16
F32 = jnp.float32
NN = (((1,), (0,)), ((), ()))
NT = (((1,), (1,)), ((), ()))
TN = (((0,), (0,)), ((), ()))
ANY = pl.BlockSpec(memory_space=pl.ANY)
SMEM = pl.BlockSpec(memory_space=pltpu.SMEM)


def dot(a, b, dims=NN):
    return lax.dot_general(a, b, dims, preferred_element_type=F32)


def gelu_both(value):
    bell = jnp.exp(-0.5 * value * value)
    denom = 1.0 + TAIL_SCALE * jnp.abs(value)
    guess = pl.reciprocal(denom, approx=True)
    t = guess * (2.0 - denom * guess)
    poly = jnp.full_like(t, TAIL[-1])
    for coef in TAIL[-2::-1]:
        poly = poly * t + coef
    tail = bell * (t * poly)
    cdf = jnp.where(value < 0.0, tail, 1.0 - tail)
    return value * cdf, cdf + value * (bell * NORMAL_PEAK)


class Dims:
    def __init__(self, width, hidden_blocks, parts):
        self.parts = parts
        self.width = width
        self.model = width // BLK
        self.hidden = hidden_blocks
        self.group = hidden_blocks // self.model
        self.mh = self.model // parts
        self.hh = hidden_blocks // parts
        self.ul = 0
        self.dr = self.mh * BLK
        self.ur = 2 * self.mh * BLK
        self.dl = self.ur + self.hh * BLK
        self.gain = self.dl + self.hh * BLK
        self.packed = self.gain + self.mh * BLK


def lanes(start, count=BLK):
    return pl.ds(pl.multiple_of(start, BLK), count)


def load_weights(f, srcs, dsts, sems):
    copies = []
    for n, (src, dst) in enumerate(zip(srcs, dsts)):
        if len(src) == 1:
            whole = pltpu.make_async_copy(src[0], dst, sems.at[2 * n])
            whole.start()
            copies.append((whole,))
            continue
        own, other = src
        half = dst.shape[0] // 2
        if own.ndim < dst.ndim:
            mine, theirs = f, 1 - f
        else:
            mine, theirs = pl.ds(f * half, half), pl.ds((1 - f) * half, half)
        a = pltpu.make_async_copy(own, dst.at[mine], sems.at[2 * n])
        b = pltpu.make_async_copy(other, dst.at[theirs], sems.at[2 * n + 1])
        a.start()
        b.start()
        copies.append((a, b))
    return copies


def done(pair):
    for copy in pair:
        copy.wait()


def inverse_rms(x_s, dims):
    rows = x_s.shape[0]
    total = jnp.zeros((rows, BLK), F32)
    for i in range(dims.model):
        part = x_s[:, i * BLK : (i + 1) * BLK].astype(F32)
        total = total + part * part
    return lax.rsqrt(jnp.sum(total, axis=1, keepdims=True) * (1.0 / dims.width) + EPSILON)


def fwd_body(dims, full, G, copies, f_x_s, small_s, up_s, dn_s, upo, dno, nrm_s, hid_s, slp_s, low_s, y_s):
    x_s = f_x_s
    rows = x_s.shape[0]
    r = inverse_rms(x_s, dims)
    upl = jnp.zeros((rows, RANK), F32)
    for h in range(dims.parts):
        for i in range(dims.mh):
            at = (h * dims.mh + i) * BLK
            gain = small_s[h, 0:1, dims.gain + i * BLK : dims.gain + (i + 1) * BLK].astype(F32)
            nrm_s[:, at : at + BLK] = (x_s[:, at : at + BLK].astype(F32) * r * gain).astype(BF)
        upl = upl + dot(
            nrm_s[:, h * dims.mh * BLK : (h + 1) * dims.mh * BLK],
            small_s[h, :, dims.ul : dims.ul + dims.mh * BLK],
            NT,
        )
    upl = upl.astype(BF)
    low_s[:, 0:RANK] = upl
    done(copies[0])

    def step(it, low):
        j0 = it * G
        h = j0 // dims.hh
        off = (j0 - h * dims.hh) * BLK
        ur = small_s[h, :, lanes(dims.ur + off, G * BLK)]
        dl = small_s[h, :, lanes(dims.dl + off, G * BLK)]
        hids = []
        for g in range(G):
            src = nrm_s[:, lanes(upo[j0 + g] * BLK)]
            lhs = jnp.concatenate([src, upl], axis=1)
            rhs = jnp.concatenate([up_s[j0 + g], ur[:, g * BLK : (g + 1) * BLK]], axis=0)
            hid, slope = gelu_both(dot(lhs, rhs))
            hid = hid.astype(BF)
            hid_s[j0 + g] = hid
            slp_s[j0 + g] = slope.astype(BF)
            hids.append(hid)
        return low + dot(jnp.concatenate(hids, axis=1), dl, NT)

    low = lax.fori_loop(0, dims.hidden // G, step, jnp.zeros((rows, RANK), F32))
    low = low.astype(BF)
    low_s[:, BLK : BLK + RANK] = low
    if full:
        done(copies[1])

        def down(it, _):
            for u in range(4):
                i = it * 4 + u
                h = i // dims.mh
                at = i * BLK
                dr = small_s[h, :, lanes(dims.dr + (i - h * dims.mh) * BLK)]
                parts = [hid_s[dno[i * dims.group + c]] for c in range(dims.group)]
                lhs = jnp.concatenate(parts + [low], axis=1)
                blocks = dn_s[pl.ds(i * dims.group, dims.group)].reshape(dims.group * BLK, BLK)
                mixed = dot(lhs, jnp.concatenate([blocks, dr], axis=0))
                y_s[:, lanes(at)] = (x_s[:, lanes(at)].astype(F32) + mixed).astype(BF)
            return 0

        lax.fori_loop(0, dims.model // 4, down, 0)


def bwd_hidden(dims, g_s, slp_s, gp_s, small_s, dn_s, dno, low_s):
    rows = g_s.shape[0]
    gdl = jnp.zeros((rows, RANK), F32)
    for h in range(dims.parts):
        gdl = gdl + dot(
            g_s[:, h * dims.mh * BLK : (h + 1) * dims.mh * BLK],
            small_s[h, :, dims.dr : dims.dr + dims.mh * BLK],
            NT,
        )
    gdl = gdl.astype(BF)
    low_s[:, BLK : BLK + RANK] = gdl

    def hid_step(it, gul):
        for u in range(2):
            i = it * 2 + u
            gi = g_s[:, lanes(i * BLK)]
            js = [dno[i * dims.group + c] for c in range(dims.group)]
            hs = [j // dims.hh for j in js]
            offs = [(j - h * dims.hh) * BLK for j, h in zip(js, hs)]
            dl = jnp.concatenate([small_s[h, :, lanes(dims.dl + o)] for h, o in zip(hs, offs)], axis=1)
            ur = jnp.concatenate([small_s[h, :, lanes(dims.ur + o)] for h, o in zip(hs, offs)], axis=1)
            blocks = dn_s[pl.ds(i * dims.group, dims.group)].reshape(dims.group * BLK, BLK)
            gh = dot(gi, blocks, NT) + dot(gdl, dl)
            slope = jnp.concatenate([slp_s[j] for j in js], axis=1).astype(F32)
            gp = (gh * slope).astype(BF)
            for c, j in enumerate(js):
                gp_s[j] = gp[:, c * BLK : (c + 1) * BLK]
            gul = gul + dot(gp, ur, NT)
        return gul

    gul = lax.fori_loop(0, dims.model // 2, hid_step, jnp.zeros((rows, RANK), F32))
    gul = gul.astype(BF)
    low_s[:, 0:RANK] = gul
    return gul


def bwd_input(dims, x_s, g_s, gp_s, small_s, up_s, grouped, gul, gn_s, gain_s, out_s):
    rows = g_s.shape[0]
    r = inverse_rms(x_s, dims)

    def step(it, acc):
        for u in range(2):
            i = it * 2 + u
            h = i // dims.mh
            off = (i - h * dims.mh) * BLK
            js = [grouped[i * dims.group + c] for c in range(dims.group)]
            lhs = jnp.concatenate([gp_s[j] for j in js], axis=1)
            rhs = jnp.concatenate([up_s[j] for j in js], axis=1)
            gn = dot(lhs, rhs, NT) + dot(gul, small_s[h, :, lanes(dims.ul + off)])
            x = x_s[:, lanes(i * BLK)].astype(F32)
            gain = small_s[h, 0:1, lanes(dims.gain + off)].astype(F32)
            scaled = gn * gain
            gn_s[:, lanes(i * BLK)] = scaled
            gain_s[0:1, lanes(i * BLK)] = jnp.sum(gn * x * r, axis=0, keepdims=True)
            acc = acc + x * scaled
        return acc

    acc = lax.fori_loop(0, dims.model // 2, step, jnp.zeros((rows, BLK), F32))
    shift = jnp.sum(acc, axis=1, keepdims=True) * (1.0 / dims.width) * (r * r * r)
    for i in range(dims.model):
        at = slice(i * BLK, (i + 1) * BLK)
        out_s[:, at] = (
            g_s[:, at].astype(F32) + r * gn_s[:, at] - x_s[:, at].astype(F32) * shift
        ).astype(BF)


def params(mib):
    return pltpu.CompilerParams(vmem_limit_bytes=mib * 1024 * 1024)


def fwd_slot(dims, sc, upo, dno, first, recv, weights, bufs, micro):
    rows = recv.shape[0]
    n_buf = 5
    shapes = (
        jax.ShapeDtypeStruct((micro, dims.hidden, rows, BLK), BF),
        jax.ShapeDtypeStruct((micro, dims.hidden, rows, BLK), BF),
        jax.ShapeDtypeStruct((micro, rows, dims.width), BF),
        jax.ShapeDtypeStruct((micro, rows, dims.width), BF),
        jax.ShapeDtypeStruct((micro, rows, 2 * BLK), BF),
    )
    n_w = len(weights[0])
    n_in = 5 + 3 * n_w + (n_buf if bufs is not None else 0)

    def kernel(*refs):
        sc, upo, dno, first, recv = refs[:5]
        up_w, dn_w, small_w = (refs[5 + k * n_w : 5 + (k + 1) * n_w] for k in range(3))
        y, hidb, slpb, nrmb, xb, lowb = refs[n_in : n_in + 6]
        up_s, dn_s, small_s, x_s, nrm_s, hid_s, slp_s, low_s, y_s, sems = refs[n_in + 6 :]

        @pl.when(sc[0] == 1)
        def _():
            m, f = sc[1], sc[2]

            @pl.when(sc[3] == 1)
            def _():
                pltpu.make_async_copy(first.at[m], x_s, sems.at[6]).start()

            @pl.when(sc[3] == 0)
            def _():
                pltpu.make_async_copy(recv, x_s, sems.at[6]).start()

            wait_x = pltpu.make_async_copy(recv, x_s, sems.at[6])
            small, up, dn = load_weights(
                f, (small_w, up_w, dn_w), (small_s, up_s, dn_s), sems
            )
            low_s[...] = jnp.zeros_like(low_s)
            wait_x.wait()
            save_x = pltpu.make_async_copy(x_s, xb.at[m], sems.at[7])
            save_x.start()
            done(small)
            fwd_body(dims, True, 8, (up, dn), x_s, small_s, up_s, dn_s, upo, dno, nrm_s, hid_s, slp_s, low_s, y_s)
            outs = [
                pltpu.make_async_copy(y_s, y, sems.at[8]),
                pltpu.make_async_copy(hid_s, hidb.at[m], sems.at[9]),
                pltpu.make_async_copy(slp_s, slpb.at[m], sems.at[10]),
                pltpu.make_async_copy(nrm_s, nrmb.at[m], sems.at[11]),
                pltpu.make_async_copy(low_s, lowb.at[m], sems.at[12]),
            ]
            for copy in outs:
                copy.start()
            save_x.wait()
            done(outs)

    args = [sc, upo, dno, first, recv] + [w for pair in weights for w in pair]
    aliases = {}
    if bufs is not None:
        aliases = {len(args) + n: n + 1 for n in range(n_buf)}
        args += list(bufs)
    out = pl.pallas_call(
        kernel,
        out_shape=(jax.ShapeDtypeStruct((rows, dims.width), BF),) + shapes,
        in_specs=[SMEM] * 3 + [ANY] * (len(args) - 3),
        out_specs=(ANY,) * 6,
        input_output_aliases=aliases,
        scratch_shapes=[
            pltpu.VMEM((dims.hidden, BLK, BLK), BF),
            pltpu.VMEM((dims.hidden, BLK, BLK), BF),
            pltpu.VMEM((dims.parts, RANK, dims.packed), BF),
            pltpu.VMEM((rows, dims.width), BF),
            pltpu.VMEM((rows, dims.width), BF),
            pltpu.VMEM((dims.hidden, rows, BLK), BF),
            pltpu.VMEM((dims.hidden, rows, BLK), BF),
            pltpu.VMEM((rows, 2 * BLK), BF),
            pltpu.VMEM((rows, dims.width), BF),
            pltpu.SemaphoreType.DMA((13,)),
        ],
        compiler_params=params(40),
        name="forward_rows",
    )(*args)
    return out[0], out[1:]


def bwd_slot(dims, sc, dno, grouped, last, recv, weights, xb, slpb, bufs, micro):
    rows = recv.shape[0]
    n_buf = 4
    shapes = (
        jax.ShapeDtypeStruct((micro, dims.hidden, rows, BLK), BF),
        jax.ShapeDtypeStruct((micro, rows, dims.width), BF),
        jax.ShapeDtypeStruct((micro, rows, 2 * BLK), BF),
        jax.ShapeDtypeStruct((micro, 8, dims.width), F32),
    )
    n_w = len(weights[0])
    n_in = 7 + 3 * n_w + (n_buf if bufs is not None else 0)

    def kernel(*refs):
        sc, dno, grouped, last, recv = refs[:5]
        up_w, dn_w, small_w = (refs[5 + k * n_w : 5 + (k + 1) * n_w] for k in range(3))
        xb, slpb = refs[5 + 3 * n_w : 7 + 3 * n_w]
        out, gpb, gb, lowb, gainb = refs[n_in : n_in + 5]
        up_s, dn_s, small_s, x_s, g_s, slp_s, gp_s, low_s, gn_s, gain_s, out_s, sems = refs[n_in + 5 :]

        @pl.when(sc[0] == 1)
        def _():
            m, f = sc[1], sc[2]

            @pl.when(sc[3] == 1)
            def _():
                pltpu.make_async_copy(last.at[m], g_s, sems.at[6]).start()

            @pl.when(sc[3] == 0)
            def _():
                pltpu.make_async_copy(recv, g_s, sems.at[6]).start()

            wait_g = pltpu.make_async_copy(recv, g_s, sems.at[6])
            get_slope = pltpu.make_async_copy(slpb.at[m], slp_s, sems.at[7])
            get_x = pltpu.make_async_copy(xb.at[m], x_s, sems.at[8])
            small, dn, up = load_weights(
                f, (small_w, dn_w, up_w), (small_s, dn_s, up_s), sems
            )
            get_slope.start()
            get_x.start()
            low_s[...] = jnp.zeros_like(low_s)
            gain_s[...] = jnp.zeros_like(gain_s)
            wait_g.wait()
            save_g = pltpu.make_async_copy(g_s, gb.at[m], sems.at[9])
            save_g.start()
            done(small)
            get_slope.wait()
            done(dn)
            gul = bwd_hidden(dims, g_s, slp_s, gp_s, small_s, dn_s, dno, low_s)
            outs = [
                pltpu.make_async_copy(gp_s, gpb.at[m], sems.at[10]),
                pltpu.make_async_copy(low_s, lowb.at[m], sems.at[11]),
            ]
            for copy in outs:
                copy.start()
            get_x.wait()
            done(up)
            bwd_input(dims, x_s, g_s, gp_s, small_s, up_s, grouped, gul, gn_s, gain_s, out_s)
            more = [
                pltpu.make_async_copy(gain_s, gainb.at[m], sems.at[12]),
                pltpu.make_async_copy(out_s, out, sems.at[13]),
            ]
            for copy in more:
                copy.start()
            save_g.wait()
            done(outs)
            done(more)

    args = [sc, dno, grouped, last, recv] + [w for pair in weights for w in pair] + [xb, slpb]
    aliases = {}
    if bufs is not None:
        aliases = {len(args) + n: n + 1 for n in range(n_buf)}
        args += list(bufs)
    out = pl.pallas_call(
        kernel,
        out_shape=(jax.ShapeDtypeStruct((rows, dims.width), BF),) + shapes,
        in_specs=[SMEM] * 3 + [ANY] * (len(args) - 3),
        out_specs=(ANY,) * 5,
        input_output_aliases=aliases,
        scratch_shapes=[
            pltpu.VMEM((dims.hidden, BLK, BLK), BF),
            pltpu.VMEM((dims.hidden, BLK, BLK), BF),
            pltpu.VMEM((dims.parts, RANK, dims.packed), BF),
            pltpu.VMEM((rows, dims.width), BF),
            pltpu.VMEM((rows, dims.width), BF),
            pltpu.VMEM((dims.hidden, rows, BLK), BF),
            pltpu.VMEM((dims.hidden, rows, BLK), BF),
            pltpu.VMEM((rows, 2 * BLK), BF),
            pltpu.VMEM((rows, dims.width), F32),
            pltpu.VMEM((8, dims.width), F32),
            pltpu.VMEM((rows, dims.width), BF),
            pltpu.SemaphoreType.DMA((14,)),
        ],
        compiler_params=params(40),
        name="backward_rows",
    )(*args)
    return out[0], out[1:]


def weight_grads(dims, sc, upo, dno, hidb, nrmb, lowf, gpb, gb, lowb, gainb):
    micro, _, rows, _ = hidb.shape
    VM = pl.BlockSpec(memory_space=pltpu.VMEM)

    two = dims.parts == 2

    def kernel(*refs):
        sc, upo, dno, hidb, nrmb, lowf, gpb, gb, lowb, gainb = refs[:10]
        outs_hbm = refs[10:-4]
        upg, dng, smg, sems = refs[-4:]
        f = sc[2]

        def cat(parts):
            return jnp.concatenate(parts, axis=0)

        def rows_of(ref, at, count=BLK):
            return cat([ref[m, :, lanes(at, count)] for m in range(micro)])

        def block_of(ref, j):
            return cat([ref[m, j] for m in range(micro)])

        up_low = cat([lowf[m, :, 0:BLK] for m in range(micro)])
        down_low = cat([lowf[m, :, BLK : 2 * BLK] for m in range(micro)])
        gul = cat([lowb[m, :, 0:BLK] for m in range(micro)])
        gdl = cat([lowb[m, :, BLK : 2 * BLK] for m in range(micro)])

        def which(h):
            return jnp.where(h == f, 0, 1) if two else h

        def down(it, _):
            for u in range(2):
                i = it * 2 + u
                h = i // dims.mh
                hid = jnp.concatenate(
                    [block_of(hidb, dno[i * dims.group + c]) for c in range(dims.group)], axis=1
                )
                gi = rows_of(gb, i * BLK)
                grad = dot(hid, gi, TN).astype(BF).reshape(dims.group, BLK, BLK)
                off = i - h * dims.mh
                w = which(h)
                dng[w, pl.ds(off * dims.group, dims.group)] = grad
                nrm = rows_of(nrmb, i * BLK)
                smg[w, :, lanes(dims.dr + off * BLK)] = dot(down_low, gi, TN)[0:RANK].astype(BF)
                smg[w, :, lanes(dims.ul + off * BLK)] = dot(gul, nrm, TN)[0:RANK].astype(BF)
                gain = jnp.zeros((8, BLK), F32)
                for m in range(micro):
                    gain = gain + gainb[m, :, lanes(i * BLK)]
                smg[w, :, lanes(dims.gain + off * BLK)] = jnp.broadcast_to(
                    jnp.sum(gain, axis=0, keepdims=True), (RANK, BLK)
                ).astype(BF)
            return 0

        lax.fori_loop(0, dims.model // 2, down, 0)

        def up(it, _):
            for u in range(4):
                j = it * 4 + u
                h = j // dims.hh
                off = j - h * dims.hh
                w = which(h)
                gp = block_of(gpb, j)
                hid = block_of(hidb, j)
                nrm = rows_of(nrmb, upo[j] * BLK)
                upg[w, off] = dot(nrm, gp, TN).astype(BF)
                smg[w, :, lanes(dims.ur + off * BLK)] = dot(up_low, gp, TN)[0:RANK].astype(BF)
                smg[w, :, lanes(dims.dl + off * BLK)] = dot(gdl, hid, TN)[0:RANK].astype(BF)
            return 0

        lax.fori_loop(0, dims.hidden // 4, up, 0)
        outs = []
        for n, src in enumerate((upg, dng, smg)):
            if two:
                outs.append(pltpu.make_async_copy(src.at[0], outs_hbm[2 * n], sems.at[2 * n]))
                outs.append(pltpu.make_async_copy(src.at[1], outs_hbm[2 * n + 1], sems.at[2 * n + 1]))
            else:
                outs.append(pltpu.make_async_copy(src, outs_hbm[n], sems.at[2 * n]))
        for copy in outs:
            copy.start()
        done(outs)

    lead = () if two else (dims.parts,)
    shapes = [lead + (dims.hh, BLK, BLK)] * 2 + [lead + (RANK, dims.packed)]
    shapes = [jax.ShapeDtypeStruct(shape, BF) for shape in shapes for _ in range(2 if two else 1)]
    got = pl.pallas_call(
        kernel,
        out_shape=tuple(shapes),
        in_specs=[SMEM] * 3 + [VM] * 7,
        out_specs=(ANY,) * len(shapes),
        scratch_shapes=[
            pltpu.VMEM((dims.parts, dims.hh, BLK, BLK), BF),
            pltpu.VMEM((dims.parts, dims.hh, BLK, BLK), BF),
            pltpu.VMEM((dims.parts, RANK, dims.packed), BF),
            pltpu.SemaphoreType.DMA((6,)),
        ],
        compiler_params=params(48),
        name="weight_gradients",
    )(sc, upo, dno, hidb, nrmb, lowf, gpb, gb, lowb, gainb)
    return [got[0:2], got[2:4], got[4:6]] if two else [got[0:1], got[1:2], got[2:3]]


def orders(up_order, down_order, dims):
    at = jnp.arange(dims.hidden, dtype=jnp.int32)
    same = (up_order[:, None] == up_order[None, :]) & (at[None, :] < at[:, None])
    place = up_order * dims.group + jnp.sum(same.astype(jnp.int32), axis=1)
    hit = place[None, :] == at[:, None]
    return jnp.sum(jnp.where(hit, at[None, :], 0), axis=1)


def shards(inputs, cotangent, norm_gain, up_blocks, down_blocks, up_left, up_right, down_left, down_right,
           up_pattern, down_pattern):
    micro, rows, width = inputs.shape
    upo, dno = up_pattern[0], down_pattern[0]
    parts = lax.axis_size("fsdp")
    dims = Dims(width, upo.shape[0], parts)
    n_sec = lax.axis_size("section")
    sec = lax.axis_index("section")
    f = lax.axis_index("fsdp")
    swap = [(0, 1), (1, 0)]
    small = jnp.concatenate(
        [up_left[0], down_right[0], up_right[0], down_left[0],
         jnp.broadcast_to(norm_gain, (RANK, norm_gain.shape[1]))], axis=1)

    def whole_layer(own, stacked):
        if parts == 2:
            return (own, lax.ppermute(own, "fsdp", swap))
        return (lax.all_gather(own, "fsdp", axis=0, tiled=not stacked),)

    small_w = whole_layer(small, True)
    up_w = whole_layer(up_blocks[0], False)
    weights = (up_w, whole_layer(down_blocks[0], False), small_w)
    grouped = orders(upo, dno, dims)
    zero = jnp.int32(0)

    def scalars(m, edge):
        live = (m >= 0) & (m < micro)
        return jnp.stack([live.astype(jnp.int32), jnp.clip(m, 0, micro - 1).astype(jnp.int32),
                          f.astype(jnp.int32), edge.astype(jnp.int32), zero, zero, zero, zero])

    state = {"token": None}

    def chained(*arrays):
        if state["token"] is None:
            return arrays
        out = lax.optimization_barrier(arrays + (state["token"],))
        return out[:-1]

    fbufs, bbufs = None, None
    frecv = inputs[0]
    brecv = inputs[0]
    last = n_sec - 1

    def forward(t):
        nonlocal fbufs, frecv
        (x,) = chained(frecv)
        y, fbufs = fwd_slot(dims, scalars(t - sec, sec == 0), upo, dno, inputs, x, weights, fbufs, micro)
        state["token"] = y
        pairs = [(s, s + 1) for s in range(last) if 0 <= t - s < micro]
        if pairs:
            frecv = lax.ppermute(y, "section", pairs)

    def backward(t):
        nonlocal bbufs, brecv
        (g,) = chained(brecv)
        out, bbufs = bwd_slot(dims, scalars(t - (last - sec), sec == last), dno, grouped, cotangent, g,
                              weights, fbufs[3], fbufs[1], bbufs, micro)
        state["token"] = out
        pairs = [(last - s, last - s - 1) for s in range(last) if 0 <= t - s < micro]
        if pairs:
            brecv = lax.ppermute(out, "section", pairs)

    slots = micro + last
    for t in range(slots):
        forward(t)
        if t >= last:
            backward(t - last)
    for t in range(slots - last, slots):
        backward(t)
    up_g, dn_g, small_g = weight_grads(
        dims, scalars(zero, sec == 0), upo, dno, fbufs[0], fbufs[2], fbufs[4], *bbufs)

    def total(pieces):
        if parts == 2:
            got = lax.ppermute(pieces[1], "fsdp", swap)
            both = (pieces[0].astype(F32) + got.astype(F32)).astype(BF)
        else:
            both = lax.psum_scatter(pieces[0], "fsdp", scatter_dimension=0, tiled=False)
        return lax.psum(both, "dp").astype(F32)

    sm = total(small_g)
    dn = total(dn_g)
    up = total(up_g)
    mw, hw = dims.mh * BLK, dims.hh * BLK
    return (
        sm[0:1, dims.gain : dims.gain + mw],
        up[None],
        dn[None],
        sm[None, :, dims.ul : dims.ul + mw],
        sm[None, :, dims.ur : dims.ur + hw],
        sm[None, :, dims.dl : dims.dl + hw],
        sm[None, :, dims.dr : dims.dr + mw],
    )


def solution(mesh):
    placed = (
        P(None, ("fsdp", "dp"), None),
        P(None, ("fsdp", "dp"), None),
        P("section", "fsdp"),
        P("section", "fsdp", None, None),
        P("section", "fsdp", None, None),
        P("section", None, "fsdp"),
        P("section", None, "fsdp"),
        P("section", None, "fsdp"),
        P("section", None, "fsdp"),
        P("section", None),
        P("section", None),
    )
    return jax.shard_map(
        shards,
        mesh=mesh,
        in_specs=placed,
        out_specs=(
            P("section", "fsdp"),
            P("section", "fsdp", None, None),
            P("section", "fsdp", None, None),
            P("section", None, "fsdp"),
            P("section", None, "fsdp"),
            P("section", None, "fsdp"),
            P("section", None, "fsdp"),
        ),
        check_vma=False,
    )
```

```python
import functools

import jax
import jax.numpy as jnp
from jax import lax
from jax.experimental import pallas as pl
from jax.experimental.pallas import tpu as pltpu
from jax.sharding import PartitionSpec as P

EPSILON = 1e-05
NORMAL_PEAK = 0.3989422804014327
TAIL_SCALE = 0.3
TAIL = (
    0.11962930931947272,
    0.12075380294875883,
    0.09991439682547013,
    0.12855881360857063,
    -0.05367866289105895,
    0.20634847173237508,
    -0.15720038925639956,
    0.03567418525278745,
)
BLK = 128
RANK = 16
BF = jnp.bfloat16
F32 = jnp.float32
NN = (((1,), (0,)), ((), ()))
NT = (((1,), (1,)), ((), ()))
TN = (((0,), (0,)), ((), ()))
ANY = pl.BlockSpec(memory_space=pl.ANY)
SMEM = pl.BlockSpec(memory_space=pltpu.SMEM)


def dot(a, b, dims=NN):
    return lax.dot_general(a, b, dims, preferred_element_type=F32)


def gelu_both(value):
    bell = jnp.exp(-0.5 * value * value)
    denom = 1.0 + TAIL_SCALE * jnp.abs(value)
    guess = pl.reciprocal(denom, approx=True)
    t = guess * (2.0 - denom * guess)
    poly = jnp.full_like(t, TAIL[-1])
    for coef in TAIL[-2::-1]:
        poly = poly * t + coef
    tail = bell * (t * poly)
    cdf = jnp.where(value < 0.0, tail, 1.0 - tail)
    return value * cdf, cdf + value * (bell * NORMAL_PEAK)


class Dims:
    def __init__(self, width, hidden_blocks, parts):
        self.parts = parts
        self.width = width
        self.model = width // BLK
        self.hidden = hidden_blocks
        self.group = hidden_blocks // self.model
        self.mh = self.model // parts
        self.hh = hidden_blocks // parts
        self.ul = 0
        self.dr = self.mh * BLK
        self.ur = 2 * self.mh * BLK
        self.dl = self.ur + self.hh * BLK
        self.gain = self.dl + self.hh * BLK
        self.packed = self.gain + self.mh * BLK


def lanes(start, count=BLK):
    return pl.ds(pl.multiple_of(start, BLK), count)


def load_weights(f, srcs, dsts, sems, first=0):
    copies = []
    for n, (src, dst) in enumerate(zip(srcs, dsts), first):
        if len(src) == 1:
            whole = pltpu.make_async_copy(src[0], dst, sems.at[2 * n])
            whole.start()
            copies.append((whole,))
            continue
        own, other = src
        half = dst.shape[0] // 2
        if own.ndim < dst.ndim:
            mine, theirs = f, 1 - f
        else:
            mine, theirs = pl.ds(f * half, half), pl.ds((1 - f) * half, half)
        a = pltpu.make_async_copy(own, dst.at[mine], sems.at[2 * n])
        b = pltpu.make_async_copy(other, dst.at[theirs], sems.at[2 * n + 1])
        a.start()
        b.start()
        copies.append((a, b))
    return copies


def done(pair):
    for copy in pair:
        copy.wait()


def inverse_rms(x_s, dims):
    rows = x_s.shape[0]
    total = jnp.zeros((rows, BLK), F32)
    for i in range(dims.model):
        part = x_s[:, i * BLK : (i + 1) * BLK].astype(F32)
        total = total + part * part
    return lax.rsqrt(jnp.sum(total, axis=1, keepdims=True) * (1.0 / dims.width) + EPSILON)


def fwd_norm(dims, x_s, small_s, nrm_s, low_s):
    rows = x_s.shape[0]
    r = inverse_rms(x_s, dims)
    upl = jnp.zeros((rows, RANK), F32)
    for h in range(dims.parts):
        for i in range(dims.mh):
            at = (h * dims.mh + i) * BLK
            gain = small_s[h, 0:1, dims.gain + i * BLK : dims.gain + (i + 1) * BLK].astype(F32)
            nrm_s[:, at : at + BLK] = (x_s[:, at : at + BLK].astype(F32) * r * gain).astype(BF)
        upl = upl + dot(
            nrm_s[:, h * dims.mh * BLK : (h + 1) * dims.mh * BLK],
            small_s[h, :, dims.ul : dims.ul + dims.mh * BLK],
            NT,
        )
    low_s[:, 0:RANK] = upl.astype(BF)


def fwd_hidden(dims, small_s, up_s, upo, nrm_s, hid_s, slp_s, low_s, G=32):
    rows = nrm_s.shape[0]
    G = min(G, dims.hh)
    upl = low_s[:, 0:RANK]

    def step(it, low):
        j0 = it * G
        h = j0 // dims.hh
        off = (j0 - h * dims.hh) * BLK
        ur = small_s[h, :, lanes(dims.ur + off, G * BLK)]
        dl = small_s[h, :, lanes(dims.dl + off, G * BLK)]
        hids = []
        for g in range(G):
            src = nrm_s[:, lanes(upo[j0 + g] * BLK)]
            lhs = jnp.concatenate([src, upl], axis=1)
            rhs = jnp.concatenate([up_s[j0 + g], ur[:, g * BLK : (g + 1) * BLK]], axis=0)
            hid, slope = gelu_both(dot(lhs, rhs))
            hid = hid.astype(BF)
            hid_s[j0 + g] = hid
            slp_s[j0 + g] = slope.astype(BF)
            hids.append(hid)
        return low + dot(jnp.concatenate(hids, axis=1), dl, NT)

    low = lax.fori_loop(0, dims.hidden // G, step, jnp.zeros((rows, RANK), F32)).astype(BF)
    low_s[:, BLK : BLK + RANK] = low
    return low


def fwd_down(dims, low, x_s, small_s, dn_s, dno, hid_s, y_s):
    def down(it, _):
        for u in range(8):
            i = it * 8 + u
            h = i // dims.mh
            at = i * BLK
            dr = small_s[h, :, lanes(dims.dr + (i - h * dims.mh) * BLK)]
            parts = [hid_s[dno[i * dims.group + c]] for c in range(dims.group)]
            lhs = jnp.concatenate(parts + [low], axis=1)
            blocks = dn_s[pl.ds(i * dims.group, dims.group)].reshape(dims.group * BLK, BLK)
            mixed = dot(lhs, jnp.concatenate([blocks, dr], axis=0))
            y_s[:, lanes(at)] = (x_s[:, lanes(at)].astype(F32) + mixed).astype(BF)
        return 0

    lax.fori_loop(0, dims.model // 8, down, 0)


def bwd_hidden(dims, g_s, slp_s, gp_s, small_s, dn_s, dno, low_s, U=8):
    rows = g_s.shape[0]
    gdl = jnp.zeros((rows, RANK), F32)
    for h in range(dims.parts):
        gdl = gdl + dot(
            g_s[:, h * dims.mh * BLK : (h + 1) * dims.mh * BLK],
            small_s[h, :, dims.dr : dims.dr + dims.mh * BLK],
            NT,
        )
    gdl = gdl.astype(BF)
    low_s[:, BLK : BLK + RANK] = gdl

    def hid_step(it, gul):
        for u in range(U):
            i = it * U + u
            gi = g_s[:, lanes(i * BLK)]
            js = [dno[i * dims.group + c] for c in range(dims.group)]
            hs = [j // dims.hh for j in js]
            offs = [(j - h * dims.hh) * BLK for j, h in zip(js, hs)]
            dl = jnp.concatenate([small_s[h, :, lanes(dims.dl + o)] for h, o in zip(hs, offs)], axis=1)
            ur = jnp.concatenate([small_s[h, :, lanes(dims.ur + o)] for h, o in zip(hs, offs)], axis=1)
            blocks = dn_s[pl.ds(i * dims.group, dims.group)].reshape(dims.group * BLK, BLK)
            gh = dot(gi, blocks, NT) + dot(gdl, dl)
            slope = jnp.concatenate([slp_s[j] for j in js], axis=1).astype(F32)
            gp = (gh * slope).astype(BF)
            for c, j in enumerate(js):
                gp_s[j] = gp[:, c * BLK : (c + 1) * BLK]
            gul = gul + dot(gp, ur, NT)
        return gul

    gul = lax.fori_loop(0, dims.model // U, hid_step, jnp.zeros((rows, RANK), F32))
    gul = gul.astype(BF)
    low_s[:, 0:RANK] = gul
    return gul


def bwd_input(dims, x_s, g_s, gp_s, small_s, up_s, grouped, gul, gn_s, gain_s, out_s):
    rows = g_s.shape[0]
    r = inverse_rms(x_s, dims)

    def step(it, acc):
        for u in range(8):
            i = it * 8 + u
            h = i // dims.mh
            off = (i - h * dims.mh) * BLK
            js = [grouped[i * dims.group + c] for c in range(dims.group)]
            lhs = jnp.concatenate([gp_s[j] for j in js], axis=1)
            rhs = jnp.concatenate([up_s[j] for j in js], axis=1)
            gn = dot(lhs, rhs, NT) + dot(gul, small_s[h, :, lanes(dims.ul + off)])
            x = x_s[:, lanes(i * BLK)].astype(F32)
            gain = small_s[h, 0:1, lanes(dims.gain + off)].astype(F32)
            scaled = gn * gain
            gn_s[:, lanes(i * BLK)] = scaled
            gain_s[0:1, lanes(i * BLK)] = jnp.sum(gn * x * r, axis=0, keepdims=True)
            acc = acc + x * scaled
        return acc

    acc = lax.fori_loop(0, dims.model // 8, step, jnp.zeros((rows, BLK), F32))
    shift = jnp.sum(acc, axis=1, keepdims=True) * (1.0 / dims.width) * (r * r * r)
    for i in range(dims.model):
        at = slice(i * BLK, (i + 1) * BLK)
        out_s[:, at] = (
            g_s[:, at].astype(F32) + r * gn_s[:, at] - x_s[:, at].astype(F32) * shift
        ).astype(BF)


def params(mib):
    return pltpu.CompilerParams(vmem_limit_bytes=mib * 1024 * 1024)


def fwd_slot(dims, sc, upo, dno, first, recv, weights, bufs, micro, held):
    rows = recv.shape[0]
    n_buf = 5
    shapes = (
        jax.ShapeDtypeStruct((micro, dims.hidden, held, BLK), BF),
        jax.ShapeDtypeStruct((micro, dims.hidden, held, BLK), BF),
        jax.ShapeDtypeStruct((micro, held, dims.width), BF),
        jax.ShapeDtypeStruct((micro, rows, dims.width), BF),
        jax.ShapeDtypeStruct((micro, held, 2 * BLK), BF),
    )
    n_w = len(weights[0])
    n_in = 5 + 3 * n_w + (n_buf if bufs is not None else 0)

    def kernel(*refs):
        sc, upo, dno, first, recv = refs[:5]
        up_w, dn_w, small_w = (refs[5 + k * n_w : 5 + (k + 1) * n_w] for k in range(3))
        y, hidb, slpb, nrmb, xb, lowb = refs[n_in : n_in + 6]
        up_s, dn_s, small_s, x_s, nrm_s, hid_s, slp_s, low_s, y_s, sems = refs[n_in + 6 :]

        @pl.when(sc[0] == 1)
        def _():
            m, f = sc[1], sc[2]

            @pl.when(sc[3] == 1)
            def _():
                pltpu.make_async_copy(first.at[m], x_s, sems.at[6]).start()

            @pl.when(sc[3] == 0)
            def _():
                pltpu.make_async_copy(recv, x_s, sems.at[6]).start()

            wait_x = pltpu.make_async_copy(recv, x_s, sems.at[6])
            small, up = load_weights(f, (small_w, up_w), (small_s, up_s), sems)
            low_s[...] = jnp.zeros_like(low_s)
            wait_x.wait()
            save_x = pltpu.make_async_copy(x_s, xb.at[m], sems.at[7])
            save_x.start()
            done(small)
            fwd_norm(dims, x_s, small_s, nrm_s, low_s)
            done(up)
            (dn,) = load_weights(f, (dn_w,), (dn_s,), sems, 2)
            low = fwd_hidden(dims, small_s, up_s, upo, nrm_s, hid_s, slp_s, low_s)
            outs = [
                pltpu.make_async_copy(hid_s, hidb.at[m, :, 0:rows], sems.at[9]),
                pltpu.make_async_copy(slp_s, slpb.at[m, :, 0:rows], sems.at[10]),
                pltpu.make_async_copy(nrm_s, nrmb.at[m, 0:rows], sems.at[11]),
                pltpu.make_async_copy(low_s, lowb.at[m, 0:rows], sems.at[12]),
            ]
            for copy in outs:
                copy.start()
            done(dn)
            fwd_down(dims, low, x_s, small_s, dn_s, dno, hid_s, y_s)
            outs.append(pltpu.make_async_copy(y_s, y, sems.at[8]))
            outs[-1].start()
            save_x.wait()
            done(outs)

    args = [sc, upo, dno, first, recv] + [w for pair in weights for w in pair]
    aliases = {}
    if bufs is not None:
        aliases = {len(args) + n: n + 1 for n in range(n_buf)}
        args += list(bufs)
    out = pl.pallas_call(
        kernel,
        out_shape=(jax.ShapeDtypeStruct((rows, dims.width), BF),) + shapes,
        in_specs=[SMEM] * 3 + [ANY] * (len(args) - 3),
        out_specs=(ANY,) * 6,
        input_output_aliases=aliases,
        scratch_shapes=[
            pltpu.VMEM((dims.hidden, BLK, BLK), BF),
            pltpu.VMEM((dims.hidden, BLK, BLK), BF),
            pltpu.VMEM((dims.parts, RANK, dims.packed), BF),
            pltpu.VMEM((rows, dims.width), BF),
            pltpu.VMEM((rows, dims.width), BF),
            pltpu.VMEM((dims.hidden, rows, BLK), BF),
            pltpu.VMEM((dims.hidden, rows, BLK), BF),
            pltpu.VMEM((rows, 2 * BLK), BF),
            pltpu.VMEM((rows, dims.width), BF),
            pltpu.SemaphoreType.DMA((13,)),
        ],
        compiler_params=params(60),
        name="forward_rows",
    )(*args)
    return out[0], out[1:]


def bwd_slot(dims, sc, dno, grouped, last, recv, weights, xb, slpb, bufs, micro, held):
    rows = recv.shape[0]
    n_buf = 4
    shapes = (
        jax.ShapeDtypeStruct((micro, dims.hidden, held, BLK), BF),
        jax.ShapeDtypeStruct((micro, held, dims.width), BF),
        jax.ShapeDtypeStruct((micro, held, 2 * BLK), BF),
        jax.ShapeDtypeStruct((micro, 8, dims.width), F32),
    )
    n_w = len(weights[0])
    n_in = 7 + 3 * n_w + (n_buf if bufs is not None else 0)

    def kernel(*refs):
        sc, dno, grouped, last, recv = refs[:5]
        up_w, dn_w, small_w = (refs[5 + k * n_w : 5 + (k + 1) * n_w] for k in range(3))
        xb, slpb = refs[5 + 3 * n_w : 7 + 3 * n_w]
        out, gpb, gb, lowb, gainb = refs[n_in : n_in + 5]
        up_s, dn_s, small_s, x_s, g_s, slp_s, gp_s, low_s, gn_s, gain_s, out_s, sems = refs[n_in + 5 :]

        @pl.when(sc[0] == 1)
        def _():
            m, f = sc[1], sc[2]

            @pl.when(sc[3] == 1)
            def _():
                pltpu.make_async_copy(last.at[m], g_s, sems.at[6]).start()

            @pl.when(sc[3] == 0)
            def _():
                pltpu.make_async_copy(recv, g_s, sems.at[6]).start()

            wait_g = pltpu.make_async_copy(recv, g_s, sems.at[6])
            get_slope = pltpu.make_async_copy(slpb.at[m, :, 0:rows], slp_s, sems.at[7])
            get_x = pltpu.make_async_copy(xb.at[m], x_s, sems.at[8])
            small, dn = load_weights(f, (small_w, dn_w), (small_s, dn_s), sems)
            get_slope.start()
            low_s[...] = jnp.zeros_like(low_s)
            gain_s[...] = jnp.zeros_like(gain_s)
            wait_g.wait()
            save_g = pltpu.make_async_copy(g_s, gb.at[m, 0:rows], sems.at[9])
            save_g.start()
            done(small)
            get_slope.wait()
            done(dn)
            (up,) = load_weights(f, (up_w,), (up_s,), sems, 2)
            get_x.start()
            gul = bwd_hidden(dims, g_s, slp_s, gp_s, small_s, dn_s, dno, low_s)
            outs = [
                pltpu.make_async_copy(gp_s, gpb.at[m, :, 0:rows], sems.at[10]),
                pltpu.make_async_copy(low_s, lowb.at[m, 0:rows], sems.at[11]),
            ]
            for copy in outs:
                copy.start()
            get_x.wait()
            done(up)
            bwd_input(dims, x_s, g_s, gp_s, small_s, up_s, grouped, gul, gn_s, gain_s, out_s)
            more = [
                pltpu.make_async_copy(gain_s, gainb.at[m], sems.at[12]),
                pltpu.make_async_copy(out_s, out, sems.at[13]),
            ]
            for copy in more:
                copy.start()
            save_g.wait()
            done(outs)
            done(more)

    args = [sc, dno, grouped, last, recv] + [w for pair in weights for w in pair] + [xb, slpb]
    aliases = {}
    if bufs is not None:
        aliases = {len(args) + n: n + 1 for n in range(n_buf)}
        args += list(bufs)
    out = pl.pallas_call(
        kernel,
        out_shape=(jax.ShapeDtypeStruct((rows, dims.width), BF),) + shapes,
        in_specs=[SMEM] * 3 + [ANY] * (len(args) - 3),
        out_specs=(ANY,) * 5,
        input_output_aliases=aliases,
        scratch_shapes=[
            pltpu.VMEM((dims.hidden, BLK, BLK), BF),
            pltpu.VMEM((dims.hidden, BLK, BLK), BF),
            pltpu.VMEM((dims.parts, RANK, dims.packed), BF),
            pltpu.VMEM((rows, dims.width), BF),
            pltpu.VMEM((rows, dims.width), BF),
            pltpu.VMEM((dims.hidden, rows, BLK), BF),
            pltpu.VMEM((dims.hidden, rows, BLK), BF),
            pltpu.VMEM((rows, 2 * BLK), BF),
            pltpu.VMEM((rows, dims.width), F32),
            pltpu.VMEM((8, dims.width), F32),
            pltpu.VMEM((rows, dims.width), BF),
            pltpu.SemaphoreType.DMA((14,)),
        ],
        compiler_params=params(60),
        name="backward_rows",
    )(*args)
    return out[0], out[1:]


def pick_rows(sc, sources, dst, sem):
    n = dst.shape[0] // len(sources[0])
    for q, triple in enumerate(sources):

        @pl.when(sc[3] == q)
        def _():
            for t, ref in enumerate(triple):
                pltpu.make_async_copy(ref.at[sc[4]], dst.at[t * n : (t + 1) * n], sem.at[t]).start()

    return tuple(
        pltpu.make_async_copy(ref.at[0], dst.at[t * n : (t + 1) * n], sem.at[t])
        for t, ref in enumerate(sources[0])
    )


def fwd_far(dims, sc, upo, sources, weights, bufs):
    hidb, slpb, nrmb, lowb = bufs
    rows = sources[0][0].shape[1]
    far = rows * len(sources[0])
    n_w, n_t, n_q = len(weights[0]), len(sources[0]), len(sources)
    args = [sc, upo] + list(weights[0]) + list(weights[2]) + [a for triple in sources for a in triple]
    n_plain = len(args)
    args += list(bufs)

    def kernel(*refs):
        sc, upo = refs[:2]
        up_w, small_w = refs[2 : 2 + n_w], refs[2 + n_w : 2 + 2 * n_w]
        base = 2 + 2 * n_w
        srcs = [refs[base + q * n_t : base + (q + 1) * n_t] for q in range(n_q)]
        hidb, slpb, nrmb, lowb = refs[n_plain + 4 : n_plain + 8]
        up_s, small_s, x_s, nrm_s, hid_s, slp_s, low_s, sems, xsem = refs[n_plain + 8 :]

        @pl.when(sc[0] == 1)
        def _():
            m, f = sc[1], sc[2]
            wait_x = pick_rows(sc, srcs, x_s, xsem)
            small, up = load_weights(f, (small_w, up_w), (small_s, up_s), sems)
            low_s[...] = jnp.zeros_like(low_s)
            done(wait_x)
            done(small)
            fwd_norm(dims, x_s, small_s, nrm_s, low_s)
            done(up)
            fwd_hidden(dims, small_s, up_s, upo, nrm_s, hid_s, slp_s, low_s, 8)
            at = slice(rows, rows + far)
            outs = [
                pltpu.make_async_copy(hid_s, hidb.at[m, :, at], sems.at[4]),
                pltpu.make_async_copy(slp_s, slpb.at[m, :, at], sems.at[5]),
                pltpu.make_async_copy(nrm_s, nrmb.at[m, at], sems.at[6]),
                pltpu.make_async_copy(low_s, lowb.at[m, at], sems.at[7]),
            ]
            for copy in outs:
                copy.start()
            done(outs)

    return pl.pallas_call(
        kernel,
        out_shape=tuple(jax.ShapeDtypeStruct(b.shape, b.dtype) for b in bufs),
        in_specs=[SMEM] * 2 + [ANY] * (len(args) - 2),
        out_specs=(ANY,) * 4,
        input_output_aliases={n_plain + n: n for n in range(4)},
        scratch_shapes=[
            pltpu.VMEM((dims.hidden, BLK, BLK), BF),
            pltpu.VMEM((dims.parts, RANK, dims.packed), BF),
            pltpu.VMEM((far, dims.width), BF),
            pltpu.VMEM((far, dims.width), BF),
            pltpu.VMEM((dims.hidden, far, BLK), BF),
            pltpu.VMEM((dims.hidden, far, BLK), BF),
            pltpu.VMEM((far, 2 * BLK), BF),
            pltpu.SemaphoreType.DMA((8,)),
            pltpu.SemaphoreType.DMA((n_t,)),
        ],
        compiler_params=params(60),
        name="forward_far_rows",
    )(*args)


def bwd_far(dims, sc, dno, sources, weights, slpb, bufs):
    rows = sources[0][0].shape[1]
    far = rows * len(sources[0])
    n_w, n_t, n_q = len(weights[0]), len(sources[0]), len(sources)
    args = [sc, dno] + list(weights[1]) + list(weights[2]) + [a for triple in sources for a in triple] + [slpb]
    n_plain = len(args)
    args += list(bufs)

    def kernel(*refs):
        sc, dno = refs[:2]
        dn_w, small_w = refs[2 : 2 + n_w], refs[2 + n_w : 2 + 2 * n_w]
        base = 2 + 2 * n_w
        srcs = [refs[base + q * n_t : base + (q + 1) * n_t] for q in range(n_q)]
        slpb = refs[n_plain - 1]
        gpb, gb, lowb = refs[n_plain + 3 : n_plain + 6]
        dn_s, small_s, g_s, slp_s, gp_s, low_s, sems, gsem = refs[n_plain + 6 :]

        @pl.when(sc[0] == 1)
        def _():
            m, f = sc[1], sc[2]
            at = slice(rows, rows + far)
            wait_g = pick_rows(sc, srcs, g_s, gsem)
            small, dn = load_weights(f, (small_w, dn_w), (small_s, dn_s), sems)
            get_slope = pltpu.make_async_copy(slpb.at[m, :, at], slp_s, sems.at[4])
            get_slope.start()
            low_s[...] = jnp.zeros_like(low_s)
            done(wait_g)
            save_g = pltpu.make_async_copy(g_s, gb.at[m, at], sems.at[5])
            save_g.start()
            done(small)
            done(dn)
            get_slope.wait()
            bwd_hidden(dims, g_s, slp_s, gp_s, small_s, dn_s, dno, low_s, 4)
            outs = [
                pltpu.make_async_copy(gp_s, gpb.at[m, :, at], sems.at[6]),
                pltpu.make_async_copy(low_s, lowb.at[m, at], sems.at[7]),
            ]
            for copy in outs:
                copy.start()
            save_g.wait()
            done(outs)

    return pl.pallas_call(
        kernel,
        out_shape=tuple(jax.ShapeDtypeStruct(b.shape, b.dtype) for b in bufs),
        in_specs=[SMEM] * 2 + [ANY] * (len(args) - 2),
        out_specs=(ANY,) * 3,
        input_output_aliases={n_plain + n: n for n in range(3)},
        scratch_shapes=[
            pltpu.VMEM((dims.hidden, BLK, BLK), BF),
            pltpu.VMEM((dims.parts, RANK, dims.packed), BF),
            pltpu.VMEM((far, dims.width), BF),
            pltpu.VMEM((dims.hidden, far, BLK), BF),
            pltpu.VMEM((dims.hidden, far, BLK), BF),
            pltpu.VMEM((far, 2 * BLK), BF),
            pltpu.SemaphoreType.DMA((8,)),
            pltpu.SemaphoreType.DMA((n_t,)),
        ],
        compiler_params=params(60),
        name="backward_far_rows",
    )(*args)


def weight_grads(dims, up, sc, order, blocks, wide, low_a, low_b, gain=None):
    micro, _, held, _ = blocks.shape
    total = micro * held
    group, model, mh, hh = dims.group, dims.model, dims.mh, dims.hh
    U = 4
    two = dims.parts == 2
    hid_at = mh * BLK
    gain_at = hid_at + hh * BLK
    packed = gain_at + (mh * BLK if up else 0)
    VM = pl.BlockSpec(memory_space=pltpu.VMEM)
    a_at, b_at = (0, 0) if up else (BLK, BLK)
    extra = [gain] if up else []

    def kernel(*refs):
        sc, order, blocks, wide, low_a, low_b = refs[:6]
        gain = refs[6] if up else None
        outs_hbm = refs[6 + len(extra) : -6]
        big, small, held_s, wide_s, sems, osems = refs[-6:]
        f = sc[2]
        get_wide = pltpu.make_async_copy(wide, wide_s, osems.at[0])
        get_wide.start()

        def fetch(it, slot, go):
            for u in range(U):
                for c in range(group):
                    j = order[(it * U + u) * group + c]
                    copy = pltpu.make_async_copy(
                        blocks.at[:, j], held_s.at[slot, u * group + c], sems.at[slot, u * group + c]
                    )
                    copy.start() if go else copy.wait()

        fetch(0, 0, True)

        def low_t(ref, at):
            rows = jnp.concatenate([ref[m, :, at : at + BLK] for m in range(micro)], axis=0)
            return rows.astype(F32).T[0:RANK].astype(BF)

        with_blocks, with_wide = low_t(low_a, a_at), low_t(low_b, b_at)
        get_wide.wait()

        def which(h):
            return jnp.where(h == f, 0, 1) if two else h

        def step(it, _):
            slot = lax.rem(it, 2)

            @pl.when(it + 1 < model // U)
            def _():
                fetch(it + 1, 1 - slot, True)

            fetch(it, slot, False)
            for u in range(U):
                i = it * U + u
                h = i // mh
                w = which(h)
                off = i - h * mh
                wi = jnp.concatenate([wide_s[m, :, lanes(i * BLK)] for m in range(micro)], axis=0)
                lhs = jnp.concatenate([wi.T, with_blocks], axis=0)
                rhs = jnp.concatenate(
                    [held_s[slot, u * group + c].reshape(total, BLK) for c in range(group)], axis=1
                )
                res = dot(lhs, rhs)
                for c in range(group):
                    j = order[i * group + c]
                    hj = j // hh
                    wj = which(hj)
                    part = res[:, c * BLK : (c + 1) * BLK]
                    if up:
                        big[wj, j - hj * hh] = part[0:BLK].astype(BF)
                    else:
                        big[w, off * group + c] = part[0:BLK].T.astype(BF)
                    small[wj, :, lanes(hid_at + (j - hj * hh) * BLK)] = part[BLK:].astype(BF)
                small[w, :, lanes(off * BLK)] = dot(with_wide, wi).astype(BF)
                if up:
                    small[w, :, lanes(gain_at + off * BLK)] = jnp.broadcast_to(
                        gain[0:1, lanes(i * BLK)], (RANK, BLK)
                    ).astype(BF)
            return 0

        lax.fori_loop(0, model // U, step, 0)
        outs = []
        for n, src in enumerate((big, small)):
            if two:
                outs.append(pltpu.make_async_copy(src.at[0], outs_hbm[2 * n], osems.at[2 * n]))
                outs.append(pltpu.make_async_copy(src.at[1], outs_hbm[2 * n + 1], osems.at[2 * n + 1]))
            else:
                outs.append(pltpu.make_async_copy(src, outs_hbm[n], osems.at[2 * n]))
        for copy in outs:
            copy.start()
        done(outs)

    lead = () if two else (dims.parts,)
    shapes = [lead + (hh, BLK, BLK), lead + (RANK, packed)]
    shapes = [jax.ShapeDtypeStruct(shape, BF) for shape in shapes for _ in range(2 if two else 1)]
    got = pl.pallas_call(
        kernel,
        out_shape=tuple(shapes),
        in_specs=[SMEM] * 2 + [ANY] * 2 + [VM] * (2 + len(extra)),
        out_specs=(ANY,) * len(shapes),
        scratch_shapes=[
            pltpu.VMEM((dims.parts, hh, BLK, BLK), BF),
            pltpu.VMEM((dims.parts, RANK, packed), BF),
            pltpu.VMEM((2, U * group, micro, held, BLK), BF),
            pltpu.VMEM((micro, held, dims.width), BF),
            pltpu.SemaphoreType.DMA((2, U * group)),
            pltpu.SemaphoreType.DMA((4,)),
        ],
        compiler_params=params(60),
        name="up_gradients" if up else "down_gradients",
    )(sc, order, blocks, wide, low_a, low_b, *extra)
    return [got[0:2], got[2:4]] if two else [got[0:1], got[1:2]]


def orders(up_order, dims):
    at = jnp.arange(dims.hidden, dtype=jnp.int32)
    same = (up_order[:, None] == up_order[None, :]) & (at[None, :] < at[:, None])
    place = up_order * dims.group + jnp.sum(same.astype(jnp.int32), axis=1)
    hit = place[None, :] == at[:, None]
    return jnp.sum(jnp.where(hit, at[None, :], 0), axis=1)


def shards(inputs, cotangent, norm_gain, up_blocks, down_blocks, up_left, up_right, down_left, down_right,
           up_pattern, down_pattern):
    micro, rows, width = inputs.shape
    upo, dno = up_pattern[0], down_pattern[0]
    parts = lax.axis_size("fsdp")
    dims = Dims(width, upo.shape[0], parts)
    n_sec = lax.axis_size("section")
    sec = lax.axis_index("section")
    f = lax.axis_index("fsdp")
    swap = [(0, 1), (1, 0)]
    held = rows
    small = jnp.concatenate(
        [up_left[0], down_right[0], up_right[0], down_left[0],
         jnp.broadcast_to(norm_gain, (RANK, norm_gain.shape[1]))], axis=1)

    def whole_layer(own, stacked):
        if parts == 2:
            return (own, lax.ppermute(own, "fsdp", swap))
        return (lax.all_gather(own, "fsdp", axis=0, tiled=not stacked),)

    small_w = whole_layer(small, True)
    up_w = whole_layer(up_blocks[0], False)
    weights = (up_w, whole_layer(down_blocks[0], False), small_w)
    grouped = orders(upo, dims)
    zero = jnp.int32(0)

    def scalars(m, edge):
        live = (m >= 0) & (m < micro)
        return jnp.stack([live.astype(jnp.int32), jnp.clip(m, 0, micro - 1).astype(jnp.int32),
                          f.astype(jnp.int32), edge.astype(jnp.int32), zero, zero, zero, zero])

    state = {"token": None}

    def chained(*arrays):
        if state["token"] is None:
            return arrays
        out = lax.optimization_barrier(arrays + (state["token"],))
        return out[:-1]

    fbufs, bbufs = None, None
    frecv = inputs[0]
    brecv = inputs[0]
    last = n_sec - 1

    def forward(t):
        nonlocal fbufs, frecv
        (x,) = chained(frecv)
        y, fbufs = fwd_slot(dims, scalars(t - sec, sec == 0), upo, dno, inputs, x, weights, fbufs, micro, held)
        state["token"] = y
        pairs = [(s, s + 1) for s in range(last) if 0 <= t - s < micro]
        if pairs:
            frecv = lax.ppermute(y, "section", pairs)

    def backward(t):
        nonlocal bbufs, brecv
        (g,) = chained(brecv)
        out, bbufs = bwd_slot(dims, scalars(t - (last - sec), sec == last), dno, grouped, cotangent, g,
                              weights, fbufs[3], fbufs[1], bbufs, micro, held)
        state["token"] = out
        pairs = [(last - s, last - s - 1) for s in range(last) if 0 <= t - s < micro]
        if pairs:
            brecv = lax.ppermute(out, "section", pairs)

    slots = micro + last
    for t in range(slots):
        forward(t)
        if t >= last:
            backward(t - last)
    for t in range(slots - last, slots):
        backward(t)
    hidb, slpb, nrmb, _, lowf = fbufs
    gpb, gb, lowb, gainb = bbufs
    sc = scalars(zero, sec == 0)

    def over_fsdp(pieces):
        if parts == 2:
            got = lax.ppermute(pieces[1], "fsdp", swap)
            return (pieces[0].astype(F32) + got.astype(F32)).astype(BF)
        return lax.psum_scatter(pieces[0], "fsdp", scatter_dimension=0, tiled=False)

    gain = jnp.sum(gainb, axis=(0, 1))[None]
    dn_g, dn_small = weight_grads(dims, False, sc, dno, hidb, gb, lowb, lowf)
    up_g, up_small = weight_grads(dims, True, sc, grouped, gpb, nrmb, lowf, lowb, gain)
    sums = lax.psum([over_fsdp(p) for p in (dn_g, dn_small, up_g, up_small)], "dp")
    dn, dns, up, ups = (s[None].astype(F32) for s in sums)
    mw, hw = dims.mh * BLK, dims.hh * BLK
    return (
        ups[:, 0, mw + hw :],
        up,
        dn,
        ups[:, :, 0:mw],
        ups[:, :, mw : mw + hw],
        dns[:, :, mw : mw + hw],
        dns[:, :, 0:mw],
    )


def solution(mesh):
    placed = (
        P(None, ("fsdp", "dp"), None),
        P(None, ("fsdp", "dp"), None),
        P("section", "fsdp"),
        P("section", "fsdp", None, None),
        P("section", "fsdp", None, None),
        P("section", None, "fsdp"),
        P("section", None, "fsdp"),
        P("section", None, "fsdp"),
        P("section", None, "fsdp"),
        P("section", None),
        P("section", None),
    )
    return jax.shard_map(
        shards,
        mesh=mesh,
        in_specs=placed,
        out_specs=(
            P("section", "fsdp"),
            P("section", "fsdp", None, None),
            P("section", "fsdp", None, None),
            P("section", None, "fsdp"),
            P("section", None, "fsdp"),
            P("section", None, "fsdp"),
            P("section", None, "fsdp"),
        ),
        check_vma=False,
    )
```

```python
import functools

import jax
import jax.numpy as jnp
from jax import lax
from jax.experimental import pallas as pl
from jax.experimental.pallas import tpu as pltpu
from jax.sharding import PartitionSpec as P

EPSILON = 1e-05
NORMAL_PEAK = 0.3989422804014327
TAIL_SCALE = 0.3
TAIL = (
    0.11962930931947272,
    0.12075380294875883,
    0.09991439682547013,
    0.12855881360857063,
    -0.05367866289105895,
    0.20634847173237508,
    -0.15720038925639956,
    0.03567418525278745,
)
BLK = 128
RANK = 16
BF = jnp.bfloat16
F32 = jnp.float32
NN = (((1,), (0,)), ((), ()))
NT = (((1,), (1,)), ((), ()))
TN = (((0,), (0,)), ((), ()))
ANY = pl.BlockSpec(memory_space=pl.ANY)
SMEM = pl.BlockSpec(memory_space=pltpu.SMEM)


def dot(a, b, dims=NN):
    return lax.dot_general(a, b, dims, preferred_element_type=F32)


def gelu_both(value):
    bell = jnp.exp(-0.5 * value * value)
    denom = 1.0 + TAIL_SCALE * jnp.abs(value)
    guess = pl.reciprocal(denom, approx=True)
    t = guess * (2.0 - denom * guess)
    poly = jnp.full_like(t, TAIL[-1])
    for coef in TAIL[-2::-1]:
        poly = poly * t + coef
    tail = bell * (t * poly)
    cdf = jnp.where(value < 0.0, tail, 1.0 - tail)
    return value * cdf, cdf + value * (bell * NORMAL_PEAK)


class Dims:
    def __init__(self, width, hidden_blocks, parts):
        self.parts = parts
        self.width = width
        self.model = width // BLK
        self.hidden = hidden_blocks
        self.group = hidden_blocks // self.model
        self.mh = self.model // parts
        self.hh = hidden_blocks // parts
        self.ul = 0
        self.dr = self.mh * BLK
        self.ur = 2 * self.mh * BLK
        self.dl = self.ur + self.hh * BLK
        self.gain = self.dl + self.hh * BLK
        self.packed = self.gain + self.mh * BLK


def lanes(start, count=BLK):
    return pl.ds(pl.multiple_of(start, BLK), count)


def load_weights(f, srcs, dsts, sems, first=0):
    copies = []
    for n, (src, dst) in enumerate(zip(srcs, dsts), first):
        if len(src) == 1:
            whole = pltpu.make_async_copy(src[0], dst, sems.at[2 * n])
            whole.start()
            copies.append((whole,))
            continue
        own, other = src
        half = dst.shape[0] // 2
        if own.ndim < dst.ndim:
            mine, theirs = f, 1 - f
        else:
            mine, theirs = pl.ds(f * half, half), pl.ds((1 - f) * half, half)
        a = pltpu.make_async_copy(own, dst.at[mine], sems.at[2 * n])
        b = pltpu.make_async_copy(other, dst.at[theirs], sems.at[2 * n + 1])
        a.start()
        b.start()
        copies.append((a, b))
    return copies


def done(pair):
    for copy in pair:
        copy.wait()


def inverse_rms(x_s, dims):
    rows = x_s.shape[0]
    total = jnp.zeros((rows, BLK), F32)
    for i in range(dims.model):
        part = x_s[:, i * BLK : (i + 1) * BLK].astype(F32)
        total = total + part * part
    return lax.rsqrt(jnp.sum(total, axis=1, keepdims=True) * (1.0 / dims.width) + EPSILON)


def fwd_norm(dims, x_s, small_s, nrm_s, low_s):
    rows = x_s.shape[0]
    r = inverse_rms(x_s, dims)
    upl = jnp.zeros((rows, RANK), F32)
    for h in range(dims.parts):
        for i in range(dims.mh):
            at = (h * dims.mh + i) * BLK
            gain = small_s[h, 0:1, dims.gain + i * BLK : dims.gain + (i + 1) * BLK].astype(F32)
            nrm_s[:, at : at + BLK] = (x_s[:, at : at + BLK].astype(F32) * r * gain).astype(BF)
        upl = upl + dot(
            nrm_s[:, h * dims.mh * BLK : (h + 1) * dims.mh * BLK],
            small_s[h, :, dims.ul : dims.ul + dims.mh * BLK],
            NT,
        )
    low_s[:, 0:RANK] = upl.astype(BF)


def fwd_hidden(dims, small_s, up_s, upo, nrm_s, hid_s, slp_s, low_s, G=32):
    rows = nrm_s.shape[0]
    G = min(G, dims.hh)
    upl = low_s[:, 0:RANK]

    def step(it, low):
        j0 = it * G
        h = j0 // dims.hh
        off = (j0 - h * dims.hh) * BLK
        ur = small_s[h, :, lanes(dims.ur + off, G * BLK)]
        dl = small_s[h, :, lanes(dims.dl + off, G * BLK)]
        hids = []
        for g in range(G):
            src = nrm_s[:, lanes(upo[j0 + g] * BLK)]
            lhs = jnp.concatenate([src, upl], axis=1)
            rhs = jnp.concatenate([up_s[j0 + g], ur[:, g * BLK : (g + 1) * BLK]], axis=0)
            hid, slope = gelu_both(dot(lhs, rhs))
            hid = hid.astype(BF)
            hid_s[j0 + g] = hid
            slp_s[j0 + g] = slope.astype(BF)
            hids.append(hid)
        return low + dot(jnp.concatenate(hids, axis=1), dl, NT)

    low = lax.fori_loop(0, dims.hidden // G, step, jnp.zeros((rows, RANK), F32)).astype(BF)
    low_s[:, BLK : BLK + RANK] = low
    return low


def fwd_down(dims, low, x_s, small_s, dn_s, dno, hid_s, y_s):
    def down(it, _):
        for u in range(8):
            i = it * 8 + u
            h = i // dims.mh
            at = i * BLK
            dr = small_s[h, :, lanes(dims.dr + (i - h * dims.mh) * BLK)]
            parts = [hid_s[dno[i * dims.group + c]] for c in range(dims.group)]
            lhs = jnp.concatenate(parts + [low], axis=1)
            blocks = dn_s[pl.ds(i * dims.group, dims.group)].reshape(dims.group * BLK, BLK)
            mixed = dot(lhs, jnp.concatenate([blocks, dr], axis=0))
            y_s[:, lanes(at)] = (x_s[:, lanes(at)].astype(F32) + mixed).astype(BF)
        return 0

    lax.fori_loop(0, dims.model // 8, down, 0)


def bwd_hidden(dims, g_s, slp_s, gp_s, small_s, dn_s, dno, low_s, U=8):
    rows = g_s.shape[0]
    gdl = jnp.zeros((rows, RANK), F32)
    for h in range(dims.parts):
        gdl = gdl + dot(
            g_s[:, h * dims.mh * BLK : (h + 1) * dims.mh * BLK],
            small_s[h, :, dims.dr : dims.dr + dims.mh * BLK],
            NT,
        )
    gdl = gdl.astype(BF)
    low_s[:, BLK : BLK + RANK] = gdl

    def hid_step(it, gul):
        for u in range(U):
            i = it * U + u
            gi = g_s[:, lanes(i * BLK)]
            js = [dno[i * dims.group + c] for c in range(dims.group)]
            hs = [j // dims.hh for j in js]
            offs = [(j - h * dims.hh) * BLK for j, h in zip(js, hs)]
            dl = jnp.concatenate([small_s[h, :, lanes(dims.dl + o)] for h, o in zip(hs, offs)], axis=1)
            ur = jnp.concatenate([small_s[h, :, lanes(dims.ur + o)] for h, o in zip(hs, offs)], axis=1)
            blocks = dn_s[pl.ds(i * dims.group, dims.group)].reshape(dims.group * BLK, BLK)
            gh = dot(gi, blocks, NT) + dot(gdl, dl)
            slope = jnp.concatenate([slp_s[j] for j in js], axis=1).astype(F32)
            gp = (gh * slope).astype(BF)
            for c, j in enumerate(js):
                gp_s[j] = gp[:, c * BLK : (c + 1) * BLK]
            gul = gul + dot(gp, ur, NT)
        return gul

    gul = lax.fori_loop(0, dims.model // U, hid_step, jnp.zeros((rows, RANK), F32))
    gul = gul.astype(BF)
    low_s[:, 0:RANK] = gul
    return gul


def bwd_input(dims, x_s, g_s, gp_s, small_s, up_s, grouped, gul, gn_s, gain_s, out_s):
    rows = g_s.shape[0]
    r = inverse_rms(x_s, dims)

    def step(it, acc):
        for u in range(8):
            i = it * 8 + u
            h = i // dims.mh
            off = (i - h * dims.mh) * BLK
            js = [grouped[i * dims.group + c] for c in range(dims.group)]
            lhs = jnp.concatenate([gp_s[j] for j in js], axis=1)
            rhs = jnp.concatenate([up_s[j] for j in js], axis=1)
            gn = dot(lhs, rhs, NT) + dot(gul, small_s[h, :, lanes(dims.ul + off)])
            x = x_s[:, lanes(i * BLK)].astype(F32)
            gain = small_s[h, 0:1, lanes(dims.gain + off)].astype(F32)
            scaled = gn * gain
            gn_s[:, lanes(i * BLK)] = scaled
            gain_s[0:1, lanes(i * BLK)] = jnp.sum(gn * x * r, axis=0, keepdims=True)
            acc = acc + x * scaled
        return acc

    acc = lax.fori_loop(0, dims.model // 8, step, jnp.zeros((rows, BLK), F32))
    shift = jnp.sum(acc, axis=1, keepdims=True) * (1.0 / dims.width) * (r * r * r)
    for i in range(dims.model):
        at = slice(i * BLK, (i + 1) * BLK)
        out_s[:, at] = (
            g_s[:, at].astype(F32) + r * gn_s[:, at] - x_s[:, at].astype(F32) * shift
        ).astype(BF)


def params(mib):
    return pltpu.CompilerParams(vmem_limit_bytes=mib * 1024 * 1024)


def fwd_slot(dims, sc, upo, dno, first, recv, weights, bufs, micro, held):
    rows = recv.shape[0]
    n_buf = 5
    shapes = (
        jax.ShapeDtypeStruct((micro, dims.hidden, held, BLK), BF),
        jax.ShapeDtypeStruct((micro, dims.hidden, held, BLK), BF),
        jax.ShapeDtypeStruct((micro, held, dims.width), BF),
        jax.ShapeDtypeStruct((micro, rows, dims.width), BF),
        jax.ShapeDtypeStruct((micro, held, 2 * BLK), BF),
    )
    n_w = len(weights[0])
    n_in = 5 + 3 * n_w + (n_buf if bufs is not None else 0)

    def kernel(*refs):
        sc, upo, dno, first, recv = refs[:5]
        up_w, dn_w, small_w = (refs[5 + k * n_w : 5 + (k + 1) * n_w] for k in range(3))
        y, hidb, slpb, nrmb, xb, lowb = refs[n_in : n_in + 6]
        up_s, dn_s, small_s, x_s, nrm_s, hid_s, slp_s, low_s, y_s, sems = refs[n_in + 6 :]

        @pl.when(sc[0] == 1)
        def _():
            m, f = sc[1], sc[2]

            @pl.when(sc[3] == 1)
            def _():
                pltpu.make_async_copy(first.at[m], x_s, sems.at[6]).start()

            @pl.when(sc[3] == 0)
            def _():
                pltpu.make_async_copy(recv, x_s, sems.at[6]).start()

            wait_x = pltpu.make_async_copy(recv, x_s, sems.at[6])
            small, up = load_weights(f, (small_w, up_w), (small_s, up_s), sems)
            low_s[...] = jnp.zeros_like(low_s)
            wait_x.wait()
            save_x = pltpu.make_async_copy(x_s, xb.at[m], sems.at[7])
            save_x.start()
            done(small)
            fwd_norm(dims, x_s, small_s, nrm_s, low_s)
            done(up)
            (dn,) = load_weights(f, (dn_w,), (dn_s,), sems, 2)
            low = fwd_hidden(dims, small_s, up_s, upo, nrm_s, hid_s, slp_s, low_s)
            outs = [
                pltpu.make_async_copy(hid_s, hidb.at[m, :, 0:rows], sems.at[9]),
                pltpu.make_async_copy(slp_s, slpb.at[m, :, 0:rows], sems.at[10]),
                pltpu.make_async_copy(nrm_s, nrmb.at[m, 0:rows], sems.at[11]),
                pltpu.make_async_copy(low_s, lowb.at[m, 0:rows], sems.at[12]),
            ]
            for copy in outs:
                copy.start()
            done(dn)
            fwd_down(dims, low, x_s, small_s, dn_s, dno, hid_s, y_s)
            outs.append(pltpu.make_async_copy(y_s, y, sems.at[8]))
            outs[-1].start()
            save_x.wait()
            done(outs)

    args = [sc, upo, dno, first, recv] + [w for pair in weights for w in pair]
    aliases = {}
    if bufs is not None:
        aliases = {len(args) + n: n + 1 for n in range(n_buf)}
        args += list(bufs)
    out = pl.pallas_call(
        kernel,
        out_shape=(jax.ShapeDtypeStruct((rows, dims.width), BF),) + shapes,
        in_specs=[SMEM] * 3 + [ANY] * (len(args) - 3),
        out_specs=(ANY,) * 6,
        input_output_aliases=aliases,
        scratch_shapes=[
            pltpu.VMEM((dims.hidden, BLK, BLK), BF),
            pltpu.VMEM((dims.hidden, BLK, BLK), BF),
            pltpu.VMEM((dims.parts, RANK, dims.packed), BF),
            pltpu.VMEM((rows, dims.width), BF),
            pltpu.VMEM((rows, dims.width), BF),
            pltpu.VMEM((dims.hidden, rows, BLK), BF),
            pltpu.VMEM((dims.hidden, rows, BLK), BF),
            pltpu.VMEM((rows, 2 * BLK), BF),
            pltpu.VMEM((rows, dims.width), BF),
            pltpu.SemaphoreType.DMA((13,)),
        ],
        compiler_params=params(60),
        name="forward_rows",
    )(*args)
    return out[0], out[1:]


def bwd_slot(dims, sc, dno, grouped, last, recv, weights, xb, slpb, bufs, micro, held):
    rows = recv.shape[0]
    n_buf = 4
    shapes = (
        jax.ShapeDtypeStruct((micro, dims.hidden, held, BLK), BF),
        jax.ShapeDtypeStruct((micro, held, dims.width), BF),
        jax.ShapeDtypeStruct((micro, held, 2 * BLK), BF),
        jax.ShapeDtypeStruct((micro, 8, dims.width), F32),
    )
    n_w = len(weights[0])
    n_in = 7 + 3 * n_w + (n_buf if bufs is not None else 0)

    def kernel(*refs):
        sc, dno, grouped, last, recv = refs[:5]
        up_w, dn_w, small_w = (refs[5 + k * n_w : 5 + (k + 1) * n_w] for k in range(3))
        xb, slpb = refs[5 + 3 * n_w : 7 + 3 * n_w]
        out, gpb, gb, lowb, gainb = refs[n_in : n_in + 5]
        up_s, dn_s, small_s, x_s, g_s, slp_s, gp_s, low_s, gn_s, gain_s, out_s, sems = refs[n_in + 5 :]

        @pl.when(sc[0] == 1)
        def _():
            m, f = sc[1], sc[2]

            @pl.when(sc[3] == 1)
            def _():
                pltpu.make_async_copy(last.at[m], g_s, sems.at[6]).start()

            @pl.when(sc[3] == 0)
            def _():
                pltpu.make_async_copy(recv, g_s, sems.at[6]).start()

            wait_g = pltpu.make_async_copy(recv, g_s, sems.at[6])
            get_slope = pltpu.make_async_copy(slpb.at[m, :, 0:rows], slp_s, sems.at[7])
            get_x = pltpu.make_async_copy(xb.at[m], x_s, sems.at[8])
            small, dn = load_weights(f, (small_w, dn_w), (small_s, dn_s), sems)
            get_slope.start()
            low_s[...] = jnp.zeros_like(low_s)
            gain_s[...] = jnp.zeros_like(gain_s)
            wait_g.wait()
            save_g = pltpu.make_async_copy(g_s, gb.at[m, 0:rows], sems.at[9])
            save_g.start()
            done(small)
            get_slope.wait()
            done(dn)
            (up,) = load_weights(f, (up_w,), (up_s,), sems, 2)
            get_x.start()
            gul = bwd_hidden(dims, g_s, slp_s, gp_s, small_s, dn_s, dno, low_s)
            outs = [
                pltpu.make_async_copy(gp_s, gpb.at[m, :, 0:rows], sems.at[10]),
                pltpu.make_async_copy(low_s, lowb.at[m, 0:rows], sems.at[11]),
            ]
            for copy in outs:
                copy.start()
            get_x.wait()
            done(up)
            bwd_input(dims, x_s, g_s, gp_s, small_s, up_s, grouped, gul, gn_s, gain_s, out_s)
            more = [
                pltpu.make_async_copy(gain_s, gainb.at[m], sems.at[12]),
                pltpu.make_async_copy(out_s, out, sems.at[13]),
            ]
            for copy in more:
                copy.start()
            save_g.wait()
            done(outs)
            done(more)

    args = [sc, dno, grouped, last, recv] + [w for pair in weights for w in pair] + [xb, slpb]
    aliases = {}
    if bufs is not None:
        aliases = {len(args) + n: n + 1 for n in range(n_buf)}
        args += list(bufs)
    out = pl.pallas_call(
        kernel,
        out_shape=(jax.ShapeDtypeStruct((rows, dims.width), BF),) + shapes,
        in_specs=[SMEM] * 3 + [ANY] * (len(args) - 3),
        out_specs=(ANY,) * 5,
        input_output_aliases=aliases,
        scratch_shapes=[
            pltpu.VMEM((dims.hidden, BLK, BLK), BF),
            pltpu.VMEM((dims.hidden, BLK, BLK), BF),
            pltpu.VMEM((dims.parts, RANK, dims.packed), BF),
            pltpu.VMEM((rows, dims.width), BF),
            pltpu.VMEM((rows, dims.width), BF),
            pltpu.VMEM((dims.hidden, rows, BLK), BF),
            pltpu.VMEM((dims.hidden, rows, BLK), BF),
            pltpu.VMEM((rows, 2 * BLK), BF),
            pltpu.VMEM((rows, dims.width), F32),
            pltpu.VMEM((8, dims.width), F32),
            pltpu.VMEM((rows, dims.width), BF),
            pltpu.SemaphoreType.DMA((14,)),
        ],
        compiler_params=params(60),
        name="backward_rows",
    )(*args)
    return out[0], out[1:]


def pick_rows(sc, sources, dst, sem):
    n = dst.shape[0] // len(sources[0])
    for q, triple in enumerate(sources):

        @pl.when(sc[3] == q)
        def _():
            for t, ref in enumerate(triple):
                pltpu.make_async_copy(ref.at[sc[4]], dst.at[t * n : (t + 1) * n], sem.at[t]).start()

    return tuple(
        pltpu.make_async_copy(ref.at[0], dst.at[t * n : (t + 1) * n], sem.at[t])
        for t, ref in enumerate(sources[0])
    )


def fwd_far(dims, sc, upo, sources, weights, bufs):
    hidb, slpb, nrmb, lowb = bufs
    rows = sources[0][0].shape[1]
    far = rows * len(sources[0])
    n_w, n_t, n_q = len(weights[0]), len(sources[0]), len(sources)
    args = [sc, upo] + list(weights[0]) + list(weights[2]) + [a for triple in sources for a in triple]
    n_plain = len(args)
    args += list(bufs)

    def kernel(*refs):
        sc, upo = refs[:2]
        up_w, small_w = refs[2 : 2 + n_w], refs[2 + n_w : 2 + 2 * n_w]
        base = 2 + 2 * n_w
        srcs = [refs[base + q * n_t : base + (q + 1) * n_t] for q in range(n_q)]
        hidb, slpb, nrmb, lowb = refs[n_plain + 4 : n_plain + 8]
        up_s, small_s, x_s, nrm_s, hid_s, slp_s, low_s, sems, xsem = refs[n_plain + 8 :]

        @pl.when(sc[0] == 1)
        def _():
            m, f = sc[1], sc[2]
            wait_x = pick_rows(sc, srcs, x_s, xsem)
            small, up = load_weights(f, (small_w, up_w), (small_s, up_s), sems)
            low_s[...] = jnp.zeros_like(low_s)
            done(wait_x)
            done(small)
            fwd_norm(dims, x_s, small_s, nrm_s, low_s)
            done(up)
            fwd_hidden(dims, small_s, up_s, upo, nrm_s, hid_s, slp_s, low_s, 8)
            at = slice(rows, rows + far)
            outs = [
                pltpu.make_async_copy(hid_s, hidb.at[m, :, at], sems.at[4]),
                pltpu.make_async_copy(slp_s, slpb.at[m, :, at], sems.at[5]),
                pltpu.make_async_copy(nrm_s, nrmb.at[m, at], sems.at[6]),
                pltpu.make_async_copy(low_s, lowb.at[m, at], sems.at[7]),
            ]
            for copy in outs:
                copy.start()
            done(outs)

    return pl.pallas_call(
        kernel,
        out_shape=tuple(jax.ShapeDtypeStruct(b.shape, b.dtype) for b in bufs),
        in_specs=[SMEM] * 2 + [ANY] * (len(args) - 2),
        out_specs=(ANY,) * 4,
        input_output_aliases={n_plain + n: n for n in range(4)},
        scratch_shapes=[
            pltpu.VMEM((dims.hidden, BLK, BLK), BF),
            pltpu.VMEM((dims.parts, RANK, dims.packed), BF),
            pltpu.VMEM((far, dims.width), BF),
            pltpu.VMEM((far, dims.width), BF),
            pltpu.VMEM((dims.hidden, far, BLK), BF),
            pltpu.VMEM((dims.hidden, far, BLK), BF),
            pltpu.VMEM((far, 2 * BLK), BF),
            pltpu.SemaphoreType.DMA((8,)),
            pltpu.SemaphoreType.DMA((n_t,)),
        ],
        compiler_params=params(60),
        name="forward_far_rows",
    )(*args)


def bwd_far(dims, sc, dno, sources, weights, slpb, bufs):
    rows = sources[0][0].shape[1]
    far = rows * len(sources[0])
    n_w, n_t, n_q = len(weights[0]), len(sources[0]), len(sources)
    args = [sc, dno] + list(weights[1]) + list(weights[2]) + [a for triple in sources for a in triple] + [slpb]
    n_plain = len(args)
    args += list(bufs)

    def kernel(*refs):
        sc, dno = refs[:2]
        dn_w, small_w = refs[2 : 2 + n_w], refs[2 + n_w : 2 + 2 * n_w]
        base = 2 + 2 * n_w
        srcs = [refs[base + q * n_t : base + (q + 1) * n_t] for q in range(n_q)]
        slpb = refs[n_plain - 1]
        gpb, gb, lowb = refs[n_plain + 3 : n_plain + 6]
        dn_s, small_s, g_s, slp_s, gp_s, low_s, sems, gsem = refs[n_plain + 6 :]

        @pl.when(sc[0] == 1)
        def _():
            m, f = sc[1], sc[2]
            at = slice(rows, rows + far)
            wait_g = pick_rows(sc, srcs, g_s, gsem)
            small, dn = load_weights(f, (small_w, dn_w), (small_s, dn_s), sems)
            get_slope = pltpu.make_async_copy(slpb.at[m, :, at], slp_s, sems.at[4])
            get_slope.start()
            low_s[...] = jnp.zeros_like(low_s)
            done(wait_g)
            save_g = pltpu.make_async_copy(g_s, gb.at[m, at], sems.at[5])
            save_g.start()
            done(small)
            done(dn)
            get_slope.wait()
            bwd_hidden(dims, g_s, slp_s, gp_s, small_s, dn_s, dno, low_s, 4)
            outs = [
                pltpu.make_async_copy(gp_s, gpb.at[m, :, at], sems.at[6]),
                pltpu.make_async_copy(low_s, lowb.at[m, at], sems.at[7]),
            ]
            for copy in outs:
                copy.start()
            save_g.wait()
            done(outs)

    return pl.pallas_call(
        kernel,
        out_shape=tuple(jax.ShapeDtypeStruct(b.shape, b.dtype) for b in bufs),
        in_specs=[SMEM] * 2 + [ANY] * (len(args) - 2),
        out_specs=(ANY,) * 3,
        input_output_aliases={n_plain + n: n for n in range(3)},
        scratch_shapes=[
            pltpu.VMEM((dims.hidden, BLK, BLK), BF),
            pltpu.VMEM((dims.parts, RANK, dims.packed), BF),
            pltpu.VMEM((far, dims.width), BF),
            pltpu.VMEM((dims.hidden, far, BLK), BF),
            pltpu.VMEM((dims.hidden, far, BLK), BF),
            pltpu.VMEM((far, 2 * BLK), BF),
            pltpu.SemaphoreType.DMA((8,)),
            pltpu.SemaphoreType.DMA((n_t,)),
        ],
        compiler_params=params(60),
        name="backward_far_rows",
    )(*args)


def weight_grads(dims, up, sc, order, blocks, wide, low_a, low_b, gain=None):
    micro, _, held, _ = blocks.shape
    total = micro * held
    group, model, mh, hh = dims.group, dims.model, dims.mh, dims.hh
    U = 4
    two = dims.parts == 2
    hid_at = mh * BLK
    gain_at = hid_at + hh * BLK
    packed = gain_at + (mh * BLK if up else 0)
    VM = pl.BlockSpec(memory_space=pltpu.VMEM)
    a_at, b_at = (0, 0) if up else (BLK, BLK)
    extra = [gain] if up else []

    def kernel(*refs):
        sc, order, blocks, wide, low_a, low_b = refs[:6]
        gain = refs[6] if up else None
        outs_hbm = refs[6 + len(extra) : -6]
        big, small, held_s, wide_s, sems, osems = refs[-6:]
        f = sc[2]
        get_wide = pltpu.make_async_copy(wide, wide_s, osems.at[0])
        get_wide.start()

        def fetch(it, slot, go):
            for u in range(U):
                for c in range(group):
                    j = order[(it * U + u) * group + c]
                    copy = pltpu.make_async_copy(
                        blocks.at[:, j], held_s.at[slot, u * group + c], sems.at[slot, u * group + c]
                    )
                    copy.start() if go else copy.wait()

        fetch(0, 0, True)

        def low_t(ref, at):
            rows = jnp.concatenate([ref[m, :, at : at + BLK] for m in range(micro)], axis=0)
            return rows.astype(F32).T[0:RANK].astype(BF)

        with_blocks, with_wide = low_t(low_a, a_at), low_t(low_b, b_at)
        get_wide.wait()

        def which(h):
            return jnp.where(h == f, 0, 1) if two else h

        def step(it, _):
            slot = lax.rem(it, 2)

            @pl.when(it + 1 < model // U)
            def _():
                fetch(it + 1, 1 - slot, True)

            fetch(it, slot, False)
            for u in range(U):
                i = it * U + u
                h = i // mh
                w = which(h)
                off = i - h * mh
                wi = jnp.concatenate([wide_s[m, :, lanes(i * BLK)] for m in range(micro)], axis=0)
                lhs = jnp.concatenate([wi.T, with_blocks], axis=0)
                rhs = jnp.concatenate(
                    [held_s[slot, u * group + c].reshape(total, BLK) for c in range(group)], axis=1
                )
                res = dot(lhs, rhs)
                for c in range(group):
                    j = order[i * group + c]
                    hj = j // hh
                    wj = which(hj)
                    part = res[:, c * BLK : (c + 1) * BLK]
                    if up:
                        big[wj, j - hj * hh] = part[0:BLK].astype(BF)
                    else:
                        big[w, off * group + c] = part[0:BLK].T.astype(BF)
                    small[wj, :, lanes(hid_at + (j - hj * hh) * BLK)] = part[BLK:].astype(BF)
                small[w, :, lanes(off * BLK)] = dot(with_wide, wi).astype(BF)
                if up:
                    small[w, :, lanes(gain_at + off * BLK)] = jnp.broadcast_to(
                        gain[0:1, lanes(i * BLK)], (RANK, BLK)
                    ).astype(BF)
            return 0

        lax.fori_loop(0, model // U, step, 0)
        outs = []
        for n, src in enumerate((big, small)):
            if two:
                outs.append(pltpu.make_async_copy(src.at[0], outs_hbm[2 * n], osems.at[2 * n]))
                outs.append(pltpu.make_async_copy(src.at[1], outs_hbm[2 * n + 1], osems.at[2 * n + 1]))
            else:
                outs.append(pltpu.make_async_copy(src, outs_hbm[n], osems.at[2 * n]))
        for copy in outs:
            copy.start()
        done(outs)

    lead = () if two else (dims.parts,)
    shapes = [lead + (hh, BLK, BLK), lead + (RANK, packed)]
    shapes = [jax.ShapeDtypeStruct(shape, BF) for shape in shapes for _ in range(2 if two else 1)]
    got = pl.pallas_call(
        kernel,
        out_shape=tuple(shapes),
        in_specs=[SMEM] * 2 + [ANY] * 2 + [VM] * (2 + len(extra)),
        out_specs=(ANY,) * len(shapes),
        scratch_shapes=[
            pltpu.VMEM((dims.parts, hh, BLK, BLK), BF),
            pltpu.VMEM((dims.parts, RANK, packed), BF),
            pltpu.VMEM((2, U * group, micro, held, BLK), BF),
            pltpu.VMEM((micro, held, dims.width), BF),
            pltpu.SemaphoreType.DMA((2, U * group)),
            pltpu.SemaphoreType.DMA((4,)),
        ],
        compiler_params=params(60),
        name="up_gradients" if up else "down_gradients",
    )(sc, order, blocks, wide, low_a, low_b, *extra)
    return [got[0:2], got[2:4]] if two else [got[0:1], got[1:2]]


def orders(up_order, dims):
    at = jnp.arange(dims.hidden, dtype=jnp.int32)
    same = (up_order[:, None] == up_order[None, :]) & (at[None, :] < at[:, None])
    place = up_order * dims.group + jnp.sum(same.astype(jnp.int32), axis=1)
    hit = place[None, :] == at[:, None]
    return jnp.sum(jnp.where(hit, at[None, :], 0), axis=1)


def shards(inputs, cotangent, norm_gain, up_blocks, down_blocks, up_left, up_right, down_left, down_right,
           up_pattern, down_pattern):
    micro, rows, width = inputs.shape
    upo, dno = up_pattern[0], down_pattern[0]
    parts = lax.axis_size("fsdp")
    dims = Dims(width, upo.shape[0], parts)
    n_sec = lax.axis_size("section")
    sec = lax.axis_index("section")
    f = lax.axis_index("fsdp")
    swap = [(0, 1), (1, 0)]
    n_dp = lax.axis_size("dp")
    held = rows * n_dp
    small = jnp.concatenate(
        [up_left[0], down_right[0], up_right[0], down_left[0],
         jnp.broadcast_to(norm_gain, (RANK, norm_gain.shape[1]))], axis=1)

    def whole_layer(own, stacked):
        if parts == 2:
            return (own, lax.ppermute(own, "fsdp", swap))
        return (lax.all_gather(own, "fsdp", axis=0, tiled=not stacked),)

    small_w = whole_layer(small, True)
    up_w = whole_layer(up_blocks[0], False)
    weights = (up_w, whole_layer(down_blocks[0], False), small_w)
    grouped = orders(upo, dims)
    zero = jnp.int32(0)

    def scalars(m, edge):
        live = (m >= 0) & (m < micro)
        return jnp.stack([live.astype(jnp.int32), jnp.clip(m, 0, micro - 1).astype(jnp.int32),
                          f.astype(jnp.int32), edge.astype(jnp.int32), zero, zero, zero, zero])

    def to_dp(block, sections):
        got = []
        for k in range(1, n_dp):
            pairs = [(s * n_dp + d, s * n_dp + (d + k) % n_dp) for s in sections for d in range(n_dp)]
            got.append(lax.ppermute(block, ("section", "dp"), pairs))
        return tuple(got)

    def flags(live, m, source, index):
        return jnp.stack([jnp.asarray(v).astype(jnp.int32) for v in (live, m, f, source, index, 0, 0, 0)])

    state = {"token": None}

    def chained(*arrays):
        if state["token"] is None:
            return arrays
        out = lax.optimization_barrier(arrays + (state["token"],))
        return out[:-1]

    fbufs, bbufs = None, None
    frecv = inputs[0]
    brecv = inputs[0]
    last = n_sec - 1
    far_x, far_g = {}, {}
    far_edge = to_dp(jnp.where(sec == 0, inputs, cotangent), (0, last))

    def forward(t):
        nonlocal fbufs, frecv
        (x,) = chained(frecv)
        y, fbufs = fwd_slot(dims, scalars(t - sec, sec == 0), upo, dno, inputs, x, weights, fbufs, micro, held)
        state["token"] = y
        pairs = [(s, s + 1) for s in range(last) if 0 <= t - s < micro]
        arrived = [s for s in range(1, n_sec) if 0 <= t - s < micro]
        if arrived:
            (late,) = chained(x)
            far_x[t] = to_dp(late[None], arrived)
        if pairs:
            frecv = lax.ppermute(y, "section", pairs)

    def backward(t):
        nonlocal bbufs, brecv
        (g,) = chained(brecv)
        out, bbufs = bwd_slot(dims, scalars(t - (last - sec), sec == last), dno, grouped, cotangent, g,
                              weights, fbufs[3], fbufs[1], bbufs, micro, held)
        state["token"] = out
        pairs = [(last - s, last - s - 1) for s in range(last) if 0 <= t - s < micro]
        arrived = [s for s in range(last) if 0 <= t - (last - s) < micro]
        if arrived:
            (late,) = chained(g)
            far_g[t] = to_dp(late[None], arrived)
        if pairs:
            brecv = lax.ppermute(out, "section", pairs)

    def forward_far(m, live, sources, source, index):
        nonlocal fbufs
        (sc,) = chained(flags(live, m, source, index))
        hidb, slpb, nrmb, xb, lowf = fbufs
        hidb, slpb, nrmb, lowf = fwd_far(dims, sc, upo, sources, weights, (hidb, slpb, nrmb, lowf))
        fbufs = (hidb, slpb, nrmb, xb, lowf)

    slots = micro + last
    for t in range(slots):
        forward(t)
        if t >= last:
            backward(t - last)
    for m in range(micro):
        forward_far(m, sec == 0, [far_edge], 0, m)
    for t in range(slots - last, slots):
        backward(t)
    for m in range(micro):
        forward_far(m, sec > 0, [far_x[m + s] for s in range(1, n_sec)], sec - 1, 0)
    gain = jnp.sum(bbufs[3], axis=(0, 1))[None]
    for other in to_dp(gain, range(n_sec)):
        gain = gain + other
    gpb, gb, lowb, _ = bbufs
    for m in range(micro):
        sources = [far_g[m + last - s] for s in range(last)] + [far_edge]
        sc = flags(True, m, sec, jnp.where(sec == last, m, 0))
        gpb, gb, lowb = bwd_far(dims, sc, dno, sources, weights, fbufs[1], (gpb, gb, lowb))
    hidb, slpb, nrmb, _, lowf = fbufs
    sc = scalars(zero, sec == 0)

    def over_fsdp(pieces):
        if parts == 2:
            got = lax.ppermute(pieces[1], "fsdp", swap)
            return (pieces[0].astype(F32) + got.astype(F32))[None]
        return lax.psum_scatter(pieces[0], "fsdp", scatter_dimension=0, tiled=False).astype(F32)[None]

    dn_g, dn_small = weight_grads(dims, False, sc, dno, hidb, gb, lowb, lowf)
    up_g, up_small = weight_grads(dims, True, sc, grouped, gpb, nrmb, lowf, lowb, gain)
    dn, dns, up, ups = (over_fsdp(p) for p in (dn_g, dn_small, up_g, up_small))
    mw, hw = dims.mh * BLK, dims.hh * BLK
    return (
        ups[:, 0, mw + hw :],
        up,
        dn,
        ups[:, :, 0:mw],
        ups[:, :, mw : mw + hw],
        dns[:, :, mw : mw + hw],
        dns[:, :, 0:mw],
    )


def solution(mesh):
    placed = (
        P(None, ("fsdp", "dp"), None),
        P(None, ("fsdp", "dp"), None),
        P("section", "fsdp"),
        P("section", "fsdp", None, None),
        P("section", "fsdp", None, None),
        P("section", None, "fsdp"),
        P("section", None, "fsdp"),
        P("section", None, "fsdp"),
        P("section", None, "fsdp"),
        P("section", None),
        P("section", None),
    )
    return jax.shard_map(
        shards,
        mesh=mesh,
        in_specs=placed,
        out_specs=(
            P("section", "fsdp"),
            P("section", "fsdp", None, None),
            P("section", "fsdp", None, None),
            P("section", None, "fsdp"),
            P("section", None, "fsdp"),
            P("section", None, "fsdp"),
            P("section", None, "fsdp"),
        ),
        check_vma=False,
    )
```

```python
import functools

import jax
import jax.numpy as jnp
from jax import lax
from jax.experimental import pallas as pl
from jax.experimental.pallas import tpu as pltpu
from jax.sharding import PartitionSpec as P

EPSILON = 1e-05
NORMAL_PEAK = 0.3989422804014327
TAIL_SCALE = 0.3
TAIL = (
    0.11962930931947272,
    0.12075380294875883,
    0.09991439682547013,
    0.12855881360857063,
    -0.05367866289105895,
    0.20634847173237508,
    -0.15720038925639956,
    0.03567418525278745,
)
BLK = 128
RANK = 16
BF = jnp.bfloat16
F32 = jnp.float32
NN = (((1,), (0,)), ((), ()))
NT = (((1,), (1,)), ((), ()))
TN = (((0,), (0,)), ((), ()))
ANY = pl.BlockSpec(memory_space=pl.ANY)
SMEM = pl.BlockSpec(memory_space=pltpu.SMEM)


def dot(a, b, dims=NN):
    return lax.dot_general(a, b, dims, preferred_element_type=F32)


def gelu_both(value):
    bell = jnp.exp(-0.5 * value * value)
    denom = 1.0 + TAIL_SCALE * jnp.abs(value)
    guess = pl.reciprocal(denom, approx=True)
    t = guess * (2.0 - denom * guess)
    poly = jnp.full_like(t, TAIL[-1])
    for coef in TAIL[-2::-1]:
        poly = poly * t + coef
    tail = bell * (t * poly)
    cdf = jnp.where(value < 0.0, tail, 1.0 - tail)
    return value * cdf, cdf + value * (bell * NORMAL_PEAK)


class Dims:
    def __init__(self, width, hidden_blocks, parts):
        self.parts = parts
        self.width = width
        self.model = width // BLK
        self.hidden = hidden_blocks
        self.group = hidden_blocks // self.model
        self.mh = self.model // parts
        self.hh = hidden_blocks // parts
        self.ul = 0
        self.dr = self.mh * BLK
        self.ur = 2 * self.mh * BLK
        self.dl = self.ur + self.hh * BLK
        self.gain = self.dl + self.hh * BLK
        self.packed = self.gain + self.mh * BLK


def lanes(start, count=BLK):
    return pl.ds(pl.multiple_of(start, BLK), count)


def load_weights(f, srcs, dsts, sems, first=0):
    copies = []
    for n, (src, dst) in enumerate(zip(srcs, dsts), first):
        if len(src) == 1:
            whole = pltpu.make_async_copy(src[0], dst, sems.at[2 * n])
            whole.start()
            copies.append((whole,))
            continue
        own, other = src
        half = dst.shape[0] // 2
        if own.ndim < dst.ndim:
            mine, theirs = f, 1 - f
        else:
            mine, theirs = pl.ds(f * half, half), pl.ds((1 - f) * half, half)
        a = pltpu.make_async_copy(own, dst.at[mine], sems.at[2 * n])
        b = pltpu.make_async_copy(other, dst.at[theirs], sems.at[2 * n + 1])
        a.start()
        b.start()
        copies.append((a, b))
    return copies


def done(pair):
    for copy in pair:
        copy.wait()


def inverse_rms(x_s, dims):
    rows = x_s.shape[0]
    total = jnp.zeros((rows, BLK), F32)
    for i in range(dims.model):
        part = x_s[:, i * BLK : (i + 1) * BLK].astype(F32)
        total = total + part * part
    return lax.rsqrt(jnp.sum(total, axis=1, keepdims=True) * (1.0 / dims.width) + EPSILON)


def fwd_norm(dims, x_s, small_s, nrm_s, low_s):
    rows = x_s.shape[0]
    r = inverse_rms(x_s, dims)
    upl = jnp.zeros((rows, RANK), F32)
    for h in range(dims.parts):
        for i in range(dims.mh):
            at = (h * dims.mh + i) * BLK
            gain = small_s[h, 0:1, dims.gain + i * BLK : dims.gain + (i + 1) * BLK].astype(F32)
            nrm_s[:, at : at + BLK] = (x_s[:, at : at + BLK].astype(F32) * r * gain).astype(BF)
        upl = upl + dot(
            nrm_s[:, h * dims.mh * BLK : (h + 1) * dims.mh * BLK],
            small_s[h, :, dims.ul : dims.ul + dims.mh * BLK],
            NT,
        )
    low_s[:, 0:RANK] = upl.astype(BF)


def fwd_hidden(dims, small_s, up_s, upo, nrm_s, hid_s, slp_s, low_s, G=32):
    rows = nrm_s.shape[0]
    G = min(G, dims.hh)
    upl = low_s[:, 0:RANK]

    def step(it, low):
        j0 = it * G
        h = j0 // dims.hh
        off = (j0 - h * dims.hh) * BLK
        ur = small_s[h, :, lanes(dims.ur + off, G * BLK)]
        dl = small_s[h, :, lanes(dims.dl + off, G * BLK)]
        hids = []
        for g in range(G):
            src = nrm_s[:, lanes(upo[j0 + g] * BLK)]
            lhs = jnp.concatenate([src, upl], axis=1)
            rhs = jnp.concatenate([up_s[j0 + g], ur[:, g * BLK : (g + 1) * BLK]], axis=0)
            hid, slope = gelu_both(dot(lhs, rhs))
            hid = hid.astype(BF)
            hid_s[j0 + g] = hid
            slp_s[j0 + g] = slope.astype(BF)
            hids.append(hid)
        return low + dot(jnp.concatenate(hids, axis=1), dl, NT)

    low = lax.fori_loop(0, dims.hidden // G, step, jnp.zeros((rows, RANK), F32)).astype(BF)
    low_s[:, BLK : BLK + RANK] = low
    return low


def fwd_down(dims, low, x_s, small_s, dn_s, dno, hid_s, y_s):
    def down(it, _):
        for u in range(8):
            i = it * 8 + u
            h = i // dims.mh
            at = i * BLK
            dr = small_s[h, :, lanes(dims.dr + (i - h * dims.mh) * BLK)]
            parts = [hid_s[dno[i * dims.group + c]] for c in range(dims.group)]
            lhs = jnp.concatenate(parts + [low], axis=1)
            blocks = dn_s[pl.ds(i * dims.group, dims.group)].reshape(dims.group * BLK, BLK)
            mixed = dot(lhs, jnp.concatenate([blocks, dr], axis=0))
            y_s[:, lanes(at)] = (x_s[:, lanes(at)].astype(F32) + mixed).astype(BF)
        return 0

    lax.fori_loop(0, dims.model // 8, down, 0)


def bwd_hidden(dims, g_s, slp_s, gp_s, small_s, dn_s, dno, low_s, U=8):
    rows = g_s.shape[0]
    gdl = jnp.zeros((rows, RANK), F32)
    for h in range(dims.parts):
        gdl = gdl + dot(
            g_s[:, h * dims.mh * BLK : (h + 1) * dims.mh * BLK],
            small_s[h, :, dims.dr : dims.dr + dims.mh * BLK],
            NT,
        )
    gdl = gdl.astype(BF)
    low_s[:, BLK : BLK + RANK] = gdl

    def hid_step(it, gul):
        for u in range(U):
            i = it * U + u
            gi = g_s[:, lanes(i * BLK)]
            js = [dno[i * dims.group + c] for c in range(dims.group)]
            hs = [j // dims.hh for j in js]
            offs = [(j - h * dims.hh) * BLK for j, h in zip(js, hs)]
            dl = jnp.concatenate([small_s[h, :, lanes(dims.dl + o)] for h, o in zip(hs, offs)], axis=1)
            ur = jnp.concatenate([small_s[h, :, lanes(dims.ur + o)] for h, o in zip(hs, offs)], axis=1)
            blocks = dn_s[pl.ds(i * dims.group, dims.group)].reshape(dims.group * BLK, BLK)
            gh = dot(gi, blocks, NT) + dot(gdl, dl)
            slope = jnp.concatenate([slp_s[j] for j in js], axis=1).astype(F32)
            gp = (gh * slope).astype(BF)
            for c, j in enumerate(js):
                gp_s[j] = gp[:, c * BLK : (c + 1) * BLK]
            gul = gul + dot(gp, ur, NT)
        return gul

    gul = lax.fori_loop(0, dims.model // U, hid_step, jnp.zeros((rows, RANK), F32))
    gul = gul.astype(BF)
    low_s[:, 0:RANK] = gul
    return gul


def bwd_input(dims, x_s, g_s, gp_s, small_s, up_s, grouped, gul, gn_s, gain_s, out_s):
    rows = g_s.shape[0]
    r = inverse_rms(x_s, dims)

    def step(it, acc):
        for u in range(8):
            i = it * 8 + u
            h = i // dims.mh
            off = (i - h * dims.mh) * BLK
            js = [grouped[i * dims.group + c] for c in range(dims.group)]
            lhs = jnp.concatenate([gp_s[j] for j in js], axis=1)
            rhs = jnp.concatenate([up_s[j] for j in js], axis=1)
            gn = dot(lhs, rhs, NT) + dot(gul, small_s[h, :, lanes(dims.ul + off)])
            x = x_s[:, lanes(i * BLK)].astype(F32)
            gain = small_s[h, 0:1, lanes(dims.gain + off)].astype(F32)
            scaled = gn * gain
            gn_s[:, lanes(i * BLK)] = scaled
            gain_s[0:1, lanes(i * BLK)] = jnp.sum(gn * x * r, axis=0, keepdims=True)
            acc = acc + x * scaled
        return acc

    acc = lax.fori_loop(0, dims.model // 8, step, jnp.zeros((rows, BLK), F32))
    shift = jnp.sum(acc, axis=1, keepdims=True) * (1.0 / dims.width) * (r * r * r)
    for i in range(dims.model):
        at = slice(i * BLK, (i + 1) * BLK)
        out_s[:, at] = (
            g_s[:, at].astype(F32) + r * gn_s[:, at] - x_s[:, at].astype(F32) * shift
        ).astype(BF)


def params(mib):
    return pltpu.CompilerParams(vmem_limit_bytes=mib * 1024 * 1024)


def fwd_slot(dims, sc, upo, dno, first, recv, weights, bufs, micro, held):
    rows = recv.shape[0]
    n_buf = 5
    shapes = (
        jax.ShapeDtypeStruct((micro, dims.hidden, held, BLK), BF),
        jax.ShapeDtypeStruct((micro, dims.hidden, held, BLK), BF),
        jax.ShapeDtypeStruct((micro, held, dims.width), BF),
        jax.ShapeDtypeStruct((micro, rows, dims.width), BF),
        jax.ShapeDtypeStruct((micro, held, 2 * BLK), BF),
    )
    n_w = len(weights[0])
    n_in = 5 + 3 * n_w + (n_buf if bufs is not None else 0)

    def kernel(*refs):
        sc, upo, dno, first, recv = refs[:5]
        up_w, dn_w, small_w = (refs[5 + k * n_w : 5 + (k + 1) * n_w] for k in range(3))
        y, hidb, slpb, nrmb, xb, lowb = refs[n_in : n_in + 6]
        up_s, dn_s, small_s, x_s, nrm_s, hid_s, slp_s, low_s, y_s, sems = refs[n_in + 6 :]

        @pl.when(sc[0] == 1)
        def _():
            m, f = sc[1], sc[2]

            @pl.when(sc[3] == 1)
            def _():
                pltpu.make_async_copy(first.at[m], x_s, sems.at[6]).start()

            @pl.when(sc[3] == 0)
            def _():
                pltpu.make_async_copy(recv, x_s, sems.at[6]).start()

            wait_x = pltpu.make_async_copy(recv, x_s, sems.at[6])
            small, up = load_weights(f, (small_w, up_w), (small_s, up_s), sems)
            low_s[...] = jnp.zeros_like(low_s)
            wait_x.wait()
            save_x = pltpu.make_async_copy(x_s, xb.at[m], sems.at[7])
            save_x.start()
            done(small)
            fwd_norm(dims, x_s, small_s, nrm_s, low_s)
            done(up)
            (dn,) = load_weights(f, (dn_w,), (dn_s,), sems, 2)
            low = fwd_hidden(dims, small_s, up_s, upo, nrm_s, hid_s, slp_s, low_s)
            outs = [
                pltpu.make_async_copy(hid_s, hidb.at[m, :, 0:rows], sems.at[9]),
                pltpu.make_async_copy(slp_s, slpb.at[m, :, 0:rows], sems.at[10]),
                pltpu.make_async_copy(nrm_s, nrmb.at[m, 0:rows], sems.at[11]),
                pltpu.make_async_copy(low_s, lowb.at[m, 0:rows], sems.at[12]),
            ]
            for copy in outs:
                copy.start()
            done(dn)
            fwd_down(dims, low, x_s, small_s, dn_s, dno, hid_s, y_s)
            outs.append(pltpu.make_async_copy(y_s, y, sems.at[8]))
            outs[-1].start()
            save_x.wait()
            done(outs)

    args = [sc, upo, dno, first, recv] + [w for pair in weights for w in pair]
    aliases = {}
    if bufs is not None:
        aliases = {len(args) + n: n + 1 for n in range(n_buf)}
        args += list(bufs)
    out = pl.pallas_call(
        kernel,
        out_shape=(jax.ShapeDtypeStruct((rows, dims.width), BF),) + shapes,
        in_specs=[SMEM] * 3 + [ANY] * (len(args) - 3),
        out_specs=(ANY,) * 6,
        input_output_aliases=aliases,
        scratch_shapes=[
            pltpu.VMEM((dims.hidden, BLK, BLK), BF),
            pltpu.VMEM((dims.hidden, BLK, BLK), BF),
            pltpu.VMEM((dims.parts, RANK, dims.packed), BF),
            pltpu.VMEM((rows, dims.width), BF),
            pltpu.VMEM((rows, dims.width), BF),
            pltpu.VMEM((dims.hidden, rows, BLK), BF),
            pltpu.VMEM((dims.hidden, rows, BLK), BF),
            pltpu.VMEM((rows, 2 * BLK), BF),
            pltpu.VMEM((rows, dims.width), BF),
            pltpu.SemaphoreType.DMA((13,)),
        ],
        compiler_params=params(60),
        name="forward_rows",
    )(*args)
    return out[0], out[1:]


def bwd_slot(dims, sc, dno, grouped, last, recv, weights, xb, slpb, bufs, micro, held):
    rows = recv.shape[0]
    n_buf = 4
    shapes = (
        jax.ShapeDtypeStruct((micro, dims.hidden, held, BLK), BF),
        jax.ShapeDtypeStruct((micro, held, dims.width), BF),
        jax.ShapeDtypeStruct((micro, held, 2 * BLK), BF),
        jax.ShapeDtypeStruct((micro, 8, dims.width), F32),
    )
    n_w = len(weights[0])
    n_in = 7 + 3 * n_w + (n_buf if bufs is not None else 0)

    def kernel(*refs):
        sc, dno, grouped, last, recv = refs[:5]
        up_w, dn_w, small_w = (refs[5 + k * n_w : 5 + (k + 1) * n_w] for k in range(3))
        xb, slpb = refs[5 + 3 * n_w : 7 + 3 * n_w]
        out, gpb, gb, lowb, gainb = refs[n_in : n_in + 5]
        up_s, dn_s, small_s, x_s, g_s, slp_s, gp_s, low_s, gn_s, gain_s, out_s, sems = refs[n_in + 5 :]

        @pl.when(sc[0] == 1)
        def _():
            m, f = sc[1], sc[2]

            @pl.when(sc[3] == 1)
            def _():
                pltpu.make_async_copy(last.at[m], g_s, sems.at[6]).start()

            @pl.when(sc[3] == 0)
            def _():
                pltpu.make_async_copy(recv, g_s, sems.at[6]).start()

            wait_g = pltpu.make_async_copy(recv, g_s, sems.at[6])
            get_slope = pltpu.make_async_copy(slpb.at[m, :, 0:rows], slp_s, sems.at[7])
            get_x = pltpu.make_async_copy(xb.at[m], x_s, sems.at[8])
            small, dn = load_weights(f, (small_w, dn_w), (small_s, dn_s), sems)
            get_slope.start()
            low_s[...] = jnp.zeros_like(low_s)
            gain_s[...] = jnp.zeros_like(gain_s)
            wait_g.wait()
            save_g = pltpu.make_async_copy(g_s, gb.at[m, 0:rows], sems.at[9])
            save_g.start()
            done(small)
            get_slope.wait()
            done(dn)
            (up,) = load_weights(f, (up_w,), (up_s,), sems, 2)
            get_x.start()
            gul = bwd_hidden(dims, g_s, slp_s, gp_s, small_s, dn_s, dno, low_s)
            outs = [
                pltpu.make_async_copy(gp_s, gpb.at[m, :, 0:rows], sems.at[10]),
                pltpu.make_async_copy(low_s, lowb.at[m, 0:rows], sems.at[11]),
            ]
            for copy in outs:
                copy.start()
            get_x.wait()
            done(up)
            bwd_input(dims, x_s, g_s, gp_s, small_s, up_s, grouped, gul, gn_s, gain_s, out_s)
            more = [
                pltpu.make_async_copy(gain_s, gainb.at[m], sems.at[12]),
                pltpu.make_async_copy(out_s, out, sems.at[13]),
            ]
            for copy in more:
                copy.start()
            save_g.wait()
            done(outs)
            done(more)

    args = [sc, dno, grouped, last, recv] + [w for pair in weights for w in pair] + [xb, slpb]
    aliases = {}
    if bufs is not None:
        aliases = {len(args) + n: n + 1 for n in range(n_buf)}
        args += list(bufs)
    out = pl.pallas_call(
        kernel,
        out_shape=(jax.ShapeDtypeStruct((rows, dims.width), BF),) + shapes,
        in_specs=[SMEM] * 3 + [ANY] * (len(args) - 3),
        out_specs=(ANY,) * 5,
        input_output_aliases=aliases,
        scratch_shapes=[
            pltpu.VMEM((dims.hidden, BLK, BLK), BF),
            pltpu.VMEM((dims.hidden, BLK, BLK), BF),
            pltpu.VMEM((dims.parts, RANK, dims.packed), BF),
            pltpu.VMEM((rows, dims.width), BF),
            pltpu.VMEM((rows, dims.width), BF),
            pltpu.VMEM((dims.hidden, rows, BLK), BF),
            pltpu.VMEM((dims.hidden, rows, BLK), BF),
            pltpu.VMEM((rows, 2 * BLK), BF),
            pltpu.VMEM((rows, dims.width), F32),
            pltpu.VMEM((8, dims.width), F32),
            pltpu.VMEM((rows, dims.width), BF),
            pltpu.SemaphoreType.DMA((14,)),
        ],
        compiler_params=params(60),
        name="backward_rows",
    )(*args)
    return out[0], out[1:]


def pick_rows(sc, sources, dst, sem, count):
    n = dst.shape[0] // (len(sources[0]) * count)
    places = [(q, t, (q * len(sources[0]) + t) * n) for q in range(count) for t in range(len(sources[0]))]
    for number, triple in enumerate(sources):

        @pl.when(sc[3] == number)
        def _():
            for q, t, at in places:
                pltpu.make_async_copy(triple[t].at[sc[4] + q], dst.at[at : at + n], sem.at[q, t]).start()

    return tuple(
        pltpu.make_async_copy(sources[0][t].at[0], dst.at[at : at + n], sem.at[q, t]) for q, t, at in places
    )


def fwd_far(dims, sc, upo, sources, weights, bufs, count):
    hidb, slpb, nrmb, lowb = bufs
    rows = sources[0][0].shape[1]
    far = rows * len(sources[0])
    n_w, n_t, n_q = len(weights[0]), len(sources[0]), len(sources)
    args = [sc, upo] + list(weights[0]) + list(weights[2]) + [a for triple in sources for a in triple]
    n_plain = len(args)
    args += list(bufs)

    def kernel(*refs):
        sc, upo = refs[:2]
        up_w, small_w = refs[2 : 2 + n_w], refs[2 + n_w : 2 + 2 * n_w]
        base = 2 + 2 * n_w
        srcs = [refs[base + q * n_t : base + (q + 1) * n_t] for q in range(n_q)]
        hidb, slpb, nrmb, lowb = refs[n_plain + 4 : n_plain + 8]
        up_s, small_s, x_s, nrm_s, hid_s, slp_s, low_s, sems, xsem, osems = refs[n_plain + 9 :]

        @pl.when(sc[0] == 1)
        def _():
            m, f = sc[1], sc[2]
            wait_x = pick_rows(sc, srcs, x_s, xsem, count)
            small, up = load_weights(f, (small_w, up_w), (small_s, up_s), sems)
            low_s[...] = jnp.zeros_like(low_s)
            done(wait_x)
            done(small)
            fwd_norm(dims, x_s, small_s, nrm_s, low_s)
            done(up)
            fwd_hidden(dims, small_s, up_s, upo, nrm_s, hid_s, slp_s, low_s, 4)
            at = slice(rows, rows + far)
            outs = []
            for q in range(count):
                mine = slice(q * far, (q + 1) * far)
                outs += [
                    pltpu.make_async_copy(hid_s.at[:, mine], hidb.at[m + q, :, at], osems.at[q, 0]),
                    pltpu.make_async_copy(slp_s.at[:, mine], slpb.at[m + q, :, at], osems.at[q, 1]),
                    pltpu.make_async_copy(nrm_s.at[mine], nrmb.at[m + q, at], osems.at[q, 2]),
                    pltpu.make_async_copy(low_s.at[mine], lowb.at[m + q, at], osems.at[q, 3]),
                ]
            for copy in outs:
                copy.start()
            done(outs)

    return pl.pallas_call(
        kernel,
        out_shape=tuple(jax.ShapeDtypeStruct(b.shape, b.dtype) for b in bufs)
        + (jax.ShapeDtypeStruct((8, BLK), F32),),
        in_specs=[SMEM] * 2 + [ANY] * (len(args) - 2),
        out_specs=(ANY,) * 5,
        input_output_aliases={n_plain + n: n for n in range(4)},
        scratch_shapes=[
            pltpu.VMEM((dims.hidden, BLK, BLK), BF),
            pltpu.VMEM((dims.parts, RANK, dims.packed), BF),
            pltpu.VMEM((count * far, dims.width), BF),
            pltpu.VMEM((count * far, dims.width), BF),
            pltpu.VMEM((dims.hidden, count * far, BLK), BF),
            pltpu.VMEM((dims.hidden, count * far, BLK), BF),
            pltpu.VMEM((count * far, 2 * BLK), BF),
            pltpu.SemaphoreType.DMA((8,)),
            pltpu.SemaphoreType.DMA((count, n_t)),
            pltpu.SemaphoreType.DMA((count, 4)),
        ],
        compiler_params=params(60),
        name="forward_far_rows",
    )(*args)


def bwd_far(dims, sc, dno, sources, weights, slpb, bufs, count):
    rows = sources[0][0].shape[1]
    far = rows * len(sources[0])
    n_w, n_t, n_q = len(weights[0]), len(sources[0]), len(sources)
    args = [sc, dno] + list(weights[1]) + list(weights[2]) + [a for triple in sources for a in triple] + [slpb]
    n_plain = len(args)
    args += list(bufs)

    def kernel(*refs):
        sc, dno = refs[:2]
        dn_w, small_w = refs[2 : 2 + n_w], refs[2 + n_w : 2 + 2 * n_w]
        base = 2 + 2 * n_w
        srcs = [refs[base + q * n_t : base + (q + 1) * n_t] for q in range(n_q)]
        slpb = refs[n_plain - 1]
        gpb, gb, lowb = refs[n_plain + 3 : n_plain + 6]
        dn_s, small_s, g_s, slp_s, gp_s, low_s, sems, gsem, osems = refs[n_plain + 7 :]

        @pl.when(sc[0] == 1)
        def _():
            m, f = sc[1], sc[2]
            at = slice(rows, rows + far)
            wait_g = pick_rows(sc, srcs, g_s, gsem, count)
            small, dn = load_weights(f, (small_w, dn_w), (small_s, dn_s), sems)
            mine = [slice(q * far, (q + 1) * far) for q in range(count)]
            get_slope = [
                pltpu.make_async_copy(slpb.at[m + q, :, at], slp_s.at[:, mine[q]], osems.at[q, 0])
                for q in range(count)
            ]
            for copy in get_slope:
                copy.start()
            low_s[...] = jnp.zeros_like(low_s)
            done(wait_g)
            save_g = [
                pltpu.make_async_copy(g_s.at[mine[q]], gb.at[m + q, at], osems.at[q, 1]) for q in range(count)
            ]
            for copy in save_g:
                copy.start()
            done(small)
            done(dn)
            done(get_slope)
            bwd_hidden(dims, g_s, slp_s, gp_s, small_s, dn_s, dno, low_s, 2)
            outs = []
            for q in range(count):
                outs += [
                    pltpu.make_async_copy(gp_s.at[:, mine[q]], gpb.at[m + q, :, at], osems.at[q, 2]),
                    pltpu.make_async_copy(low_s.at[mine[q]], lowb.at[m + q, at], osems.at[q, 3]),
                ]
            for copy in outs:
                copy.start()
            done(save_g)
            done(outs)

    return pl.pallas_call(
        kernel,
        out_shape=tuple(jax.ShapeDtypeStruct(b.shape, b.dtype) for b in bufs)
        + (jax.ShapeDtypeStruct((8, BLK), F32),),
        in_specs=[SMEM] * 2 + [ANY] * (len(args) - 2),
        out_specs=(ANY,) * 4,
        input_output_aliases={n_plain + n: n for n in range(3)},
        scratch_shapes=[
            pltpu.VMEM((dims.hidden, BLK, BLK), BF),
            pltpu.VMEM((dims.parts, RANK, dims.packed), BF),
            pltpu.VMEM((count * far, dims.width), BF),
            pltpu.VMEM((dims.hidden, count * far, BLK), BF),
            pltpu.VMEM((dims.hidden, count * far, BLK), BF),
            pltpu.VMEM((count * far, 2 * BLK), BF),
            pltpu.SemaphoreType.DMA((8,)),
            pltpu.SemaphoreType.DMA((count, n_t)),
            pltpu.SemaphoreType.DMA((count, 4)),
        ],
        compiler_params=params(60),
        name="backward_far_rows",
    )(*args)


def weight_grads(dims, up, sc, order, blocks, wide, low_a, low_b, gain=None):
    micro, _, held, _ = blocks.shape
    total = micro * held
    group, model, mh, hh = dims.group, dims.model, dims.mh, dims.hh
    U = 4
    two = dims.parts == 2
    hid_at = mh * BLK
    gain_at = hid_at + hh * BLK
    packed = gain_at + (mh * BLK if up else 0)
    VM = pl.BlockSpec(memory_space=pltpu.VMEM)
    a_at, b_at = (0, 0) if up else (BLK, BLK)
    extra = [gain] if up else []

    def kernel(*refs):
        sc, order, blocks, wide, low_a, low_b = refs[:6]
        gain = refs[6] if up else None
        outs_hbm = refs[6 + len(extra) : -6]
        big, small, held_s, wide_s, sems, osems = refs[-6:]
        f = sc[2]
        get_wide = pltpu.make_async_copy(wide, wide_s, osems.at[0])
        get_wide.start()

        def fetch(it, slot, go):
            for u in range(U):
                for c in range(group):
                    j = order[(it * U + u) * group + c]
                    copy = pltpu.make_async_copy(
                        blocks.at[:, j], held_s.at[slot, u * group + c], sems.at[slot, u * group + c]
                    )
                    copy.start() if go else copy.wait()

        fetch(0, 0, True)

        def low_t(ref, at):
            rows = jnp.concatenate([ref[m, :, at : at + BLK] for m in range(micro)], axis=0)
            return rows.astype(F32).T[0:RANK].astype(BF)

        with_blocks, with_wide = low_t(low_a, a_at), low_t(low_b, b_at)
        get_wide.wait()

        def which(h):
            return jnp.where(h == f, 0, 1) if two else h

        def step(it, _):
            slot = lax.rem(it, 2)

            @pl.when(it + 1 < model // U)
            def _():
                fetch(it + 1, 1 - slot, True)

            fetch(it, slot, False)
            for u in range(U):
                i = it * U + u
                h = i // mh
                w = which(h)
                off = i - h * mh
                wi = jnp.concatenate([wide_s[m, :, lanes(i * BLK)] for m in range(micro)], axis=0)
                lhs = jnp.concatenate([wi.T, with_blocks], axis=0)
                rhs = jnp.concatenate(
                    [held_s[slot, u * group + c].reshape(total, BLK) for c in range(group)], axis=1
                )
                res = dot(lhs, rhs)
                for c in range(group):
                    j = order[i * group + c]
                    hj = j // hh
                    wj = which(hj)
                    part = res[:, c * BLK : (c + 1) * BLK]
                    if up:
                        big[wj, j - hj * hh] = part[0:BLK].astype(BF)
                    else:
                        big[w, off * group + c] = part[0:BLK].T.astype(BF)
                    small[wj, :, lanes(hid_at + (j - hj * hh) * BLK)] = part[BLK:].astype(BF)
                small[w, :, lanes(off * BLK)] = dot(with_wide, wi).astype(BF)
                if up:
                    small[w, :, lanes(gain_at + off * BLK)] = jnp.broadcast_to(
                        gain[0:1, lanes(i * BLK)], (RANK, BLK)
                    ).astype(BF)
            return 0

        lax.fori_loop(0, model // U, step, 0)
        outs = []
        for n, src in enumerate((big, small)):
            if two:
                outs.append(pltpu.make_async_copy(src.at[0], outs_hbm[2 * n], osems.at[2 * n]))
                outs.append(pltpu.make_async_copy(src.at[1], outs_hbm[2 * n + 1], osems.at[2 * n + 1]))
            else:
                outs.append(pltpu.make_async_copy(src, outs_hbm[n], osems.at[2 * n]))
        for copy in outs:
            copy.start()
        done(outs)

    lead = () if two else (dims.parts,)
    shapes = [lead + (hh, BLK, BLK), lead + (RANK, packed)]
    shapes = [jax.ShapeDtypeStruct(shape, BF) for shape in shapes for _ in range(2 if two else 1)]
    got = pl.pallas_call(
        kernel,
        out_shape=tuple(shapes),
        in_specs=[SMEM] * 2 + [ANY] * 2 + [VM] * (2 + len(extra)),
        out_specs=(ANY,) * len(shapes),
        scratch_shapes=[
            pltpu.VMEM((dims.parts, hh, BLK, BLK), BF),
            pltpu.VMEM((dims.parts, RANK, packed), BF),
            pltpu.VMEM((2, U * group, micro, held, BLK), BF),
            pltpu.VMEM((micro, held, dims.width), BF),
            pltpu.SemaphoreType.DMA((2, U * group)),
            pltpu.SemaphoreType.DMA((4,)),
        ],
        compiler_params=params(60),
        name="up_gradients" if up else "down_gradients",
    )(sc, order, blocks, wide, low_a, low_b, *extra)
    return [got[0:2], got[2:4]] if two else [got[0:1], got[1:2]]


def orders(up_order, dims):
    at = jnp.arange(dims.hidden, dtype=jnp.int32)
    same = (up_order[:, None] == up_order[None, :]) & (at[None, :] < at[:, None])
    place = up_order * dims.group + jnp.sum(same.astype(jnp.int32), axis=1)
    hit = place[None, :] == at[:, None]
    return jnp.sum(jnp.where(hit, at[None, :], 0), axis=1)


def shards(inputs, cotangent, norm_gain, up_blocks, down_blocks, up_left, up_right, down_left, down_right,
           up_pattern, down_pattern):
    micro, rows, width = inputs.shape
    upo, dno = up_pattern[0], down_pattern[0]
    parts = lax.axis_size("fsdp")
    dims = Dims(width, upo.shape[0], parts)
    n_sec = lax.axis_size("section")
    sec = lax.axis_index("section")
    f = lax.axis_index("fsdp")
    swap = [(0, 1), (1, 0)]
    n_dp = lax.axis_size("dp")
    held = rows * n_dp
    small = jnp.concatenate(
        [up_left[0], down_right[0], up_right[0], down_left[0],
         jnp.broadcast_to(norm_gain, (RANK, norm_gain.shape[1]))], axis=1)

    def whole_layer(own, stacked):
        if parts == 2:
            return (own, lax.ppermute(own, "fsdp", swap))
        return (lax.all_gather(own, "fsdp", axis=0, tiled=not stacked),)

    small_w = whole_layer(small, True)
    up_w = whole_layer(up_blocks[0], False)
    weights = (up_w, whole_layer(down_blocks[0], False), small_w)
    grouped = orders(upo, dims)
    zero = jnp.int32(0)

    def scalars(m, edge):
        live = (m >= 0) & (m < micro)
        return jnp.stack([live.astype(jnp.int32), jnp.clip(m, 0, micro - 1).astype(jnp.int32),
                          f.astype(jnp.int32), edge.astype(jnp.int32), zero, zero, zero, zero])

    def shifted(block, sections, k):
        pairs = [(s * n_dp + d, s * n_dp + (d + k) % n_dp) for s in sections for d in range(n_dp)]
        return lax.ppermute(block, ("section", "dp"), pairs)

    def to_dp(block, sections):
        return tuple(shifted(block, sections, k) for k in range(1, n_dp))

    def flags(live, m, source, index):
        return jnp.stack([jnp.asarray(v).astype(jnp.int32) for v in (live, m, f, source, index, 0, 0, 0)])

    state = {"token": None, "due": []}

    def chained(*arrays):
        due = tuple(v for n, v in state["due"] if n <= 0)
        state["due"] = [(n - 1, v) for n, v in state["due"] if n > 0]
        if state["token"] is not None:
            due = due + (state["token"],)
        if not due:
            return arrays
        out = lax.optimization_barrier(arrays + due)
        return out[: len(arrays)]

    shifts = [1] + list(range(n_dp - 1, 1, -1))
    queue = []

    def send_one(hold):
        if queue:
            store, k, payload, sections = queue.pop(0)
            block, _ = lax.optimization_barrier((payload(), state["token"]))
            store[k] = shifted(block, sections, k)
            state["due"].append((hold, store[k]))

    def enqueue(payload, sections):
        store = {}
        queue.extend((store, k, payload, sections) for k in shifts)
        return store

    fbufs, bbufs = None, None
    frecv = inputs[0]
    brecv = inputs[0]
    last = n_sec - 1
    edge = jnp.where(sec == 0, inputs, cotangent)
    far_edge = enqueue(lambda: edge, (0, last))

    def forward(t):
        nonlocal fbufs, frecv
        (x,) = chained(frecv)
        y, fbufs = fwd_slot(dims, scalars(t - sec, sec == 0), upo, dno, inputs, x, weights, fbufs, micro, held)
        state["token"] = y
        pairs = [(s, s + 1) for s in range(last) if 0 <= t - s < micro]
        if pairs:
            frecv = lax.ppermute(y, "section", pairs)

    def backward(t):
        nonlocal bbufs, brecv
        (g,) = chained(brecv)
        out, bbufs = bwd_slot(dims, scalars(t - (last - sec), sec == last), dno, grouped, cotangent, g,
                              weights, fbufs[3], fbufs[1], bbufs, micro, held)
        state["token"] = out
        pairs = [(last - s, last - s - 1) for s in range(last) if 0 <= t - s < micro]
        if pairs:
            brecv = lax.ppermute(out, "section", pairs)

    def forward_far(m, live, sources, source, index):
        nonlocal fbufs
        (sc,) = chained(flags(live, m, source, index))
        hidb, slpb, nrmb, xb, lowf = fbufs
        hidb, slpb, nrmb, lowf, state["token"] = fwd_far(dims, sc, upo, sources, weights, (hidb, slpb, nrmb, lowf), half)
        fbufs = (hidb, slpb, nrmb, xb, lowf)

    slots = micro + last
    half = micro // 2
    early, late = slice(0, half), slice(half, micro)
    inner, outer = list(range(1, n_sec)), list(range(last))

    def triple(store):
        return tuple(store[k] for k in range(1, n_dp))

    for t in range(slots):
        if t == slots - 1:
            forward_far(0, sec == 0, [triple(far_edge)], 0, 0)
        forward(t)
        if t < last:
            send_one(3)
        if t == slots - 1:
            x_late = enqueue(lambda: fbufs[3][late], inner)
        if t > last + 1:
            send_one(1)
        if t >= last:
            backward(t - last)
        if t == last + 1:
            x_early = enqueue(lambda: fbufs[3][early], inner)
        if t > last:
            send_one(1)
        if t == slots - 1:
            send_one(1)

    for t in range(slots - last, slots):
        backward(t)
        if t == slots - 3:
            g_early = enqueue(lambda: bbufs[1][early, 0:rows], outer)
        if t == slots - 1:
            g_late = enqueue(lambda: bbufs[1][late, 0:rows], outer)
        hold = 2 if t == slots - 1 else 1
        send_one(hold)
        if t != slots - 2:
            send_one(hold)
    gpb, gb, lowb, gain_rows = bbufs

    def far_forward(m, hold):
        if m < half:
            forward_far(m, sec > 0, [triple(x_early)], 0, m)
        else:
            forward_far(m, True, [triple(x_late), triple(far_edge)],
                        jnp.where(sec == 0, 1, 0), jnp.where(sec == 0, m, m - half))
        send_one(hold)

    def far_backward(m):
        nonlocal gpb, gb, lowb
        sources = [triple(g_early if m < half else g_late), triple(far_edge)]
        (sc,) = chained(flags(True, m, jnp.where(sec == last, 1, 0), jnp.where(sec == last, m, m % half)))
        gpb, gb, lowb, state["token"] = bwd_far(dims, sc, dno, sources, weights, fbufs[1], (gpb, gb, lowb), half)
        send_one(1)

    far_forward(0, 2)
    far_forward(half, 1)
    far_backward(0)
    while queue:
        send_one(2)
    gain = jnp.sum(gain_rows, axis=(0, 1))[None]
    for other in to_dp(gain, range(n_sec)):
        gain = gain + other
    far_backward(half)
    hidb, slpb, nrmb, _, lowf = fbufs
    sc = scalars(zero, sec == 0)

    def over_fsdp(pieces):
        if parts == 2:
            got = lax.ppermute(pieces[1], "fsdp", swap)
            return (pieces[0].astype(F32) + got.astype(F32))[None]
        return lax.psum_scatter(pieces[0], "fsdp", scatter_dimension=0, tiled=False).astype(F32)[None]

    dn_g, dn_small = weight_grads(dims, False, sc, dno, hidb, gb, lowb, lowf)
    up_g, up_small = weight_grads(dims, True, sc, grouped, gpb, nrmb, lowf, lowb, gain)
    dn, dns, up, ups = (over_fsdp(p) for p in (dn_g, dn_small, up_g, up_small))
    mw, hw = dims.mh * BLK, dims.hh * BLK
    return (
        ups[:, 0, mw + hw :],
        up,
        dn,
        ups[:, :, 0:mw],
        ups[:, :, mw : mw + hw],
        dns[:, :, mw : mw + hw],
        dns[:, :, 0:mw],
    )


def solution(mesh):
    placed = (
        P(None, ("fsdp", "dp"), None),
        P(None, ("fsdp", "dp"), None),
        P("section", "fsdp"),
        P("section", "fsdp", None, None),
        P("section", "fsdp", None, None),
        P("section", None, "fsdp"),
        P("section", None, "fsdp"),
        P("section", None, "fsdp"),
        P("section", None, "fsdp"),
        P("section", None),
        P("section", None),
    )
    return jax.shard_map(
        shards,
        mesh=mesh,
        in_specs=placed,
        out_specs=(
            P("section", "fsdp"),
            P("section", "fsdp", None, None),
            P("section", "fsdp", None, None),
            P("section", None, "fsdp"),
            P("section", None, "fsdp"),
            P("section", None, "fsdp"),
            P("section", None, "fsdp"),
        ),
        check_vma=False,
    )
```

```python
import functools

import jax
import jax.numpy as jnp
from jax import lax
from jax.experimental import pallas as pl
from jax.experimental.pallas import tpu as pltpu
from jax.sharding import PartitionSpec as P

EPSILON = 1e-05
NORMAL_PEAK = 0.3989422804014327
TAIL_SCALE = 0.3
TAIL = (
    0.11962930931947272,
    0.12075380294875883,
    0.09991439682547013,
    0.12855881360857063,
    -0.05367866289105895,
    0.20634847173237508,
    -0.15720038925639956,
    0.03567418525278745,
)
BLK = 128
RANK = 16
BF = jnp.bfloat16
F32 = jnp.float32
NN = (((1,), (0,)), ((), ()))
NT = (((1,), (1,)), ((), ()))
TN = (((0,), (0,)), ((), ()))
ANY = pl.BlockSpec(memory_space=pl.ANY)
SMEM = pl.BlockSpec(memory_space=pltpu.SMEM)


def dot(a, b, dims=NN):
    return lax.dot_general(a, b, dims, preferred_element_type=F32)


def gelu_both(value):
    bell = jnp.exp(-0.5 * value * value)
    denom = 1.0 + TAIL_SCALE * jnp.abs(value)
    guess = pl.reciprocal(denom, approx=True)
    t = guess * (2.0 - denom * guess)
    poly = jnp.full_like(t, TAIL[-1])
    for coef in TAIL[-2::-1]:
        poly = poly * t + coef
    tail = bell * (t * poly)
    cdf = jnp.where(value < 0.0, tail, 1.0 - tail)
    return value * cdf, cdf + value * (bell * NORMAL_PEAK)


class Dims:
    def __init__(self, width, hidden_blocks, parts):
        self.parts = parts
        self.width = width
        self.model = width // BLK
        self.hidden = hidden_blocks
        self.group = hidden_blocks // self.model
        self.mh = self.model // parts
        self.hh = hidden_blocks // parts
        self.ul = 0
        self.dr = self.mh * BLK
        self.ur = 2 * self.mh * BLK
        self.dl = self.ur + self.hh * BLK
        self.gain = self.dl + self.hh * BLK
        self.packed = self.gain + self.mh * BLK


def lanes(start, count=BLK):
    return pl.ds(pl.multiple_of(start, BLK), count)


def load_weights(f, srcs, dsts, sems, first=0):
    copies = []
    for n, (src, dst) in enumerate(zip(srcs, dsts), first):
        if len(src) == 1:
            whole = pltpu.make_async_copy(src[0], dst, sems.at[2 * n])
            whole.start()
            copies.append((whole,))
            continue
        own, other = src
        half = dst.shape[0] // 2
        if own.ndim < dst.ndim:
            mine, theirs = f, 1 - f
        else:
            mine, theirs = pl.ds(f * half, half), pl.ds((1 - f) * half, half)
        a = pltpu.make_async_copy(own, dst.at[mine], sems.at[2 * n])
        b = pltpu.make_async_copy(other, dst.at[theirs], sems.at[2 * n + 1])
        a.start()
        b.start()
        copies.append((a, b))
    return copies


def done(pair):
    for copy in pair:
        copy.wait()


def inverse_rms(x_s, dims):
    rows = x_s.shape[0]
    total = jnp.zeros((rows, BLK), F32)
    for i in range(dims.model):
        part = x_s[:, i * BLK : (i + 1) * BLK].astype(F32)
        total = total + part * part
    return lax.rsqrt(jnp.sum(total, axis=1, keepdims=True) * (1.0 / dims.width) + EPSILON)


def fwd_norm(dims, x_s, small_s, nrm_s, low_s):
    rows = x_s.shape[0]
    r = inverse_rms(x_s, dims)
    upl = jnp.zeros((rows, RANK), F32)
    for h in range(dims.parts):
        for i in range(dims.mh):
            at = (h * dims.mh + i) * BLK
            gain = small_s[h, 0:1, dims.gain + i * BLK : dims.gain + (i + 1) * BLK].astype(F32)
            nrm_s[:, at : at + BLK] = (x_s[:, at : at + BLK].astype(F32) * r * gain).astype(BF)
        upl = upl + dot(
            nrm_s[:, h * dims.mh * BLK : (h + 1) * dims.mh * BLK],
            small_s[h, :, dims.ul : dims.ul + dims.mh * BLK],
            NT,
        )
    low_s[:, 0:RANK] = upl.astype(BF)


def fwd_hidden(dims, small_s, up_s, upo, nrm_s, hid_s, slp_s, low_s, G=32):
    rows = nrm_s.shape[0]
    G = min(G, dims.hh)
    upl = low_s[:, 0:RANK]

    def step(it, low):
        j0 = it * G
        h = j0 // dims.hh
        off = (j0 - h * dims.hh) * BLK
        ur = small_s[h, :, lanes(dims.ur + off, G * BLK)]
        dl = small_s[h, :, lanes(dims.dl + off, G * BLK)]
        hids = []
        for g in range(G):
            src = nrm_s[:, lanes(upo[j0 + g] * BLK)]
            lhs = jnp.concatenate([src, upl], axis=1)
            rhs = jnp.concatenate([up_s[j0 + g], ur[:, g * BLK : (g + 1) * BLK]], axis=0)
            hid, slope = gelu_both(dot(lhs, rhs))
            hid = hid.astype(BF)
            hid_s[j0 + g] = hid
            slp_s[j0 + g] = slope.astype(BF)
            hids.append(hid)
        return low + dot(jnp.concatenate(hids, axis=1), dl, NT)

    low = lax.fori_loop(0, dims.hidden // G, step, jnp.zeros((rows, RANK), F32)).astype(BF)
    low_s[:, BLK : BLK + RANK] = low
    return low


def fwd_down(dims, low, x_s, small_s, dn_s, dno, hid_s, y_s):
    def down(it, _):
        for u in range(8):
            i = it * 8 + u
            h = i // dims.mh
            at = i * BLK
            dr = small_s[h, :, lanes(dims.dr + (i - h * dims.mh) * BLK)]
            parts = [hid_s[dno[i * dims.group + c]] for c in range(dims.group)]
            lhs = jnp.concatenate(parts + [low], axis=1)
            blocks = dn_s[pl.ds(i * dims.group, dims.group)].reshape(dims.group * BLK, BLK)
            mixed = dot(lhs, jnp.concatenate([blocks, dr], axis=0))
            y_s[:, lanes(at)] = (x_s[:, lanes(at)].astype(F32) + mixed).astype(BF)
        return 0

    lax.fori_loop(0, dims.model // 8, down, 0)


def bwd_hidden(dims, g_s, slp_s, gp_s, small_s, dn_s, dno, low_s, U=8):
    rows = g_s.shape[0]
    gdl = jnp.zeros((rows, RANK), F32)
    for h in range(dims.parts):
        gdl = gdl + dot(
            g_s[:, h * dims.mh * BLK : (h + 1) * dims.mh * BLK],
            small_s[h, :, dims.dr : dims.dr + dims.mh * BLK],
            NT,
        )
    gdl = gdl.astype(BF)
    low_s[:, BLK : BLK + RANK] = gdl

    def hid_step(it, gul):
        for u in range(U):
            i = it * U + u
            gi = g_s[:, lanes(i * BLK)]
            js = [dno[i * dims.group + c] for c in range(dims.group)]
            hs = [j // dims.hh for j in js]
            offs = [(j - h * dims.hh) * BLK for j, h in zip(js, hs)]
            dl = jnp.concatenate([small_s[h, :, lanes(dims.dl + o)] for h, o in zip(hs, offs)], axis=1)
            ur = jnp.concatenate([small_s[h, :, lanes(dims.ur + o)] for h, o in zip(hs, offs)], axis=1)
            blocks = dn_s[pl.ds(i * dims.group, dims.group)].reshape(dims.group * BLK, BLK)
            gh = dot(gi, blocks, NT) + dot(gdl, dl)
            slope = jnp.concatenate([slp_s[j] for j in js], axis=1).astype(F32)
            gp = (gh * slope).astype(BF)
            for c, j in enumerate(js):
                gp_s[j] = gp[:, c * BLK : (c + 1) * BLK]
            gul = gul + dot(gp, ur, NT)
        return gul

    gul = lax.fori_loop(0, dims.model // U, hid_step, jnp.zeros((rows, RANK), F32))
    gul = gul.astype(BF)
    low_s[:, 0:RANK] = gul
    return gul


def bwd_input(dims, x_s, g_s, gp_s, small_s, up_s, grouped, gul, gn_s, gain_s, out_s):
    rows = g_s.shape[0]
    r = inverse_rms(x_s, dims)

    def step(it, acc):
        for u in range(8):
            i = it * 8 + u
            h = i // dims.mh
            off = (i - h * dims.mh) * BLK
            js = [grouped[i * dims.group + c] for c in range(dims.group)]
            lhs = jnp.concatenate([gp_s[j] for j in js], axis=1)
            rhs = jnp.concatenate([up_s[j] for j in js], axis=1)
            gn = dot(lhs, rhs, NT) + dot(gul, small_s[h, :, lanes(dims.ul + off)])
            x = x_s[:, lanes(i * BLK)].astype(F32)
            gain = small_s[h, 0:1, lanes(dims.gain + off)].astype(F32)
            scaled = gn * gain
            gn_s[:, lanes(i * BLK)] = scaled
            gain_s[0:1, lanes(i * BLK)] = jnp.sum(gn * x * r, axis=0, keepdims=True)
            acc = acc + x * scaled
        return acc

    acc = lax.fori_loop(0, dims.model // 8, step, jnp.zeros((rows, BLK), F32))
    shift = jnp.sum(acc, axis=1, keepdims=True) * (1.0 / dims.width) * (r * r * r)
    for i in range(dims.model):
        at = slice(i * BLK, (i + 1) * BLK)
        out_s[:, at] = (
            g_s[:, at].astype(F32) + r * gn_s[:, at] - x_s[:, at].astype(F32) * shift
        ).astype(BF)


def params(mib):
    return pltpu.CompilerParams(vmem_limit_bytes=mib * 1024 * 1024)


def fwd_slot(dims, sc, upo, dno, first, recv, weights, bufs, micro, held):
    rows = recv.shape[0]
    n_buf = 5
    shapes = (
        jax.ShapeDtypeStruct((micro, dims.hidden, held, BLK), BF),
        jax.ShapeDtypeStruct((micro, dims.hidden, held, BLK), BF),
        jax.ShapeDtypeStruct((micro, held, dims.width), BF),
        jax.ShapeDtypeStruct((micro, rows, dims.width), BF),
        jax.ShapeDtypeStruct((micro, held, 2 * BLK), BF),
    )
    n_w = len(weights[0])
    n_in = 5 + 3 * n_w + (n_buf if bufs is not None else 0)

    def kernel(*refs):
        sc, upo, dno, first, recv = refs[:5]
        up_w, dn_w, small_w = (refs[5 + k * n_w : 5 + (k + 1) * n_w] for k in range(3))
        y, hidb, slpb, nrmb, xb, lowb = refs[n_in : n_in + 6]
        up_s, dn_s, small_s, x_s, nrm_s, hid_s, slp_s, low_s, y_s, sems = refs[n_in + 6 :]

        @pl.when(sc[0] == 1)
        def _():
            m, f = sc[1], sc[2]

            @pl.when(sc[3] == 1)
            def _():
                pltpu.make_async_copy(first.at[m], x_s, sems.at[6]).start()

            @pl.when(sc[3] == 0)
            def _():
                pltpu.make_async_copy(recv, x_s, sems.at[6]).start()

            wait_x = pltpu.make_async_copy(recv, x_s, sems.at[6])
            small, up = load_weights(f, (small_w, up_w), (small_s, up_s), sems)
            low_s[...] = jnp.zeros_like(low_s)
            wait_x.wait()
            save_x = pltpu.make_async_copy(x_s, xb.at[m], sems.at[7])
            save_x.start()
            done(small)
            fwd_norm(dims, x_s, small_s, nrm_s, low_s)
            done(up)
            (dn,) = load_weights(f, (dn_w,), (dn_s,), sems, 2)
            low = fwd_hidden(dims, small_s, up_s, upo, nrm_s, hid_s, slp_s, low_s)
            outs = [
                pltpu.make_async_copy(hid_s, hidb.at[m, :, 0:rows], sems.at[9]),
                pltpu.make_async_copy(slp_s, slpb.at[m, :, 0:rows], sems.at[10]),
                pltpu.make_async_copy(nrm_s, nrmb.at[m, 0:rows], sems.at[11]),
                pltpu.make_async_copy(low_s, lowb.at[m, 0:rows], sems.at[12]),
            ]
            for copy in outs:
                copy.start()
            done(dn)
            fwd_down(dims, low, x_s, small_s, dn_s, dno, hid_s, y_s)
            outs.append(pltpu.make_async_copy(y_s, y, sems.at[8]))
            outs[-1].start()
            save_x.wait()
            done(outs)

    args = [sc, upo, dno, first, recv] + [w for pair in weights for w in pair]
    aliases = {}
    if bufs is not None:
        aliases = {len(args) + n: n + 1 for n in range(n_buf)}
        args += list(bufs)
    out = pl.pallas_call(
        kernel,
        out_shape=(jax.ShapeDtypeStruct((rows, dims.width), BF),) + shapes,
        in_specs=[SMEM] * 3 + [ANY] * (len(args) - 3),
        out_specs=(ANY,) * 6,
        input_output_aliases=aliases,
        scratch_shapes=[
            pltpu.VMEM((dims.hidden, BLK, BLK), BF),
            pltpu.VMEM((dims.hidden, BLK, BLK), BF),
            pltpu.VMEM((dims.parts, RANK, dims.packed), BF),
            pltpu.VMEM((rows, dims.width), BF),
            pltpu.VMEM((rows, dims.width), BF),
            pltpu.VMEM((dims.hidden, rows, BLK), BF),
            pltpu.VMEM((dims.hidden, rows, BLK), BF),
            pltpu.VMEM((rows, 2 * BLK), BF),
            pltpu.VMEM((rows, dims.width), BF),
            pltpu.SemaphoreType.DMA((13,)),
        ],
        compiler_params=params(60),
        name="forward_rows",
    )(*args)
    return out[0], out[1:]


def bwd_slot(dims, sc, dno, grouped, last, recv, weights, xb, slpb, bufs, micro, held):
    rows = recv.shape[0]
    n_buf = 4
    shapes = (
        jax.ShapeDtypeStruct((micro, dims.hidden, held, BLK), BF),
        jax.ShapeDtypeStruct((micro, held, dims.width), BF),
        jax.ShapeDtypeStruct((micro, held, 2 * BLK), BF),
        jax.ShapeDtypeStruct((micro, 8, dims.width), F32),
    )
    n_w = len(weights[0])
    n_in = 7 + 3 * n_w + (n_buf if bufs is not None else 0)

    def kernel(*refs):
        sc, dno, grouped, last, recv = refs[:5]
        up_w, dn_w, small_w = (refs[5 + k * n_w : 5 + (k + 1) * n_w] for k in range(3))
        xb, slpb = refs[5 + 3 * n_w : 7 + 3 * n_w]
        out, gpb, gb, lowb, gainb = refs[n_in : n_in + 5]
        up_s, dn_s, small_s, x_s, g_s, slp_s, gp_s, low_s, gn_s, gain_s, out_s, sems = refs[n_in + 5 :]

        @pl.when(sc[0] == 1)
        def _():
            m, f = sc[1], sc[2]

            @pl.when(sc[3] == 1)
            def _():
                pltpu.make_async_copy(last.at[m], g_s, sems.at[6]).start()

            @pl.when(sc[3] == 0)
            def _():
                pltpu.make_async_copy(recv, g_s, sems.at[6]).start()

            wait_g = pltpu.make_async_copy(recv, g_s, sems.at[6])
            get_slope = pltpu.make_async_copy(slpb.at[m, :, 0:rows], slp_s, sems.at[7])
            get_x = pltpu.make_async_copy(xb.at[m], x_s, sems.at[8])
            small, dn = load_weights(f, (small_w, dn_w), (small_s, dn_s), sems)
            get_slope.start()
            low_s[...] = jnp.zeros_like(low_s)
            gain_s[...] = jnp.zeros_like(gain_s)
            wait_g.wait()
            save_g = pltpu.make_async_copy(g_s, gb.at[m, 0:rows], sems.at[9])
            save_g.start()
            done(small)
            get_slope.wait()
            done(dn)
            (up,) = load_weights(f, (up_w,), (up_s,), sems, 2)
            get_x.start()
            gul = bwd_hidden(dims, g_s, slp_s, gp_s, small_s, dn_s, dno, low_s)
            outs = [
                pltpu.make_async_copy(gp_s, gpb.at[m, :, 0:rows], sems.at[10]),
                pltpu.make_async_copy(low_s, lowb.at[m, 0:rows], sems.at[11]),
            ]
            for copy in outs:
                copy.start()
            get_x.wait()
            done(up)
            bwd_input(dims, x_s, g_s, gp_s, small_s, up_s, grouped, gul, gn_s, gain_s, out_s)
            more = [
                pltpu.make_async_copy(gain_s, gainb.at[m], sems.at[12]),
                pltpu.make_async_copy(out_s, out, sems.at[13]),
            ]
            for copy in more:
                copy.start()
            save_g.wait()
            done(outs)
            done(more)

    args = [sc, dno, grouped, last, recv] + [w for pair in weights for w in pair] + [xb, slpb]
    aliases = {}
    if bufs is not None:
        aliases = {len(args) + n: n + 1 for n in range(n_buf)}
        args += list(bufs)
    out = pl.pallas_call(
        kernel,
        out_shape=(jax.ShapeDtypeStruct((rows, dims.width), BF),) + shapes,
        in_specs=[SMEM] * 3 + [ANY] * (len(args) - 3),
        out_specs=(ANY,) * 5,
        input_output_aliases=aliases,
        scratch_shapes=[
            pltpu.VMEM((dims.hidden, BLK, BLK), BF),
            pltpu.VMEM((dims.hidden, BLK, BLK), BF),
            pltpu.VMEM((dims.parts, RANK, dims.packed), BF),
            pltpu.VMEM((rows, dims.width), BF),
            pltpu.VMEM((rows, dims.width), BF),
            pltpu.VMEM((dims.hidden, rows, BLK), BF),
            pltpu.VMEM((dims.hidden, rows, BLK), BF),
            pltpu.VMEM((rows, 2 * BLK), BF),
            pltpu.VMEM((rows, dims.width), F32),
            pltpu.VMEM((8, dims.width), F32),
            pltpu.VMEM((rows, dims.width), BF),
            pltpu.SemaphoreType.DMA((14,)),
        ],
        compiler_params=params(60),
        name="backward_rows",
    )(*args)
    return out[0], out[1:]


def pick_rows(sc, sources, dst, sem, count):
    n = dst.shape[0] // (len(sources[0]) * count)
    places = [(q, t, (q * len(sources[0]) + t) * n) for q in range(count) for t in range(len(sources[0]))]
    for number, triple in enumerate(sources):

        @pl.when(sc[3] == number)
        def _():
            for q, t, at in places:
                pltpu.make_async_copy(triple[t].at[sc[4] + q], dst.at[at : at + n], sem.at[q, t]).start()

    return tuple(
        pltpu.make_async_copy(sources[0][t].at[0], dst.at[at : at + n], sem.at[q, t]) for q, t, at in places
    )


def fwd_far(dims, sc, upo, sources, weights, bufs, count):
    hidb, slpb, nrmb, lowb = bufs
    rows = sources[0][0].shape[1]
    far = rows * len(sources[0])
    n_w, n_t, n_q = len(weights[0]), len(sources[0]), len(sources)
    args = [sc, upo] + list(weights[0]) + list(weights[2]) + [a for triple in sources for a in triple]
    n_plain = len(args)
    args += list(bufs)

    def kernel(*refs):
        sc, upo = refs[:2]
        up_w, small_w = refs[2 : 2 + n_w], refs[2 + n_w : 2 + 2 * n_w]
        base = 2 + 2 * n_w
        srcs = [refs[base + q * n_t : base + (q + 1) * n_t] for q in range(n_q)]
        hidb, slpb, nrmb, lowb = refs[n_plain + 4 : n_plain + 8]
        up_s, small_s, x_s, nrm_s, hid_s, slp_s, low_s, sems, xsem, osems = refs[n_plain + 9 :]

        @pl.when(sc[0] == 1)
        def _():
            m, f = sc[1], sc[2]
            wait_x = pick_rows(sc, srcs, x_s, xsem, count)
            small, up = load_weights(f, (small_w, up_w), (small_s, up_s), sems)
            low_s[...] = jnp.zeros_like(low_s)
            done(wait_x)
            done(small)
            fwd_norm(dims, x_s, small_s, nrm_s, low_s)
            done(up)
            fwd_hidden(dims, small_s, up_s, upo, nrm_s, hid_s, slp_s, low_s, 4)
            at = slice(rows, rows + far)
            outs = []
            for q in range(count):
                mine = slice(q * far, (q + 1) * far)
                outs += [
                    pltpu.make_async_copy(hid_s.at[:, mine], hidb.at[m + q, :, at], osems.at[q, 0]),
                    pltpu.make_async_copy(slp_s.at[:, mine], slpb.at[m + q, :, at], osems.at[q, 1]),
                    pltpu.make_async_copy(nrm_s.at[mine], nrmb.at[m + q, at], osems.at[q, 2]),
                    pltpu.make_async_copy(low_s.at[mine], lowb.at[m + q, at], osems.at[q, 3]),
                ]
            for copy in outs:
                copy.start()
            done(outs)

    return pl.pallas_call(
        kernel,
        out_shape=tuple(jax.ShapeDtypeStruct(b.shape, b.dtype) for b in bufs)
        + (jax.ShapeDtypeStruct((8, BLK), F32),),
        in_specs=[SMEM] * 2 + [ANY] * (len(args) - 2),
        out_specs=(ANY,) * 5,
        input_output_aliases={n_plain + n: n for n in range(4)},
        scratch_shapes=[
            pltpu.VMEM((dims.hidden, BLK, BLK), BF),
            pltpu.VMEM((dims.parts, RANK, dims.packed), BF),
            pltpu.VMEM((count * far, dims.width), BF),
            pltpu.VMEM((count * far, dims.width), BF),
            pltpu.VMEM((dims.hidden, count * far, BLK), BF),
            pltpu.VMEM((dims.hidden, count * far, BLK), BF),
            pltpu.VMEM((count * far, 2 * BLK), BF),
            pltpu.SemaphoreType.DMA((8,)),
            pltpu.SemaphoreType.DMA((count, n_t)),
            pltpu.SemaphoreType.DMA((count, 4)),
        ],
        compiler_params=params(60),
        name="forward_far_rows",
    )(*args)


def bwd_far(dims, sc, dno, sources, weights, slpb, bufs, count):
    rows = sources[0][0].shape[1]
    far = rows * len(sources[0])
    n_w, n_t, n_q = len(weights[0]), len(sources[0]), len(sources)
    args = [sc, dno] + list(weights[1]) + list(weights[2]) + [a for triple in sources for a in triple] + [slpb]
    n_plain = len(args)
    args += list(bufs)

    def kernel(*refs):
        sc, dno = refs[:2]
        dn_w, small_w = refs[2 : 2 + n_w], refs[2 + n_w : 2 + 2 * n_w]
        base = 2 + 2 * n_w
        srcs = [refs[base + q * n_t : base + (q + 1) * n_t] for q in range(n_q)]
        slpb = refs[n_plain - 1]
        gpb, gb, lowb = refs[n_plain + 3 : n_plain + 6]
        dn_s, small_s, g_s, slp_s, gp_s, low_s, sems, gsem, osems = refs[n_plain + 7 :]

        @pl.when(sc[0] == 1)
        def _():
            m, f = sc[1], sc[2]
            at = slice(rows, rows + far)
            wait_g = pick_rows(sc, srcs, g_s, gsem, count)
            small, dn = load_weights(f, (small_w, dn_w), (small_s, dn_s), sems)
            mine = [slice(q * far, (q + 1) * far) for q in range(count)]
            get_slope = [
                pltpu.make_async_copy(slpb.at[m + q, :, at], slp_s.at[:, mine[q]], osems.at[q, 0])
                for q in range(count)
            ]
            for copy in get_slope:
                copy.start()
            low_s[...] = jnp.zeros_like(low_s)
            done(wait_g)
            save_g = [
                pltpu.make_async_copy(g_s.at[mine[q]], gb.at[m + q, at], osems.at[q, 1]) for q in range(count)
            ]
            for copy in save_g:
                copy.start()
            done(small)
            done(dn)
            done(get_slope)
            bwd_hidden(dims, g_s, slp_s, gp_s, small_s, dn_s, dno, low_s, 2)
            outs = []
            for q in range(count):
                outs += [
                    pltpu.make_async_copy(gp_s.at[:, mine[q]], gpb.at[m + q, :, at], osems.at[q, 2]),
                    pltpu.make_async_copy(low_s.at[mine[q]], lowb.at[m + q, at], osems.at[q, 3]),
                ]
            for copy in outs:
                copy.start()
            done(save_g)
            done(outs)

    return pl.pallas_call(
        kernel,
        out_shape=tuple(jax.ShapeDtypeStruct(b.shape, b.dtype) for b in bufs)
        + (jax.ShapeDtypeStruct((8, BLK), F32),),
        in_specs=[SMEM] * 2 + [ANY] * (len(args) - 2),
        out_specs=(ANY,) * 4,
        input_output_aliases={n_plain + n: n for n in range(3)},
        scratch_shapes=[
            pltpu.VMEM((dims.hidden, BLK, BLK), BF),
            pltpu.VMEM((dims.parts, RANK, dims.packed), BF),
            pltpu.VMEM((count * far, dims.width), BF),
            pltpu.VMEM((dims.hidden, count * far, BLK), BF),
            pltpu.VMEM((dims.hidden, count * far, BLK), BF),
            pltpu.VMEM((count * far, 2 * BLK), BF),
            pltpu.SemaphoreType.DMA((8,)),
            pltpu.SemaphoreType.DMA((count, n_t)),
            pltpu.SemaphoreType.DMA((count, 4)),
        ],
        compiler_params=params(60),
        name="backward_far_rows",
    )(*args)


def weight_grads(dims, up, sc, order, blocks, wide, low_a, low_b, gain=None):
    micro, _, held, _ = blocks.shape
    total = micro * held
    group, model, mh, hh = dims.group, dims.model, dims.mh, dims.hh
    U = 4
    two = dims.parts == 2
    hid_at = mh * BLK
    gain_at = hid_at + hh * BLK
    packed = gain_at + (mh * BLK if up else 0)
    VM = pl.BlockSpec(memory_space=pltpu.VMEM)
    a_at, b_at = (0, 0) if up else (BLK, BLK)
    extra = [gain] if up else []

    def kernel(*refs):
        sc, order, blocks, wide, low_a, low_b = refs[:6]
        gain = refs[6] if up else None
        outs_hbm = refs[6 + len(extra) : -6]
        big, small, held_s, wide_s, sems, osems = refs[-6:]
        f = sc[2]
        get_wide = pltpu.make_async_copy(wide, wide_s, osems.at[0])
        get_wide.start()

        def fetch(it, slot, go):
            for u in range(U):
                for c in range(group):
                    j = order[(it * U + u) * group + c]
                    copy = pltpu.make_async_copy(
                        blocks.at[:, j], held_s.at[slot, u * group + c], sems.at[slot, u * group + c]
                    )
                    copy.start() if go else copy.wait()

        fetch(0, 0, True)

        def low_t(ref, at):
            rows = jnp.concatenate([ref[m, :, at : at + BLK] for m in range(micro)], axis=0)
            return rows.astype(F32).T[0:RANK].astype(BF)

        with_blocks, with_wide = low_t(low_a, a_at), low_t(low_b, b_at)
        get_wide.wait()

        def which(h):
            return jnp.where(h == f, 0, 1) if two else h

        def step(it, _):
            slot = lax.rem(it, 2)

            @pl.when(it + 1 < model // U)
            def _():
                fetch(it + 1, 1 - slot, True)

            fetch(it, slot, False)
            for u in range(U):
                i = it * U + u
                h = i // mh
                w = which(h)
                off = i - h * mh
                wi = jnp.concatenate([wide_s[m, :, lanes(i * BLK)] for m in range(micro)], axis=0)
                lhs = jnp.concatenate([wi.T, with_blocks], axis=0)
                rhs = jnp.concatenate(
                    [held_s[slot, u * group + c].reshape(total, BLK) for c in range(group)], axis=1
                )
                res = dot(lhs, rhs)
                for c in range(group):
                    j = order[i * group + c]
                    hj = j // hh
                    wj = which(hj)
                    part = res[:, c * BLK : (c + 1) * BLK]
                    if up:
                        big[wj, j - hj * hh] = part[0:BLK].astype(BF)
                    else:
                        big[w, off * group + c] = part[0:BLK].T.astype(BF)
                    small[wj, :, lanes(hid_at + (j - hj * hh) * BLK)] = part[BLK:].astype(BF)
                small[w, :, lanes(off * BLK)] = dot(with_wide, wi).astype(BF)
                if up:
                    small[w, :, lanes(gain_at + off * BLK)] = jnp.broadcast_to(
                        gain[0:1, lanes(i * BLK)], (RANK, BLK)
                    ).astype(BF)
            return 0

        lax.fori_loop(0, model // U, step, 0)
        outs = []
        for n, src in enumerate((big, small)):
            if two:
                outs.append(pltpu.make_async_copy(src.at[0], outs_hbm[2 * n], osems.at[2 * n]))
                outs.append(pltpu.make_async_copy(src.at[1], outs_hbm[2 * n + 1], osems.at[2 * n + 1]))
            else:
                outs.append(pltpu.make_async_copy(src, outs_hbm[n], osems.at[2 * n]))
        for copy in outs:
            copy.start()
        done(outs)

    lead = () if two else (dims.parts,)
    shapes = [lead + (hh, BLK, BLK), lead + (RANK, packed)]
    shapes = [jax.ShapeDtypeStruct(shape, BF) for shape in shapes for _ in range(2 if two else 1)]
    got = pl.pallas_call(
        kernel,
        out_shape=tuple(shapes),
        in_specs=[SMEM] * 2 + [ANY] * 2 + [VM] * (2 + len(extra)),
        out_specs=(ANY,) * len(shapes),
        scratch_shapes=[
            pltpu.VMEM((dims.parts, hh, BLK, BLK), BF),
            pltpu.VMEM((dims.parts, RANK, packed), BF),
            pltpu.VMEM((2, U * group, micro, held, BLK), BF),
            pltpu.VMEM((micro, held, dims.width), BF),
            pltpu.SemaphoreType.DMA((2, U * group)),
            pltpu.SemaphoreType.DMA((4,)),
        ],
        compiler_params=params(60),
        name="up_gradients" if up else "down_gradients",
    )(sc, order, blocks, wide, low_a, low_b, *extra)
    return [got[0:2], got[2:4]] if two else [got[0:1], got[1:2]]


def orders(up_order, dims):
    at = jnp.arange(dims.hidden, dtype=jnp.int32)
    same = (up_order[:, None] == up_order[None, :]) & (at[None, :] < at[:, None])
    place = up_order * dims.group + jnp.sum(same.astype(jnp.int32), axis=1)
    hit = place[None, :] == at[:, None]
    return jnp.sum(jnp.where(hit, at[None, :], 0), axis=1)


def shards(inputs, cotangent, norm_gain, up_blocks, down_blocks, up_left, up_right, down_left, down_right,
           up_pattern, down_pattern):
    micro, rows, width = inputs.shape
    upo, dno = up_pattern[0], down_pattern[0]
    parts = lax.axis_size("fsdp")
    dims = Dims(width, upo.shape[0], parts)
    n_sec = lax.axis_size("section")
    sec = lax.axis_index("section")
    f = lax.axis_index("fsdp")
    swap = [(0, 1), (1, 0)]
    n_dp = lax.axis_size("dp")
    held = rows * n_dp
    small = jnp.concatenate(
        [up_left[0], down_right[0], up_right[0], down_left[0],
         jnp.broadcast_to(norm_gain, (RANK, norm_gain.shape[1]))], axis=1)

    def whole_layer(own, stacked):
        if parts == 2:
            return (own, lax.ppermute(own, "fsdp", swap))
        return (lax.all_gather(own, "fsdp", axis=0, tiled=not stacked),)

    small_w = whole_layer(small, True)
    up_w = whole_layer(up_blocks[0], False)
    weights = (up_w, whole_layer(down_blocks[0], False), small_w)
    grouped = orders(upo, dims)
    zero = jnp.int32(0)

    def scalars(m, edge):
        live = (m >= 0) & (m < micro)
        return jnp.stack([live.astype(jnp.int32), jnp.clip(m, 0, micro - 1).astype(jnp.int32),
                          f.astype(jnp.int32), edge.astype(jnp.int32), zero, zero, zero, zero])

    def shifted(block, sections, k):
        pairs = [(s * n_dp + d, s * n_dp + (d + k) % n_dp) for s in sections for d in range(n_dp)]
        return lax.ppermute(block, ("section", "dp"), pairs)

    def to_dp(block, sections):
        return tuple(shifted(block, sections, k) for k in range(1, n_dp))

    def flags(live, m, source, index):
        return jnp.stack([jnp.asarray(v).astype(jnp.int32) for v in (live, m, f, source, index, 0, 0, 0)])

    state = {"token": None, "due": []}

    def chained(*arrays):
        due = tuple(v for n, v in state["due"] if n <= 0)
        state["due"] = [(n - 1, v) for n, v in state["due"] if n > 0]
        if state["token"] is not None:
            due = due + (state["token"],)
        if not due:
            return arrays
        out = lax.optimization_barrier(arrays + due)
        return out[: len(arrays)]

    shifts = [1] + list(range(n_dp - 1, 1, -1))
    queue = []

    def send_one(hold):
        if queue:
            store, k, payload, sections = queue.pop(0)
            block, _ = lax.optimization_barrier((payload(), state["token"]))
            store[k] = shifted(block, sections, k)
            state["due"].append((hold, store[k]))

    def enqueue(payload, sections):
        store = {}
        queue.extend((store, k, payload, sections) for k in shifts)
        return store

    fbufs, bbufs = None, None
    frecv = inputs[0]
    brecv = inputs[0]
    last = n_sec - 1
    edge = jnp.where(sec == 0, inputs, cotangent)
    far_edge = enqueue(lambda: edge, (0, last))

    def forward(t):
        nonlocal fbufs, frecv
        (x,) = chained(frecv)
        y, fbufs = fwd_slot(dims, scalars(t - sec, sec == 0), upo, dno, inputs, x, weights, fbufs, micro, held)
        state["token"] = y
        pairs = [(s, s + 1) for s in range(last) if 0 <= t - s < micro]
        if pairs:
            frecv = lax.ppermute(y, "section", pairs)

    def backward(t):
        nonlocal bbufs, brecv
        (g,) = chained(brecv)
        out, bbufs = bwd_slot(dims, scalars(t - (last - sec), sec == last), dno, grouped, cotangent, g,
                              weights, fbufs[3], fbufs[1], bbufs, micro, held)
        state["token"] = out
        pairs = [(last - s, last - s - 1) for s in range(last) if 0 <= t - s < micro]
        if pairs:
            brecv = lax.ppermute(out, "section", pairs)

    def forward_far(m, live, sources, source, index):
        nonlocal fbufs
        (sc,) = chained(flags(live, m, source, index))
        hidb, slpb, nrmb, xb, lowf = fbufs
        hidb, slpb, nrmb, lowf, state["token"] = fwd_far(dims, sc, upo, sources, weights, (hidb, slpb, nrmb, lowf), half)
        fbufs = (hidb, slpb, nrmb, xb, lowf)

    slots = micro + last
    half = micro // 2
    early, late = slice(0, half), slice(half, micro)
    inner, outer = list(range(1, n_sec)), list(range(last))

    def triple(store):
        return tuple(store[k] for k in range(1, n_dp))

    for t in range(slots):
        if t == slots - 1:
            forward_far(0, sec == 0, [triple(far_edge)], 0, 0)
        forward(t)
        if t < last:
            send_one(3)
        if t == slots - 1:
            x_late = enqueue(lambda: fbufs[3][late], inner)
        if t > last + 1:
            send_one(1)
        if t >= last:
            backward(t - last)
        if t == last + 1:
            x_early = enqueue(lambda: fbufs[3][early], inner)
        if t > last:
            send_one(1)
        if t == slots - 1:
            send_one(1)

    for t in range(slots - last, slots):
        backward(t)
        if t == slots - 3:
            g_early = enqueue(lambda: bbufs[1][early, 0:rows], outer)
        if t == slots - 1:
            g_late = enqueue(lambda: bbufs[1][late, 0:rows], outer)
        hold = 2 if t == slots - 1 else 1
        send_one(hold)
        if t != slots - 2:
            send_one(hold)
        else:
            forward_far(0, sec > 0, [triple(x_early)], 0, 0)
    gpb, gb, lowb, gain_rows = bbufs

    def far_backward(m):
        nonlocal gpb, gb, lowb
        sources = [triple(g_early if m < half else g_late), triple(far_edge)]
        (sc,) = chained(flags(True, m, jnp.where(sec == last, 1, 0), jnp.where(sec == last, m, m % half)))
        gpb, gb, lowb, state["token"] = bwd_far(dims, sc, dno, sources, weights, fbufs[1], (gpb, gb, lowb), half)
        send_one(1)

    forward_far(half, True, [triple(x_late), triple(far_edge)], jnp.where(sec == 0, 1, 0), jnp.where(sec == 0, half, 0))
    send_one(1)
    far_backward(0)
    while queue:
        send_one(2)
    gain = jnp.sum(gain_rows, axis=(0, 1))[None]
    for other in to_dp(gain, range(n_sec)):
        gain = gain + other
    far_backward(half)
    hidb, slpb, nrmb, _, lowf = fbufs
    sc = scalars(zero, sec == 0)

    def over_fsdp(pieces):
        if parts == 2:
            got = lax.ppermute(pieces[1], "fsdp", swap)
            return (pieces[0].astype(F32) + got.astype(F32))[None]
        return lax.psum_scatter(pieces[0], "fsdp", scatter_dimension=0, tiled=False).astype(F32)[None]

    dn_g, dn_small = weight_grads(dims, False, sc, dno, hidb, gb, lowb, lowf)
    up_g, up_small = weight_grads(dims, True, sc, grouped, gpb, nrmb, lowf, lowb, gain)
    dn, dns, up, ups = (over_fsdp(p) for p in (dn_g, dn_small, up_g, up_small))
    mw, hw = dims.mh * BLK, dims.hh * BLK
    return (
        ups[:, 0, mw + hw :],
        up,
        dn,
        ups[:, :, 0:mw],
        ups[:, :, mw : mw + hw],
        dns[:, :, mw : mw + hw],
        dns[:, :, 0:mw],
    )


def solution(mesh):
    placed = (
        P(None, ("fsdp", "dp"), None),
        P(None, ("fsdp", "dp"), None),
        P("section", "fsdp"),
        P("section", "fsdp", None, None),
        P("section", "fsdp", None, None),
        P("section", None, "fsdp"),
        P("section", None, "fsdp"),
        P("section", None, "fsdp"),
        P("section", None, "fsdp"),
        P("section", None),
        P("section", None),
    )
    return jax.shard_map(
        shards,
        mesh=mesh,
        in_specs=placed,
        out_specs=(
            P("section", "fsdp"),
            P("section", "fsdp", None, None),
            P("section", "fsdp", None, None),
            P("section", None, "fsdp"),
            P("section", None, "fsdp"),
            P("section", None, "fsdp"),
            P("section", None, "fsdp"),
        ),
        check_vma=False,
    )
```

```python
import functools

import jax
import jax.numpy as jnp
from jax import lax
from jax.experimental import pallas as pl
from jax.experimental.pallas import tpu as pltpu
from jax.sharding import PartitionSpec as P

EPSILON = 1e-05
NORMAL_PEAK = 0.3989422804014327
TAIL_SCALE = 0.3
TAIL = (
    0.11962930931947272,
    0.12075380294875883,
    0.09991439682547013,
    0.12855881360857063,
    -0.05367866289105895,
    0.20634847173237508,
    -0.15720038925639956,
    0.03567418525278745,
)
BLK = 128
RANK = 16
BF = jnp.bfloat16
F32 = jnp.float32
NN = (((1,), (0,)), ((), ()))
NT = (((1,), (1,)), ((), ()))
TN = (((0,), (0,)), ((), ()))
ANY = pl.BlockSpec(memory_space=pl.ANY)
SMEM = pl.BlockSpec(memory_space=pltpu.SMEM)


def dot(a, b, dims=NN):
    return lax.dot_general(a, b, dims, preferred_element_type=F32)


def gelu_both(value):
    bell = jnp.exp(-0.5 * value * value)
    denom = 1.0 + TAIL_SCALE * jnp.abs(value)
    guess = pl.reciprocal(denom, approx=True)
    t = guess * (2.0 - denom * guess)
    poly = jnp.full_like(t, TAIL[-1])
    for coef in TAIL[-2::-1]:
        poly = poly * t + coef
    tail = bell * (t * poly)
    cdf = jnp.where(value < 0.0, tail, 1.0 - tail)
    return value * cdf, cdf + value * (bell * NORMAL_PEAK)


class Dims:
    def __init__(self, width, hidden_blocks, parts):
        self.parts = parts
        self.width = width
        self.model = width // BLK
        self.hidden = hidden_blocks
        self.group = hidden_blocks // self.model
        self.mh = self.model // parts
        self.hh = hidden_blocks // parts
        self.ul = 0
        self.dr = self.mh * BLK
        self.ur = 2 * self.mh * BLK
        self.dl = self.ur + self.hh * BLK
        self.gain = self.dl + self.hh * BLK
        self.packed = self.gain + self.mh * BLK


def lanes(start, count=BLK):
    return pl.ds(pl.multiple_of(start, BLK), count)


def load_weights(f, srcs, dsts, sems, first=0):
    copies = []
    for n, (src, dst) in enumerate(zip(srcs, dsts), first):
        if len(src) == 1:
            whole = pltpu.make_async_copy(src[0], dst, sems.at[2 * n])
            whole.start()
            copies.append((whole,))
            continue
        own, other = src
        half = dst.shape[0] // 2
        if own.ndim < dst.ndim:
            mine, theirs = f, 1 - f
        else:
            mine, theirs = pl.ds(f * half, half), pl.ds((1 - f) * half, half)
        a = pltpu.make_async_copy(own, dst.at[mine], sems.at[2 * n])
        b = pltpu.make_async_copy(other, dst.at[theirs], sems.at[2 * n + 1])
        a.start()
        b.start()
        copies.append((a, b))
    return copies


def done(pair):
    for copy in pair:
        copy.wait()


def inverse_rms(x_s, dims):
    rows = x_s.shape[0]
    total = jnp.zeros((rows, BLK), F32)
    for i in range(dims.model):
        part = x_s[:, i * BLK : (i + 1) * BLK].astype(F32)
        total = total + part * part
    return lax.rsqrt(jnp.sum(total, axis=1, keepdims=True) * (1.0 / dims.width) + EPSILON)


def fwd_norm(dims, x_s, small_s, nrm_s, low_s):
    rows = x_s.shape[0]
    r = inverse_rms(x_s, dims)
    upl = jnp.zeros((rows, RANK), F32)
    for h in range(dims.parts):
        for i in range(dims.mh):
            at = (h * dims.mh + i) * BLK
            gain = small_s[h, 0:1, dims.gain + i * BLK : dims.gain + (i + 1) * BLK].astype(F32)
            nrm_s[:, at : at + BLK] = (x_s[:, at : at + BLK].astype(F32) * r * gain).astype(BF)
        upl = upl + dot(
            nrm_s[:, h * dims.mh * BLK : (h + 1) * dims.mh * BLK],
            small_s[h, :, dims.ul : dims.ul + dims.mh * BLK],
            NT,
        )
    low_s[:, 0:RANK] = upl.astype(BF)


def fwd_hidden(dims, small_s, up_s, upo, nrm_s, hid_s, slp_s, low_s, G=32):
    rows = nrm_s.shape[0]
    G = min(G, dims.hh)
    upl = low_s[:, 0:RANK]

    def step(it, low):
        j0 = it * G
        h = j0 // dims.hh
        off = (j0 - h * dims.hh) * BLK
        ur = small_s[h, :, lanes(dims.ur + off, G * BLK)]
        dl = small_s[h, :, lanes(dims.dl + off, G * BLK)]
        hids = []
        for g in range(G):
            src = nrm_s[:, lanes(upo[j0 + g] * BLK)]
            lhs = jnp.concatenate([src, upl], axis=1)
            rhs = jnp.concatenate([up_s[j0 + g], ur[:, g * BLK : (g + 1) * BLK]], axis=0)
            hid, slope = gelu_both(dot(lhs, rhs))
            hid = hid.astype(BF)
            hid_s[j0 + g] = hid
            slp_s[j0 + g] = slope.astype(BF)
            hids.append(hid)
        return low + dot(jnp.concatenate(hids, axis=1), dl, NT)

    low = lax.fori_loop(0, dims.hidden // G, step, jnp.zeros((rows, RANK), F32)).astype(BF)
    low_s[:, BLK : BLK + RANK] = low
    return low


def fwd_down(dims, low, x_s, small_s, dn_s, dno, hid_s, y_s):
    def down(it, _):
        for u in range(8):
            i = it * 8 + u
            h = i // dims.mh
            at = i * BLK
            dr = small_s[h, :, lanes(dims.dr + (i - h * dims.mh) * BLK)]
            parts = [hid_s[dno[i * dims.group + c]] for c in range(dims.group)]
            lhs = jnp.concatenate(parts + [low], axis=1)
            blocks = dn_s[pl.ds(i * dims.group, dims.group)].reshape(dims.group * BLK, BLK)
            mixed = dot(lhs, jnp.concatenate([blocks, dr], axis=0))
            y_s[:, lanes(at)] = (x_s[:, lanes(at)].astype(F32) + mixed).astype(BF)
        return 0

    lax.fori_loop(0, dims.model // 8, down, 0)


def bwd_hidden(dims, g_s, slp_s, gp_s, small_s, dn_s, dno, low_s, U=8):
    rows = g_s.shape[0]
    gdl = jnp.zeros((rows, RANK), F32)
    for h in range(dims.parts):
        gdl = gdl + dot(
            g_s[:, h * dims.mh * BLK : (h + 1) * dims.mh * BLK],
            small_s[h, :, dims.dr : dims.dr + dims.mh * BLK],
            NT,
        )
    gdl = gdl.astype(BF)
    low_s[:, BLK : BLK + RANK] = gdl

    def hid_step(it, gul):
        for u in range(U):
            i = it * U + u
            gi = g_s[:, lanes(i * BLK)]
            js = [dno[i * dims.group + c] for c in range(dims.group)]
            hs = [j // dims.hh for j in js]
            offs = [(j - h * dims.hh) * BLK for j, h in zip(js, hs)]
            dl = jnp.concatenate([small_s[h, :, lanes(dims.dl + o)] for h, o in zip(hs, offs)], axis=1)
            ur = jnp.concatenate([small_s[h, :, lanes(dims.ur + o)] for h, o in zip(hs, offs)], axis=1)
            blocks = dn_s[pl.ds(i * dims.group, dims.group)].reshape(dims.group * BLK, BLK)
            gh = dot(gi, blocks, NT) + dot(gdl, dl)
            slope = jnp.concatenate([slp_s[j] for j in js], axis=1).astype(F32)
            gp = (gh * slope).astype(BF)
            for c, j in enumerate(js):
                gp_s[j] = gp[:, c * BLK : (c + 1) * BLK]
            gul = gul + dot(gp, ur, NT)
        return gul

    gul = lax.fori_loop(0, dims.model // U, hid_step, jnp.zeros((rows, RANK), F32))
    gul = gul.astype(BF)
    low_s[:, 0:RANK] = gul
    return gul


def bwd_input(dims, x_s, g_s, gp_s, small_s, up_s, grouped, gul, gn_s, gain_s, out_s):
    rows = g_s.shape[0]
    r = inverse_rms(x_s, dims)

    def step(it, acc):
        for u in range(8):
            i = it * 8 + u
            h = i // dims.mh
            off = (i - h * dims.mh) * BLK
            js = [grouped[i * dims.group + c] for c in range(dims.group)]
            lhs = jnp.concatenate([gp_s[j] for j in js], axis=1)
            rhs = jnp.concatenate([up_s[j] for j in js], axis=1)
            gn = dot(lhs, rhs, NT) + dot(gul, small_s[h, :, lanes(dims.ul + off)])
            x = x_s[:, lanes(i * BLK)].astype(F32)
            gain = small_s[h, 0:1, lanes(dims.gain + off)].astype(F32)
            scaled = gn * gain
            gn_s[:, lanes(i * BLK)] = scaled
            gain_s[0:1, lanes(i * BLK)] = jnp.sum(gn * x * r, axis=0, keepdims=True)
            acc = acc + x * scaled
        return acc

    acc = lax.fori_loop(0, dims.model // 8, step, jnp.zeros((rows, BLK), F32))
    shift = jnp.sum(acc, axis=1, keepdims=True) * (1.0 / dims.width) * (r * r * r)
    for i in range(dims.model):
        at = slice(i * BLK, (i + 1) * BLK)
        out_s[:, at] = (
            g_s[:, at].astype(F32) + r * gn_s[:, at] - x_s[:, at].astype(F32) * shift
        ).astype(BF)


def params(mib):
    return pltpu.CompilerParams(vmem_limit_bytes=mib * 1024 * 1024)


def fwd_slot(dims, sc, upo, dno, first, recv, weights, bufs, micro, held):
    rows = recv.shape[0]
    n_buf = 5
    shapes = (
        jax.ShapeDtypeStruct((micro, dims.hidden, held, BLK), BF),
        jax.ShapeDtypeStruct((micro, dims.hidden, held, BLK), BF),
        jax.ShapeDtypeStruct((micro, held, dims.width), BF),
        jax.ShapeDtypeStruct((micro, rows, dims.width), BF),
        jax.ShapeDtypeStruct((micro, held, 2 * BLK), BF),
    )
    n_w = len(weights[0])
    n_in = 5 + 3 * n_w + (n_buf if bufs is not None else 0)

    def kernel(*refs):
        sc, upo, dno, first, recv = refs[:5]
        up_w, dn_w, small_w = (refs[5 + k * n_w : 5 + (k + 1) * n_w] for k in range(3))
        y, hidb, slpb, nrmb, xb, lowb = refs[n_in : n_in + 6]
        up_s, dn_s, small_s, x_s, nrm_s, hid_s, slp_s, low_s, y_s, sems = refs[n_in + 6 :]

        @pl.when(sc[0] == 1)
        def _():
            m, f = sc[1], sc[2]

            @pl.when(sc[3] == 1)
            def _():
                pltpu.make_async_copy(first.at[m], x_s, sems.at[6]).start()

            @pl.when(sc[3] == 0)
            def _():
                pltpu.make_async_copy(recv, x_s, sems.at[6]).start()

            wait_x = pltpu.make_async_copy(recv, x_s, sems.at[6])
            small, up = load_weights(f, (small_w, up_w), (small_s, up_s), sems)
            low_s[...] = jnp.zeros_like(low_s)
            wait_x.wait()
            save_x = pltpu.make_async_copy(x_s, xb.at[m], sems.at[7])
            save_x.start()
            done(small)
            fwd_norm(dims, x_s, small_s, nrm_s, low_s)
            done(up)
            (dn,) = load_weights(f, (dn_w,), (dn_s,), sems, 2)
            low = fwd_hidden(dims, small_s, up_s, upo, nrm_s, hid_s, slp_s, low_s)
            outs = [
                pltpu.make_async_copy(hid_s, hidb.at[m, :, 0:rows], sems.at[9]),
                pltpu.make_async_copy(slp_s, slpb.at[m, :, 0:rows], sems.at[10]),
                pltpu.make_async_copy(nrm_s, nrmb.at[m, 0:rows], sems.at[11]),
                pltpu.make_async_copy(low_s, lowb.at[m, 0:rows], sems.at[12]),
            ]
            for copy in outs:
                copy.start()
            done(dn)
            fwd_down(dims, low, x_s, small_s, dn_s, dno, hid_s, y_s)
            outs.append(pltpu.make_async_copy(y_s, y, sems.at[8]))
            outs[-1].start()
            save_x.wait()
            done(outs)

    args = [sc, upo, dno, first, recv] + [w for pair in weights for w in pair]
    aliases = {}
    if bufs is not None:
        aliases = {len(args) + n: n + 1 for n in range(n_buf)}
        args += list(bufs)
    out = pl.pallas_call(
        kernel,
        out_shape=(jax.ShapeDtypeStruct((rows, dims.width), BF),) + shapes,
        in_specs=[SMEM] * 3 + [ANY] * (len(args) - 3),
        out_specs=(ANY,) * 6,
        input_output_aliases=aliases,
        scratch_shapes=[
            pltpu.VMEM((dims.hidden, BLK, BLK), BF),
            pltpu.VMEM((dims.hidden, BLK, BLK), BF),
            pltpu.VMEM((dims.parts, RANK, dims.packed), BF),
            pltpu.VMEM((rows, dims.width), BF),
            pltpu.VMEM((rows, dims.width), BF),
            pltpu.VMEM((dims.hidden, rows, BLK), BF),
            pltpu.VMEM((dims.hidden, rows, BLK), BF),
            pltpu.VMEM((rows, 2 * BLK), BF),
            pltpu.VMEM((rows, dims.width), BF),
            pltpu.SemaphoreType.DMA((13,)),
        ],
        compiler_params=params(60),
        name="forward_rows",
    )(*args)
    return out[0], out[1:]


def bwd_slot(dims, sc, dno, grouped, last, recv, weights, xb, slpb, bufs, micro, held):
    rows = recv.shape[0]
    n_buf = 4
    shapes = (
        jax.ShapeDtypeStruct((micro, dims.hidden, held, BLK), BF),
        jax.ShapeDtypeStruct((micro, held, dims.width), BF),
        jax.ShapeDtypeStruct((micro, held, 2 * BLK), BF),
        jax.ShapeDtypeStruct((micro, 8, dims.width), F32),
    )
    n_w = len(weights[0])
    n_in = 7 + 3 * n_w + (n_buf if bufs is not None else 0)

    def kernel(*refs):
        sc, dno, grouped, last, recv = refs[:5]
        up_w, dn_w, small_w = (refs[5 + k * n_w : 5 + (k + 1) * n_w] for k in range(3))
        xb, slpb = refs[5 + 3 * n_w : 7 + 3 * n_w]
        out, gpb, gb, lowb, gainb = refs[n_in : n_in + 5]
        up_s, dn_s, small_s, x_s, g_s, slp_s, gp_s, low_s, gn_s, gain_s, out_s, sems = refs[n_in + 5 :]

        @pl.when(sc[0] == 1)
        def _():
            m, f = sc[1], sc[2]

            @pl.when(sc[3] == 1)
            def _():
                pltpu.make_async_copy(last.at[m], g_s, sems.at[6]).start()

            @pl.when(sc[3] == 0)
            def _():
                pltpu.make_async_copy(recv, g_s, sems.at[6]).start()

            wait_g = pltpu.make_async_copy(recv, g_s, sems.at[6])
            get_slope = pltpu.make_async_copy(slpb.at[m, :, 0:rows], slp_s, sems.at[7])
            get_x = pltpu.make_async_copy(xb.at[m], x_s, sems.at[8])
            small, dn = load_weights(f, (small_w, dn_w), (small_s, dn_s), sems)
            get_slope.start()
            low_s[...] = jnp.zeros_like(low_s)
            gain_s[...] = jnp.zeros_like(gain_s)
            wait_g.wait()
            save_g = pltpu.make_async_copy(g_s, gb.at[m, 0:rows], sems.at[9])
            save_g.start()
            done(small)
            get_slope.wait()
            done(dn)
            (up,) = load_weights(f, (up_w,), (up_s,), sems, 2)
            get_x.start()
            gul = bwd_hidden(dims, g_s, slp_s, gp_s, small_s, dn_s, dno, low_s)
            outs = [
                pltpu.make_async_copy(gp_s, gpb.at[m, :, 0:rows], sems.at[10]),
                pltpu.make_async_copy(low_s, lowb.at[m, 0:rows], sems.at[11]),
            ]
            for copy in outs:
                copy.start()
            get_x.wait()
            done(up)
            bwd_input(dims, x_s, g_s, gp_s, small_s, up_s, grouped, gul, gn_s, gain_s, out_s)
            more = [
                pltpu.make_async_copy(gain_s, gainb.at[m], sems.at[12]),
                pltpu.make_async_copy(out_s, out, sems.at[13]),
            ]
            for copy in more:
                copy.start()
            save_g.wait()
            done(outs)
            done(more)

    args = [sc, dno, grouped, last, recv] + [w for pair in weights for w in pair] + [xb, slpb]
    aliases = {}
    if bufs is not None:
        aliases = {len(args) + n: n + 1 for n in range(n_buf)}
        args += list(bufs)
    out = pl.pallas_call(
        kernel,
        out_shape=(jax.ShapeDtypeStruct((rows, dims.width), BF),) + shapes,
        in_specs=[SMEM] * 3 + [ANY] * (len(args) - 3),
        out_specs=(ANY,) * 5,
        input_output_aliases=aliases,
        scratch_shapes=[
            pltpu.VMEM((dims.hidden, BLK, BLK), BF),
            pltpu.VMEM((dims.hidden, BLK, BLK), BF),
            pltpu.VMEM((dims.parts, RANK, dims.packed), BF),
            pltpu.VMEM((rows, dims.width), BF),
            pltpu.VMEM((rows, dims.width), BF),
            pltpu.VMEM((dims.hidden, rows, BLK), BF),
            pltpu.VMEM((dims.hidden, rows, BLK), BF),
            pltpu.VMEM((rows, 2 * BLK), BF),
            pltpu.VMEM((rows, dims.width), F32),
            pltpu.VMEM((8, dims.width), F32),
            pltpu.VMEM((rows, dims.width), BF),
            pltpu.SemaphoreType.DMA((14,)),
        ],
        compiler_params=params(60),
        name="backward_rows",
    )(*args)
    return out[0], out[1:]


def pick_rows(sc, sources, dst, sem, count):
    n = dst.shape[0] // (len(sources[0]) * count)
    places = [(q, t, (q * len(sources[0]) + t) * n) for q in range(count) for t in range(len(sources[0]))]
    for number, triple in enumerate(sources):

        @pl.when(sc[3] == number)
        def _():
            for q, t, at in places:
                pltpu.make_async_copy(triple[t].at[sc[4] + q], dst.at[at : at + n], sem.at[q, t]).start()

    return tuple(
        pltpu.make_async_copy(sources[0][t].at[0], dst.at[at : at + n], sem.at[q, t]) for q, t, at in places
    )


def fwd_far(dims, sc, upo, sources, weights, bufs, count):
    hidb, slpb, nrmb, lowb = bufs
    rows = sources[0][0].shape[1]
    far = rows * len(sources[0])
    n_w, n_t, n_q = len(weights[0]), len(sources[0]), len(sources)
    args = [sc, upo] + list(weights[0]) + list(weights[2]) + [a for triple in sources for a in triple]
    n_plain = len(args)
    args += list(bufs)

    def kernel(*refs):
        sc, upo = refs[:2]
        up_w, small_w = refs[2 : 2 + n_w], refs[2 + n_w : 2 + 2 * n_w]
        base = 2 + 2 * n_w
        srcs = [refs[base + q * n_t : base + (q + 1) * n_t] for q in range(n_q)]
        hidb, slpb, nrmb, lowb = refs[n_plain + 4 : n_plain + 8]
        up_s, small_s, x_s, nrm_s, hid_s, slp_s, low_s, sems, xsem, osems = refs[n_plain + 9 :]

        @pl.when(sc[0] == 1)
        def _():
            m, f = sc[1], sc[2]
            wait_x = pick_rows(sc, srcs, x_s, xsem, count)
            small, up = load_weights(f, (small_w, up_w), (small_s, up_s), sems)
            low_s[...] = jnp.zeros_like(low_s)
            done(wait_x)
            done(small)
            fwd_norm(dims, x_s, small_s, nrm_s, low_s)
            done(up)
            fwd_hidden(dims, small_s, up_s, upo, nrm_s, hid_s, slp_s, low_s, 4)
            at = slice(rows, rows + far)
            outs = []
            for q in range(count):
                mine = slice(q * far, (q + 1) * far)
                outs += [
                    pltpu.make_async_copy(hid_s.at[:, mine], hidb.at[m + q, :, at], osems.at[q, 0]),
                    pltpu.make_async_copy(slp_s.at[:, mine], slpb.at[m + q, :, at], osems.at[q, 1]),
                    pltpu.make_async_copy(nrm_s.at[mine], nrmb.at[m + q, at], osems.at[q, 2]),
                    pltpu.make_async_copy(low_s.at[mine], lowb.at[m + q, at], osems.at[q, 3]),
                ]
            for copy in outs:
                copy.start()
            done(outs)

    return pl.pallas_call(
        kernel,
        out_shape=tuple(jax.ShapeDtypeStruct(b.shape, b.dtype) for b in bufs)
        + (jax.ShapeDtypeStruct((8, BLK), F32),),
        in_specs=[SMEM] * 2 + [ANY] * (len(args) - 2),
        out_specs=(ANY,) * 5,
        input_output_aliases={n_plain + n: n for n in range(4)},
        scratch_shapes=[
            pltpu.VMEM((dims.hidden, BLK, BLK), BF),
            pltpu.VMEM((dims.parts, RANK, dims.packed), BF),
            pltpu.VMEM((count * far, dims.width), BF),
            pltpu.VMEM((count * far, dims.width), BF),
            pltpu.VMEM((dims.hidden, count * far, BLK), BF),
            pltpu.VMEM((dims.hidden, count * far, BLK), BF),
            pltpu.VMEM((count * far, 2 * BLK), BF),
            pltpu.SemaphoreType.DMA((8,)),
            pltpu.SemaphoreType.DMA((count, n_t)),
            pltpu.SemaphoreType.DMA((count, 4)),
        ],
        compiler_params=params(60),
        name="forward_far_rows",
    )(*args)


def bwd_far(dims, sc, dno, sources, weights, slpb, bufs, count):
    rows = sources[0][0].shape[1]
    far = rows * len(sources[0])
    n_w, n_t, n_q = len(weights[0]), len(sources[0]), len(sources)
    args = [sc, dno] + list(weights[1]) + list(weights[2]) + [a for triple in sources for a in triple] + [slpb]
    n_plain = len(args)
    args += list(bufs)

    def kernel(*refs):
        sc, dno = refs[:2]
        dn_w, small_w = refs[2 : 2 + n_w], refs[2 + n_w : 2 + 2 * n_w]
        base = 2 + 2 * n_w
        srcs = [refs[base + q * n_t : base + (q + 1) * n_t] for q in range(n_q)]
        slpb = refs[n_plain - 1]
        gpb, gb, lowb = refs[n_plain + 3 : n_plain + 6]
        dn_s, small_s, g_s, slp_s, gp_s, low_s, sems, gsem, osems = refs[n_plain + 7 :]

        @pl.when(sc[0] == 1)
        def _():
            m, f = sc[1], sc[2]
            at = slice(rows, rows + far)
            wait_g = pick_rows(sc, srcs, g_s, gsem, count)
            small, dn = load_weights(f, (small_w, dn_w), (small_s, dn_s), sems)
            mine = [slice(q * far, (q + 1) * far) for q in range(count)]
            get_slope = [
                pltpu.make_async_copy(slpb.at[m + q, :, at], slp_s.at[:, mine[q]], osems.at[q, 0])
                for q in range(count)
            ]
            for copy in get_slope:
                copy.start()
            low_s[...] = jnp.zeros_like(low_s)
            done(wait_g)
            save_g = [
                pltpu.make_async_copy(g_s.at[mine[q]], gb.at[m + q, at], osems.at[q, 1]) for q in range(count)
            ]
            for copy in save_g:
                copy.start()
            done(small)
            done(dn)
            done(get_slope)
            bwd_hidden(dims, g_s, slp_s, gp_s, small_s, dn_s, dno, low_s, 2)
            outs = []
            for q in range(count):
                outs += [
                    pltpu.make_async_copy(gp_s.at[:, mine[q]], gpb.at[m + q, :, at], osems.at[q, 2]),
                    pltpu.make_async_copy(low_s.at[mine[q]], lowb.at[m + q, at], osems.at[q, 3]),
                ]
            for copy in outs:
                copy.start()
            done(save_g)
            done(outs)

    return pl.pallas_call(
        kernel,
        out_shape=tuple(jax.ShapeDtypeStruct(b.shape, b.dtype) for b in bufs)
        + (jax.ShapeDtypeStruct((8, BLK), F32),),
        in_specs=[SMEM] * 2 + [ANY] * (len(args) - 2),
        out_specs=(ANY,) * 4,
        input_output_aliases={n_plain + n: n for n in range(3)},
        scratch_shapes=[
            pltpu.VMEM((dims.hidden, BLK, BLK), BF),
            pltpu.VMEM((dims.parts, RANK, dims.packed), BF),
            pltpu.VMEM((count * far, dims.width), BF),
            pltpu.VMEM((dims.hidden, count * far, BLK), BF),
            pltpu.VMEM((dims.hidden, count * far, BLK), BF),
            pltpu.VMEM((count * far, 2 * BLK), BF),
            pltpu.SemaphoreType.DMA((8,)),
            pltpu.SemaphoreType.DMA((count, n_t)),
            pltpu.SemaphoreType.DMA((count, 4)),
        ],
        compiler_params=params(60),
        name="backward_far_rows",
    )(*args)


def weight_grads(dims, up, sc, order, blocks, wide, low_a, low_b, gain=None):
    micro, _, held, _ = blocks.shape
    total = micro * held
    group, model, mh, hh = dims.group, dims.model, dims.mh, dims.hh
    U = 4
    two = dims.parts == 2
    hid_at = mh * BLK
    gain_at = hid_at + hh * BLK
    packed = gain_at + (mh * BLK if up else 0)
    VM = pl.BlockSpec(memory_space=pltpu.VMEM)
    a_at, b_at = (0, 0) if up else (BLK, BLK)
    extra = [gain] if up else []

    def kernel(*refs):
        sc, order, blocks, wide, low_a, low_b = refs[:6]
        gain = refs[6] if up else None
        outs_hbm = refs[6 + len(extra) : -6]
        big, small, held_s, wide_s, sems, osems = refs[-6:]
        f = sc[2]
        get_wide = pltpu.make_async_copy(wide, wide_s, osems.at[0])
        get_wide.start()

        def fetch(it, slot, go):
            for u in range(U):
                for c in range(group):
                    j = order[(it * U + u) * group + c]
                    copy = pltpu.make_async_copy(
                        blocks.at[:, j], held_s.at[slot, u * group + c], sems.at[slot, u * group + c]
                    )
                    copy.start() if go else copy.wait()

        fetch(0, 0, True)

        def low_t(ref, at):
            rows = jnp.concatenate([ref[m, :, at : at + BLK] for m in range(micro)], axis=0)
            return rows.astype(F32).T[0:RANK].astype(BF)

        with_blocks, with_wide = low_t(low_a, a_at), low_t(low_b, b_at)
        get_wide.wait()

        def which(h):
            return jnp.where(h == f, 0, 1) if two else h

        def step(it, _):
            slot = lax.rem(it, 2)

            @pl.when(it + 1 < model // U)
            def _():
                fetch(it + 1, 1 - slot, True)

            fetch(it, slot, False)
            for u in range(U):
                i = it * U + u
                h = i // mh
                w = which(h)
                off = i - h * mh
                wi = jnp.concatenate([wide_s[m, :, lanes(i * BLK)] for m in range(micro)], axis=0)
                lhs = jnp.concatenate([wi.T, with_blocks], axis=0)
                rhs = jnp.concatenate(
                    [held_s[slot, u * group + c].reshape(total, BLK) for c in range(group)], axis=1
                )
                res = dot(lhs, rhs)
                for c in range(group):
                    j = order[i * group + c]
                    hj = j // hh
                    wj = which(hj)
                    part = res[:, c * BLK : (c + 1) * BLK]
                    if up:
                        big[wj, j - hj * hh] = part[0:BLK].astype(BF)
                    else:
                        big[w, off * group + c] = part[0:BLK].T.astype(BF)
                    small[wj, :, lanes(hid_at + (j - hj * hh) * BLK)] = part[BLK:].astype(BF)
                small[w, :, lanes(off * BLK)] = dot(with_wide, wi).astype(BF)
                if up:
                    small[w, :, lanes(gain_at + off * BLK)] = jnp.broadcast_to(
                        gain[0:1, lanes(i * BLK)], (RANK, BLK)
                    ).astype(BF)
            return 0

        lax.fori_loop(0, model // U, step, 0)
        outs = []
        for n, src in enumerate((big, small)):
            if two:
                outs.append(pltpu.make_async_copy(src.at[0], outs_hbm[2 * n], osems.at[2 * n]))
                outs.append(pltpu.make_async_copy(src.at[1], outs_hbm[2 * n + 1], osems.at[2 * n + 1]))
            else:
                outs.append(pltpu.make_async_copy(src, outs_hbm[n], osems.at[2 * n]))
        for copy in outs:
            copy.start()
        done(outs)

    lead = () if two else (dims.parts,)
    shapes = [lead + (hh, BLK, BLK), lead + (RANK, packed)]
    shapes = [jax.ShapeDtypeStruct(shape, BF) for shape in shapes for _ in range(2 if two else 1)]
    got = pl.pallas_call(
        kernel,
        out_shape=tuple(shapes),
        in_specs=[SMEM] * 2 + [ANY] * 2 + [VM] * (2 + len(extra)),
        out_specs=(ANY,) * len(shapes),
        scratch_shapes=[
            pltpu.VMEM((dims.parts, hh, BLK, BLK), BF),
            pltpu.VMEM((dims.parts, RANK, packed), BF),
            pltpu.VMEM((2, U * group, micro, held, BLK), BF),
            pltpu.VMEM((micro, held, dims.width), BF),
            pltpu.SemaphoreType.DMA((2, U * group)),
            pltpu.SemaphoreType.DMA((4,)),
        ],
        compiler_params=params(60),
        name="up_gradients" if up else "down_gradients",
    )(sc, order, blocks, wide, low_a, low_b, *extra)
    return [got[0:2], got[2:4]] if two else [got[0:1], got[1:2]]


def orders(up_order, dims):
    at = jnp.arange(dims.hidden, dtype=jnp.int32)
    same = (up_order[:, None] == up_order[None, :]) & (at[None, :] < at[:, None])
    place = up_order * dims.group + jnp.sum(same.astype(jnp.int32), axis=1)
    hit = place[None, :] == at[:, None]
    return jnp.sum(jnp.where(hit, at[None, :], 0), axis=1)


def shards(inputs, cotangent, norm_gain, up_blocks, down_blocks, up_left, up_right, down_left, down_right,
           up_pattern, down_pattern):
    micro, rows, width = inputs.shape
    upo, dno = up_pattern[0], down_pattern[0]
    parts = lax.axis_size("fsdp")
    dims = Dims(width, upo.shape[0], parts)
    n_sec = lax.axis_size("section")
    sec = lax.axis_index("section")
    f = lax.axis_index("fsdp")
    swap = [(0, 1), (1, 0)]
    n_dp = lax.axis_size("dp")
    held = rows * n_dp
    small = jnp.concatenate(
        [up_left[0], down_right[0], up_right[0], down_left[0],
         jnp.broadcast_to(norm_gain, (RANK, norm_gain.shape[1]))], axis=1)

    def whole_layer(own, stacked):
        if parts == 2:
            return (own, lax.ppermute(own, "fsdp", swap))
        return (lax.all_gather(own, "fsdp", axis=0, tiled=not stacked),)

    small_w = whole_layer(small, True)
    up_w = whole_layer(up_blocks[0], False)
    weights = (up_w, whole_layer(down_blocks[0], False), small_w)
    grouped = orders(upo, dims)
    zero = jnp.int32(0)

    def scalars(m, edge):
        live = (m >= 0) & (m < micro)
        return jnp.stack([live.astype(jnp.int32), jnp.clip(m, 0, micro - 1).astype(jnp.int32),
                          f.astype(jnp.int32), edge.astype(jnp.int32), zero, zero, zero, zero])

    def shifted(block, sections, k):
        pairs = [(s * n_dp + d, s * n_dp + (d + k) % n_dp) for s in sections for d in range(n_dp)]
        return lax.ppermute(block, ("section", "dp"), pairs)

    def to_dp(block, sections):
        return tuple(shifted(block, sections, k) for k in range(1, n_dp))

    def flags(live, m, source, index):
        return jnp.stack([jnp.asarray(v).astype(jnp.int32) for v in (live, m, f, source, index, 0, 0, 0)])

    state = {"token": None, "due": []}

    def chained(*arrays):
        due = tuple(v for n, v in state["due"] if n <= 0)
        state["due"] = [(n - 1, v) for n, v in state["due"] if n > 0]
        if state["token"] is not None:
            due = due + (state["token"],)
        if not due:
            return arrays
        out = lax.optimization_barrier(arrays + due)
        return out[: len(arrays)]

    shifts = [1] + list(range(n_dp - 1, 1, -1))
    queue = []

    def send_one(hold):
        if queue:
            store, k, payload, sections = queue.pop(0)
            block, _ = lax.optimization_barrier((payload(), state["token"]))
            store[k] = shifted(block, sections, k)
            state["due"].append((hold, store[k]))

    def enqueue(payload, sections):
        store = {}
        queue.extend((store, k, payload, sections) for k in shifts)
        return store

    fbufs, bbufs = None, None
    frecv = inputs[0]
    brecv = inputs[0]
    last = n_sec - 1
    edge = jnp.where(sec == 0, inputs, cotangent)
    far_edge = enqueue(lambda: edge, (0, last))

    def forward(t):
        nonlocal fbufs, frecv
        (x,) = chained(frecv)
        y, fbufs = fwd_slot(dims, scalars(t - sec, sec == 0), upo, dno, inputs, x, weights, fbufs, micro, held)
        state["token"] = y
        pairs = [(s, s + 1) for s in range(last) if 0 <= t - s < micro]
        if pairs:
            frecv = lax.ppermute(y, "section", pairs)

    def backward(t):
        nonlocal bbufs, brecv
        (g,) = chained(brecv)
        out, bbufs = bwd_slot(dims, scalars(t - (last - sec), sec == last), dno, grouped, cotangent, g,
                              weights, fbufs[3], fbufs[1], bbufs, micro, held)
        state["token"] = out
        pairs = [(last - s, last - s - 1) for s in range(last) if 0 <= t - s < micro]
        if pairs:
            brecv = lax.ppermute(out, "section", pairs)

    def forward_far(m, live, sources, source, index):
        nonlocal fbufs
        (sc,) = chained(flags(live, m, source, index))
        hidb, slpb, nrmb, xb, lowf = fbufs
        hidb, slpb, nrmb, lowf, state["token"] = fwd_far(dims, sc, upo, sources, weights, (hidb, slpb, nrmb, lowf), half)
        fbufs = (hidb, slpb, nrmb, xb, lowf)

    slots = micro + last
    half = micro // 2
    early, late = slice(0, half), slice(half, micro)
    inner, outer = list(range(1, n_sec)), list(range(last))

    def triple(store):
        return tuple(store[k] for k in range(1, n_dp))

    for t in range(slots):
        if t == slots - 1:
            forward_far(0, sec == 0, [triple(far_edge)], 0, 0)
        forward(t)
        if t < last:
            send_one(3)
        if t == slots - 1:
            x_late = enqueue(lambda: fbufs[3][late], inner)
        if t > last + 1:
            send_one(1)
        if t >= last:
            backward(t - last)
        if t == last + 1:
            x_early = enqueue(lambda: fbufs[3][early], inner)
        if t > last:
            send_one(1)
        if t == slots - 1:
            send_one(1)

    for t in range(slots - last, slots):
        backward(t)
        if t == slots - 3:
            g_early = enqueue(lambda: bbufs[1][early, 0:rows], outer)
        if t == slots - 1:
            g_late = enqueue(lambda: bbufs[1][late, 0:rows], outer)
        hold = 2 if t >= slots - 2 else 1
        send_one(hold)
        if t != slots - 2:
            send_one(hold)
        else:
            forward_far(0, sec > 0, [triple(x_early)], 0, 0)
    gpb, gb, lowb, gain_rows = bbufs

    def far_backward(m):
        nonlocal gpb, gb, lowb
        sources = [triple(g_early if m < half else g_late), triple(far_edge)]
        (sc,) = chained(flags(True, m, jnp.where(sec == last, 1, 0), jnp.where(sec == last, m, m % half)))
        gpb, gb, lowb, state["token"] = bwd_far(dims, sc, dno, sources, weights, fbufs[1], (gpb, gb, lowb), half)
        send_one(1)

    forward_far(half, True, [triple(x_late), triple(far_edge)], jnp.where(sec == 0, 1, 0), jnp.where(sec == 0, half, 0))
    send_one(1)
    far_backward(0)
    while queue:
        send_one(2)
    gain = jnp.sum(gain_rows, axis=(0, 1))[None]
    for other in to_dp(gain, range(n_sec)):
        gain = gain + other
    far_backward(half)
    hidb, slpb, nrmb, _, lowf = fbufs
    sc = scalars(zero, sec == 0)

    def over_fsdp(pieces, ahead=()):
        if parts == 2:
            got = lax.ppermute(pieces[1], "fsdp", swap)
            got = lax.optimization_barrier((got, *ahead))[0]
            return (pieces[0].astype(F32) + got.astype(F32))[None]
        return lax.psum_scatter(pieces[0], "fsdp", scatter_dimension=0, tiled=False).astype(F32)[None]

    dn_g, dn_small = weight_grads(dims, False, sc, dno, hidb, gb, lowb, lowf)
    up_g, up_small = weight_grads(dims, True, sc, grouped, gpb, nrmb, lowf, lowb, gain)
    dn, dns = over_fsdp(dn_g), over_fsdp(dn_small)
    up, ups = over_fsdp(up_g, (dn,)), over_fsdp(up_small)
    mw, hw = dims.mh * BLK, dims.hh * BLK
    return (
        ups[:, 0, mw + hw :],
        up,
        dn,
        ups[:, :, 0:mw],
        ups[:, :, mw : mw + hw],
        dns[:, :, mw : mw + hw],
        dns[:, :, 0:mw],
    )


def solution(mesh):
    placed = (
        P(None, ("fsdp", "dp"), None),
        P(None, ("fsdp", "dp"), None),
        P("section", "fsdp"),
        P("section", "fsdp", None, None),
        P("section", "fsdp", None, None),
        P("section", None, "fsdp"),
        P("section", None, "fsdp"),
        P("section", None, "fsdp"),
        P("section", None, "fsdp"),
        P("section", None),
        P("section", None),
    )
    return jax.shard_map(
        shards,
        mesh=mesh,
        in_specs=placed,
        out_specs=(
            P("section", "fsdp"),
            P("section", "fsdp", None, None),
            P("section", "fsdp", None, None),
            P("section", None, "fsdp"),
            P("section", None, "fsdp"),
            P("section", None, "fsdp"),
            P("section", None, "fsdp"),
        ),
        check_vma=False,
    )
```

```python
import functools

import jax
import jax.numpy as jnp
from jax import lax
from jax.experimental import pallas as pl
from jax.experimental.pallas import tpu as pltpu
from jax.sharding import PartitionSpec as P

EPSILON = 1e-05
NORMAL_PEAK = 0.3989422804014327
TAIL_SCALE = 0.3
TAIL = (
    0.11962930931947272,
    0.12075380294875883,
    0.09991439682547013,
    0.12855881360857063,
    -0.05367866289105895,
    0.20634847173237508,
    -0.15720038925639956,
    0.03567418525278745,
)
BLK = 128
RANK = 16
BF = jnp.bfloat16
F32 = jnp.float32
NN = (((1,), (0,)), ((), ()))
NT = (((1,), (1,)), ((), ()))
TN = (((0,), (0,)), ((), ()))
ANY = pl.BlockSpec(memory_space=pl.ANY)
SMEM = pl.BlockSpec(memory_space=pltpu.SMEM)


def dot(a, b, dims=NN):
    return lax.dot_general(a, b, dims, preferred_element_type=F32)


def gelu_both(value):
    bell = jnp.exp(-0.5 * value * value)
    denom = 1.0 + TAIL_SCALE * jnp.abs(value)
    guess = pl.reciprocal(denom, approx=True)
    t = guess * (2.0 - denom * guess)
    poly = jnp.full_like(t, TAIL[-1])
    for coef in TAIL[-2::-1]:
        poly = poly * t + coef
    tail = bell * (t * poly)
    cdf = jnp.where(value < 0.0, tail, 1.0 - tail)
    return value * cdf, cdf + value * (bell * NORMAL_PEAK)


class Dims:
    def __init__(self, width, hidden_blocks, parts):
        self.parts = parts
        self.width = width
        self.model = width // BLK
        self.hidden = hidden_blocks
        self.group = hidden_blocks // self.model
        self.mh = self.model // parts
        self.hh = hidden_blocks // parts
        self.ul = 0
        self.dr = self.mh * BLK
        self.ur = 2 * self.mh * BLK
        self.dl = self.ur + self.hh * BLK
        self.gain = self.dl + self.hh * BLK
        self.packed = self.gain + self.mh * BLK


def lanes(start, count=BLK):
    return pl.ds(pl.multiple_of(start, BLK), count)


def load_weights(f, srcs, dsts, sems, first=0):
    copies = []
    for n, (src, dst) in enumerate(zip(srcs, dsts), first):
        if len(src) == 1:
            whole = pltpu.make_async_copy(src[0], dst, sems.at[2 * n])
            whole.start()
            copies.append((whole,))
            continue
        own, other = src
        half = dst.shape[0] // 2
        if own.ndim < dst.ndim:
            mine, theirs = f, 1 - f
        else:
            mine, theirs = pl.ds(f * half, half), pl.ds((1 - f) * half, half)
        a = pltpu.make_async_copy(own, dst.at[mine], sems.at[2 * n])
        b = pltpu.make_async_copy(other, dst.at[theirs], sems.at[2 * n + 1])
        a.start()
        b.start()
        copies.append((a, b))
    return copies


def done(pair):
    for copy in pair:
        copy.wait()


def inverse_rms(x_s, dims):
    rows = x_s.shape[0]
    total = jnp.zeros((rows, BLK), F32)
    for i in range(dims.model):
        part = x_s[:, i * BLK : (i + 1) * BLK].astype(F32)
        total = total + part * part
    return lax.rsqrt(jnp.sum(total, axis=1, keepdims=True) * (1.0 / dims.width) + EPSILON)


def fwd_norm(dims, x_s, small_s, nrm_s, low_s):
    rows = x_s.shape[0]
    r = inverse_rms(x_s, dims)
    upl = jnp.zeros((rows, RANK), F32)
    for h in range(dims.parts):
        for i in range(dims.mh):
            at = (h * dims.mh + i) * BLK
            gain = small_s[h, 0:1, dims.gain + i * BLK : dims.gain + (i + 1) * BLK].astype(F32)
            nrm_s[:, at : at + BLK] = (x_s[:, at : at + BLK].astype(F32) * r * gain).astype(BF)
        upl = upl + dot(
            nrm_s[:, h * dims.mh * BLK : (h + 1) * dims.mh * BLK],
            small_s[h, :, dims.ul : dims.ul + dims.mh * BLK],
            NT,
        )
    low_s[:, 0:RANK] = upl.astype(BF)


def fwd_hidden(dims, small_s, up_s, upo, nrm_s, hid_s, slp_s, low_s, G=32):
    rows = nrm_s.shape[0]
    G = min(G, dims.hh)
    upl = low_s[:, 0:RANK]

    def step(it, low):
        j0 = it * G
        h = j0 // dims.hh
        off = (j0 - h * dims.hh) * BLK
        ur = small_s[h, :, lanes(dims.ur + off, G * BLK)]
        dl = small_s[h, :, lanes(dims.dl + off, G * BLK)]
        hids = []
        for g in range(G):
            src = nrm_s[:, lanes(upo[j0 + g] * BLK)]
            lhs = jnp.concatenate([src, upl], axis=1)
            rhs = jnp.concatenate([up_s[j0 + g], ur[:, g * BLK : (g + 1) * BLK]], axis=0)
            hid, slope = gelu_both(dot(lhs, rhs))
            hid = hid.astype(BF)
            hid_s[j0 + g] = hid
            slp_s[j0 + g] = slope.astype(BF)
            hids.append(hid)
        return low + dot(jnp.concatenate(hids, axis=1), dl, NT)

    low = lax.fori_loop(0, dims.hidden // G, step, jnp.zeros((rows, RANK), F32)).astype(BF)
    low_s[:, BLK : BLK + RANK] = low
    return low


def fwd_down(dims, low, x_s, small_s, dn_s, dno, hid_s, y_s):
    def down(it, _):
        for u in range(8):
            i = it * 8 + u
            h = i // dims.mh
            at = i * BLK
            dr = small_s[h, :, lanes(dims.dr + (i - h * dims.mh) * BLK)]
            parts = [hid_s[dno[i * dims.group + c]] for c in range(dims.group)]
            lhs = jnp.concatenate(parts + [low], axis=1)
            blocks = dn_s[pl.ds(i * dims.group, dims.group)].reshape(dims.group * BLK, BLK)
            mixed = dot(lhs, jnp.concatenate([blocks, dr], axis=0))
            y_s[:, lanes(at)] = (x_s[:, lanes(at)].astype(F32) + mixed).astype(BF)
        return 0

    lax.fori_loop(0, dims.model // 8, down, 0)


def bwd_hidden(dims, g_s, slp_s, gp_s, small_s, dn_s, dno, low_s, U=8):
    rows = g_s.shape[0]
    gdl = jnp.zeros((rows, RANK), F32)
    for h in range(dims.parts):
        gdl = gdl + dot(
            g_s[:, h * dims.mh * BLK : (h + 1) * dims.mh * BLK],
            small_s[h, :, dims.dr : dims.dr + dims.mh * BLK],
            NT,
        )
    gdl = gdl.astype(BF)
    low_s[:, BLK : BLK + RANK] = gdl

    def hid_step(it, gul):
        for u in range(U):
            i = it * U + u
            gi = g_s[:, lanes(i * BLK)]
            js = [dno[i * dims.group + c] for c in range(dims.group)]
            hs = [j // dims.hh for j in js]
            offs = [(j - h * dims.hh) * BLK for j, h in zip(js, hs)]
            dl = jnp.concatenate([small_s[h, :, lanes(dims.dl + o)] for h, o in zip(hs, offs)], axis=1)
            ur = jnp.concatenate([small_s[h, :, lanes(dims.ur + o)] for h, o in zip(hs, offs)], axis=1)
            blocks = dn_s[pl.ds(i * dims.group, dims.group)].reshape(dims.group * BLK, BLK)
            gh = dot(gi, blocks, NT) + dot(gdl, dl)
            slope = jnp.concatenate([slp_s[j] for j in js], axis=1).astype(F32)
            gp = (gh * slope).astype(BF)
            for c, j in enumerate(js):
                gp_s[j] = gp[:, c * BLK : (c + 1) * BLK]
            gul = gul + dot(gp, ur, NT)
        return gul

    gul = lax.fori_loop(0, dims.model // U, hid_step, jnp.zeros((rows, RANK), F32))
    gul = gul.astype(BF)
    low_s[:, 0:RANK] = gul
    return gul


def bwd_input(dims, x_s, g_s, gp_s, small_s, up_s, grouped, gul, gn_s, gain_s, out_s):
    rows = g_s.shape[0]
    r = inverse_rms(x_s, dims)

    def step(it, acc):
        for u in range(8):
            i = it * 8 + u
            h = i // dims.mh
            off = (i - h * dims.mh) * BLK
            js = [grouped[i * dims.group + c] for c in range(dims.group)]
            lhs = jnp.concatenate([gp_s[j] for j in js], axis=1)
            rhs = jnp.concatenate([up_s[j] for j in js], axis=1)
            gn = dot(lhs, rhs, NT) + dot(gul, small_s[h, :, lanes(dims.ul + off)])
            x = x_s[:, lanes(i * BLK)].astype(F32)
            gain = small_s[h, 0:1, lanes(dims.gain + off)].astype(F32)
            scaled = gn * gain
            gn_s[:, lanes(i * BLK)] = scaled
            gain_s[0:1, lanes(i * BLK)] = jnp.sum(gn * x * r, axis=0, keepdims=True)
            acc = acc + x * scaled
        return acc

    acc = lax.fori_loop(0, dims.model // 8, step, jnp.zeros((rows, BLK), F32))
    shift = jnp.sum(acc, axis=1, keepdims=True) * (1.0 / dims.width) * (r * r * r)
    for i in range(dims.model):
        at = slice(i * BLK, (i + 1) * BLK)
        out_s[:, at] = (
            g_s[:, at].astype(F32) + r * gn_s[:, at] - x_s[:, at].astype(F32) * shift
        ).astype(BF)


def params(mib):
    return pltpu.CompilerParams(vmem_limit_bytes=mib * 1024 * 1024)


def fwd_slot(dims, sc, upo, dno, first, recv, weights, bufs, micro, held):
    rows = recv.shape[0]
    n_buf = 5
    shapes = (
        jax.ShapeDtypeStruct((micro, dims.hidden, held, BLK), BF),
        jax.ShapeDtypeStruct((micro, dims.hidden, held, BLK), BF),
        jax.ShapeDtypeStruct((micro, held, dims.width), BF),
        jax.ShapeDtypeStruct((micro, rows, dims.width), BF),
        jax.ShapeDtypeStruct((micro, held, 2 * BLK), BF),
    )
    n_w = len(weights[0])
    n_in = 5 + 3 * n_w + (n_buf if bufs is not None else 0)

    def kernel(*refs):
        sc, upo, dno, first, recv = refs[:5]
        up_w, dn_w, small_w = (refs[5 + k * n_w : 5 + (k + 1) * n_w] for k in range(3))
        y, hidb, slpb, nrmb, xb, lowb = refs[n_in : n_in + 6]
        up_s, dn_s, small_s, x_s, nrm_s, hid_s, slp_s, low_s, y_s, sems = refs[n_in + 6 :]

        @pl.when(sc[0] == 1)
        def _():
            m, f = sc[1], sc[2]

            @pl.when(sc[3] == 1)
            def _():
                pltpu.make_async_copy(first.at[m], x_s, sems.at[6]).start()

            @pl.when(sc[3] == 0)
            def _():
                pltpu.make_async_copy(recv, x_s, sems.at[6]).start()

            wait_x = pltpu.make_async_copy(recv, x_s, sems.at[6])
            small, up = load_weights(f, (small_w, up_w), (small_s, up_s), sems)
            low_s[...] = jnp.zeros_like(low_s)
            wait_x.wait()
            save_x = pltpu.make_async_copy(x_s, xb.at[m], sems.at[7])
            save_x.start()
            done(small)
            fwd_norm(dims, x_s, small_s, nrm_s, low_s)
            done(up)
            (dn,) = load_weights(f, (dn_w,), (dn_s,), sems, 2)
            low = fwd_hidden(dims, small_s, up_s, upo, nrm_s, hid_s, slp_s, low_s)
            outs = [
                pltpu.make_async_copy(hid_s, hidb.at[m, :, 0:rows], sems.at[9]),
                pltpu.make_async_copy(slp_s, slpb.at[m, :, 0:rows], sems.at[10]),
                pltpu.make_async_copy(nrm_s, nrmb.at[m, 0:rows], sems.at[11]),
                pltpu.make_async_copy(low_s, lowb.at[m, 0:rows], sems.at[12]),
            ]
            for copy in outs:
                copy.start()
            done(dn)
            fwd_down(dims, low, x_s, small_s, dn_s, dno, hid_s, y_s)
            outs.append(pltpu.make_async_copy(y_s, y, sems.at[8]))
            outs[-1].start()
            save_x.wait()
            done(outs)

    args = [sc, upo, dno, first, recv] + [w for pair in weights for w in pair]
    aliases = {}
    if bufs is not None:
        aliases = {len(args) + n: n + 1 for n in range(n_buf)}
        args += list(bufs)
    out = pl.pallas_call(
        kernel,
        out_shape=(jax.ShapeDtypeStruct((rows, dims.width), BF),) + shapes,
        in_specs=[SMEM] * 3 + [ANY] * (len(args) - 3),
        out_specs=(ANY,) * 6,
        input_output_aliases=aliases,
        scratch_shapes=[
            pltpu.VMEM((dims.hidden, BLK, BLK), BF),
            pltpu.VMEM((dims.hidden, BLK, BLK), BF),
            pltpu.VMEM((dims.parts, RANK, dims.packed), BF),
            pltpu.VMEM((rows, dims.width), BF),
            pltpu.VMEM((rows, dims.width), BF),
            pltpu.VMEM((dims.hidden, rows, BLK), BF),
            pltpu.VMEM((dims.hidden, rows, BLK), BF),
            pltpu.VMEM((rows, 2 * BLK), BF),
            pltpu.VMEM((rows, dims.width), BF),
            pltpu.SemaphoreType.DMA((13,)),
        ],
        compiler_params=params(60),
        name="forward_rows",
    )(*args)
    return out[0], out[1:]


def bwd_slot(dims, sc, dno, grouped, last, recv, weights, xb, slpb, bufs, micro, held):
    rows = recv.shape[0]
    n_buf = 4
    shapes = (
        jax.ShapeDtypeStruct((micro, dims.hidden, held, BLK), BF),
        jax.ShapeDtypeStruct((micro, held, dims.width), BF),
        jax.ShapeDtypeStruct((micro, held, 2 * BLK), BF),
        jax.ShapeDtypeStruct((micro, 8, dims.width), F32),
    )
    n_w = len(weights[0])
    n_in = 7 + 3 * n_w + (n_buf if bufs is not None else 0)

    def kernel(*refs):
        sc, dno, grouped, last, recv = refs[:5]
        up_w, dn_w, small_w = (refs[5 + k * n_w : 5 + (k + 1) * n_w] for k in range(3))
        xb, slpb = refs[5 + 3 * n_w : 7 + 3 * n_w]
        out, gpb, gb, lowb, gainb = refs[n_in : n_in + 5]
        up_s, dn_s, small_s, x_s, g_s, slp_s, gp_s, low_s, gn_s, gain_s, out_s, sems = refs[n_in + 5 :]

        @pl.when(sc[0] == 1)
        def _():
            m, f = sc[1], sc[2]

            @pl.when(sc[3] == 1)
            def _():
                pltpu.make_async_copy(last.at[m], g_s, sems.at[6]).start()

            @pl.when(sc[3] == 0)
            def _():
                pltpu.make_async_copy(recv, g_s, sems.at[6]).start()

            wait_g = pltpu.make_async_copy(recv, g_s, sems.at[6])
            get_slope = pltpu.make_async_copy(slpb.at[m, :, 0:rows], slp_s, sems.at[7])
            get_x = pltpu.make_async_copy(xb.at[m], x_s, sems.at[8])
            small, dn = load_weights(f, (small_w, dn_w), (small_s, dn_s), sems)
            get_slope.start()
            low_s[...] = jnp.zeros_like(low_s)
            gain_s[...] = jnp.zeros_like(gain_s)
            wait_g.wait()
            save_g = pltpu.make_async_copy(g_s, gb.at[m, 0:rows], sems.at[9])
            save_g.start()
            done(small)
            get_slope.wait()
            done(dn)
            (up,) = load_weights(f, (up_w,), (up_s,), sems, 2)
            get_x.start()
            gul = bwd_hidden(dims, g_s, slp_s, gp_s, small_s, dn_s, dno, low_s)
            outs = [
                pltpu.make_async_copy(gp_s, gpb.at[m, :, 0:rows], sems.at[10]),
                pltpu.make_async_copy(low_s, lowb.at[m, 0:rows], sems.at[11]),
            ]
            for copy in outs:
                copy.start()
            get_x.wait()
            done(up)
            bwd_input(dims, x_s, g_s, gp_s, small_s, up_s, grouped, gul, gn_s, gain_s, out_s)
            more = [
                pltpu.make_async_copy(gain_s, gainb.at[m], sems.at[12]),
                pltpu.make_async_copy(out_s, out, sems.at[13]),
            ]
            for copy in more:
                copy.start()
            save_g.wait()
            done(outs)
            done(more)

    args = [sc, dno, grouped, last, recv] + [w for pair in weights for w in pair] + [xb, slpb]
    aliases = {}
    if bufs is not None:
        aliases = {len(args) + n: n + 1 for n in range(n_buf)}
        args += list(bufs)
    out = pl.pallas_call(
        kernel,
        out_shape=(jax.ShapeDtypeStruct((rows, dims.width), BF),) + shapes,
        in_specs=[SMEM] * 3 + [ANY] * (len(args) - 3),
        out_specs=(ANY,) * 5,
        input_output_aliases=aliases,
        scratch_shapes=[
            pltpu.VMEM((dims.hidden, BLK, BLK), BF),
            pltpu.VMEM((dims.hidden, BLK, BLK), BF),
            pltpu.VMEM((dims.parts, RANK, dims.packed), BF),
            pltpu.VMEM((rows, dims.width), BF),
            pltpu.VMEM((rows, dims.width), BF),
            pltpu.VMEM((dims.hidden, rows, BLK), BF),
            pltpu.VMEM((dims.hidden, rows, BLK), BF),
            pltpu.VMEM((rows, 2 * BLK), BF),
            pltpu.VMEM((rows, dims.width), F32),
            pltpu.VMEM((8, dims.width), F32),
            pltpu.VMEM((rows, dims.width), BF),
            pltpu.SemaphoreType.DMA((14,)),
        ],
        compiler_params=params(60),
        name="backward_rows",
    )(*args)
    return out[0], out[1:]


def pick_rows(sc, sources, dst, sem, count):
    n = dst.shape[0] // (len(sources[0]) * count)
    places = [(q, t, (q * len(sources[0]) + t) * n) for q in range(count) for t in range(len(sources[0]))]
    for number, triple in enumerate(sources):

        @pl.when(sc[3] == number)
        def _():
            for q, t, at in places:
                pltpu.make_async_copy(triple[t].at[sc[4] + q], dst.at[at : at + n], sem.at[q, t]).start()

    return tuple(
        pltpu.make_async_copy(sources[0][t].at[0], dst.at[at : at + n], sem.at[q, t]) for q, t, at in places
    )


def fwd_far(dims, sc, upo, sources, weights, bufs, count):
    hidb, slpb, nrmb, lowb = bufs
    rows = sources[0][0].shape[1]
    far = rows * len(sources[0])
    n_w, n_t, n_q = len(weights[0]), len(sources[0]), len(sources)
    args = [sc, upo] + list(weights[0]) + list(weights[2]) + [a for triple in sources for a in triple]
    n_plain = len(args)
    args += list(bufs)

    def kernel(*refs):
        sc, upo = refs[:2]
        up_w, small_w = refs[2 : 2 + n_w], refs[2 + n_w : 2 + 2 * n_w]
        base = 2 + 2 * n_w
        srcs = [refs[base + q * n_t : base + (q + 1) * n_t] for q in range(n_q)]
        hidb, slpb, nrmb, lowb = refs[n_plain + 4 : n_plain + 8]
        up_s, small_s, x_s, nrm_s, hid_s, slp_s, low_s, sems, xsem, osems = refs[n_plain + 9 :]

        @pl.when(sc[0] == 1)
        def _():
            m, f = sc[1], sc[2]
            wait_x = pick_rows(sc, srcs, x_s, xsem, count)
            small, up = load_weights(f, (small_w, up_w), (small_s, up_s), sems)
            low_s[...] = jnp.zeros_like(low_s)
            done(wait_x)
            done(small)
            fwd_norm(dims, x_s, small_s, nrm_s, low_s)
            done(up)
            fwd_hidden(dims, small_s, up_s, upo, nrm_s, hid_s, slp_s, low_s, 8)
            at = slice(rows, rows + far)
            outs = []
            for q in range(count):
                mine = slice(q * far, (q + 1) * far)
                outs += [
                    pltpu.make_async_copy(hid_s.at[:, mine], hidb.at[m + q, :, at], osems.at[q, 0]),
                    pltpu.make_async_copy(slp_s.at[:, mine], slpb.at[m + q, :, at], osems.at[q, 1]),
                    pltpu.make_async_copy(nrm_s.at[mine], nrmb.at[m + q, at], osems.at[q, 2]),
                    pltpu.make_async_copy(low_s.at[mine], lowb.at[m + q, at], osems.at[q, 3]),
                ]
            for copy in outs:
                copy.start()
            done(outs)

    return pl.pallas_call(
        kernel,
        out_shape=tuple(jax.ShapeDtypeStruct(b.shape, b.dtype) for b in bufs)
        + (jax.ShapeDtypeStruct((8, BLK), F32),),
        in_specs=[SMEM] * 2 + [ANY] * (len(args) - 2),
        out_specs=(ANY,) * 5,
        input_output_aliases={n_plain + n: n for n in range(4)},
        scratch_shapes=[
            pltpu.VMEM((dims.hidden, BLK, BLK), BF),
            pltpu.VMEM((dims.parts, RANK, dims.packed), BF),
            pltpu.VMEM((count * far, dims.width), BF),
            pltpu.VMEM((count * far, dims.width), BF),
            pltpu.VMEM((dims.hidden, count * far, BLK), BF),
            pltpu.VMEM((dims.hidden, count * far, BLK), BF),
            pltpu.VMEM((count * far, 2 * BLK), BF),
            pltpu.SemaphoreType.DMA((8,)),
            pltpu.SemaphoreType.DMA((count, n_t)),
            pltpu.SemaphoreType.DMA((count, 4)),
        ],
        compiler_params=params(60),
        name="forward_far_rows",
    )(*args)


def bwd_far(dims, sc, dno, sources, weights, slpb, bufs, count):
    rows = sources[0][0].shape[1]
    far = rows * len(sources[0])
    n_w, n_t, n_q = len(weights[0]), len(sources[0]), len(sources)
    args = [sc, dno] + list(weights[1]) + list(weights[2]) + [a for triple in sources for a in triple] + [slpb]
    n_plain = len(args)
    args += list(bufs)

    def kernel(*refs):
        sc, dno = refs[:2]
        dn_w, small_w = refs[2 : 2 + n_w], refs[2 + n_w : 2 + 2 * n_w]
        base = 2 + 2 * n_w
        srcs = [refs[base + q * n_t : base + (q + 1) * n_t] for q in range(n_q)]
        slpb = refs[n_plain - 1]
        gpb, gb, lowb = refs[n_plain + 3 : n_plain + 6]
        dn_s, small_s, g_s, slp_s, gp_s, low_s, sems, gsem, osems = refs[n_plain + 7 :]

        @pl.when(sc[0] == 1)
        def _():
            m, f = sc[1], sc[2]
            at = slice(rows, rows + far)
            wait_g = pick_rows(sc, srcs, g_s, gsem, count)
            small, dn = load_weights(f, (small_w, dn_w), (small_s, dn_s), sems)
            mine = [slice(q * far, (q + 1) * far) for q in range(count)]
            get_slope = [
                pltpu.make_async_copy(slpb.at[m + q, :, at], slp_s.at[:, mine[q]], osems.at[q, 0])
                for q in range(count)
            ]
            for copy in get_slope:
                copy.start()
            low_s[...] = jnp.zeros_like(low_s)
            done(wait_g)
            save_g = [
                pltpu.make_async_copy(g_s.at[mine[q]], gb.at[m + q, at], osems.at[q, 1]) for q in range(count)
            ]
            for copy in save_g:
                copy.start()
            done(small)
            done(dn)
            done(get_slope)
            bwd_hidden(dims, g_s, slp_s, gp_s, small_s, dn_s, dno, low_s, 2)
            outs = []
            for q in range(count):
                outs += [
                    pltpu.make_async_copy(gp_s.at[:, mine[q]], gpb.at[m + q, :, at], osems.at[q, 2]),
                    pltpu.make_async_copy(low_s.at[mine[q]], lowb.at[m + q, at], osems.at[q, 3]),
                ]
            for copy in outs:
                copy.start()
            done(save_g)
            done(outs)

    return pl.pallas_call(
        kernel,
        out_shape=tuple(jax.ShapeDtypeStruct(b.shape, b.dtype) for b in bufs)
        + (jax.ShapeDtypeStruct((8, BLK), F32),),
        in_specs=[SMEM] * 2 + [ANY] * (len(args) - 2),
        out_specs=(ANY,) * 4,
        input_output_aliases={n_plain + n: n for n in range(3)},
        scratch_shapes=[
            pltpu.VMEM((dims.hidden, BLK, BLK), BF),
            pltpu.VMEM((dims.parts, RANK, dims.packed), BF),
            pltpu.VMEM((count * far, dims.width), BF),
            pltpu.VMEM((dims.hidden, count * far, BLK), BF),
            pltpu.VMEM((dims.hidden, count * far, BLK), BF),
            pltpu.VMEM((count * far, 2 * BLK), BF),
            pltpu.SemaphoreType.DMA((8,)),
            pltpu.SemaphoreType.DMA((count, n_t)),
            pltpu.SemaphoreType.DMA((count, 4)),
        ],
        compiler_params=params(60),
        name="backward_far_rows",
    )(*args)


def weight_grads(dims, up, sc, order, blocks, wide, low_a, low_b, gain=None):
    micro, _, held, _ = blocks.shape
    total = micro * held
    group, model, mh, hh = dims.group, dims.model, dims.mh, dims.hh
    U = 4
    two = dims.parts == 2
    hid_at = mh * BLK
    gain_at = hid_at + hh * BLK
    packed = gain_at + (mh * BLK if up else 0)
    VM = pl.BlockSpec(memory_space=pltpu.VMEM)
    a_at, b_at = (0, 0) if up else (BLK, BLK)
    extra = [gain] if up else []

    def kernel(*refs):
        sc, order, blocks, wide, low_a, low_b = refs[:6]
        gain = refs[6] if up else None
        outs_hbm = refs[6 + len(extra) : -6]
        big, small, held_s, wide_s, sems, osems = refs[-6:]
        f = sc[2]
        get_wide = pltpu.make_async_copy(wide, wide_s, osems.at[0])
        get_wide.start()

        def fetch(it, slot, go):
            for u in range(U):
                for c in range(group):
                    j = order[(it * U + u) * group + c]
                    copy = pltpu.make_async_copy(
                        blocks.at[:, j], held_s.at[slot, u * group + c], sems.at[slot, u * group + c]
                    )
                    copy.start() if go else copy.wait()

        fetch(0, 0, True)

        def low_t(ref, at):
            rows = jnp.concatenate([ref[m, :, at : at + BLK] for m in range(micro)], axis=0)
            return rows.astype(F32).T[0:RANK].astype(BF)

        with_blocks, with_wide = low_t(low_a, a_at), low_t(low_b, b_at)
        get_wide.wait()

        def which(h):
            return jnp.where(h == f, 0, 1) if two else h

        def step(it, _):
            slot = lax.rem(it, 2)

            @pl.when(it + 1 < model // U)
            def _():
                fetch(it + 1, 1 - slot, True)

            fetch(it, slot, False)
            for u in range(U):
                i = it * U + u
                h = i // mh
                w = which(h)
                off = i - h * mh
                wi = jnp.concatenate([wide_s[m, :, lanes(i * BLK)] for m in range(micro)], axis=0)
                lhs = jnp.concatenate([wi.T, with_blocks], axis=0)
                rhs = jnp.concatenate(
                    [held_s[slot, u * group + c].reshape(total, BLK) for c in range(group)], axis=1
                )
                res = dot(lhs, rhs)
                for c in range(group):
                    j = order[i * group + c]
                    hj = j // hh
                    wj = which(hj)
                    part = res[:, c * BLK : (c + 1) * BLK]
                    if up:
                        big[wj, j - hj * hh] = part[0:BLK].astype(BF)
                    else:
                        big[w, off * group + c] = part[0:BLK].T.astype(BF)
                    small[wj, :, lanes(hid_at + (j - hj * hh) * BLK)] = part[BLK:].astype(BF)
                small[w, :, lanes(off * BLK)] = dot(with_wide, wi).astype(BF)
                if up:
                    small[w, :, lanes(gain_at + off * BLK)] = jnp.broadcast_to(
                        gain[0:1, lanes(i * BLK)], (RANK, BLK)
                    ).astype(BF)
            return 0

        lax.fori_loop(0, model // U, step, 0)
        outs = []
        for n, src in enumerate((big, small)):
            if two:
                outs.append(pltpu.make_async_copy(src.at[0], outs_hbm[2 * n], osems.at[2 * n]))
                outs.append(pltpu.make_async_copy(src.at[1], outs_hbm[2 * n + 1], osems.at[2 * n + 1]))
            else:
                outs.append(pltpu.make_async_copy(src, outs_hbm[n], osems.at[2 * n]))
        for copy in outs:
            copy.start()
        done(outs)

    lead = () if two else (dims.parts,)
    shapes = [lead + (hh, BLK, BLK), lead + (RANK, packed)]
    shapes = [jax.ShapeDtypeStruct(shape, BF) for shape in shapes for _ in range(2 if two else 1)]
    got = pl.pallas_call(
        kernel,
        out_shape=tuple(shapes),
        in_specs=[SMEM] * 2 + [ANY] * 2 + [VM] * (2 + len(extra)),
        out_specs=(ANY,) * len(shapes),
        scratch_shapes=[
            pltpu.VMEM((dims.parts, hh, BLK, BLK), BF),
            pltpu.VMEM((dims.parts, RANK, packed), BF),
            pltpu.VMEM((2, U * group, micro, held, BLK), BF),
            pltpu.VMEM((micro, held, dims.width), BF),
            pltpu.SemaphoreType.DMA((2, U * group)),
            pltpu.SemaphoreType.DMA((4,)),
        ],
        compiler_params=params(60),
        name="up_gradients" if up else "down_gradients",
    )(sc, order, blocks, wide, low_a, low_b, *extra)
    return [got[0:2], got[2:4]] if two else [got[0:1], got[1:2]]


def orders(up_order, dims):
    at = jnp.arange(dims.hidden, dtype=jnp.int32)
    same = (up_order[:, None] == up_order[None, :]) & (at[None, :] < at[:, None])
    place = up_order * dims.group + jnp.sum(same.astype(jnp.int32), axis=1)
    hit = place[None, :] == at[:, None]
    return jnp.sum(jnp.where(hit, at[None, :], 0), axis=1)


def shards(inputs, cotangent, norm_gain, up_blocks, down_blocks, up_left, up_right, down_left, down_right,
           up_pattern, down_pattern):
    micro, rows, width = inputs.shape
    upo, dno = up_pattern[0], down_pattern[0]
    parts = lax.axis_size("fsdp")
    dims = Dims(width, upo.shape[0], parts)
    n_sec = lax.axis_size("section")
    sec = lax.axis_index("section")
    f = lax.axis_index("fsdp")
    swap = [(0, 1), (1, 0)]
    n_dp = lax.axis_size("dp")
    held = rows * n_dp
    small = jnp.concatenate(
        [up_left[0], down_right[0], up_right[0], down_left[0],
         jnp.broadcast_to(norm_gain, (RANK, norm_gain.shape[1]))], axis=1)

    def whole_layer(own, stacked):
        if parts == 2:
            return (own, lax.ppermute(own, "fsdp", swap))
        return (lax.all_gather(own, "fsdp", axis=0, tiled=not stacked),)

    small_w = whole_layer(small, True)
    up_w = whole_layer(up_blocks[0], False)
    weights = (up_w, whole_layer(down_blocks[0], False), small_w)
    grouped = orders(upo, dims)
    zero = jnp.int32(0)

    def scalars(m, edge):
        live = (m >= 0) & (m < micro)
        return jnp.stack([live.astype(jnp.int32), jnp.clip(m, 0, micro - 1).astype(jnp.int32),
                          f.astype(jnp.int32), edge.astype(jnp.int32), zero, zero, zero, zero])

    def shifted(block, sections, k):
        pairs = [(s * n_dp + d, s * n_dp + (d + k) % n_dp) for s in sections for d in range(n_dp)]
        return lax.ppermute(block, ("section", "dp"), pairs)

    def to_dp(block, sections):
        return tuple(shifted(block, sections, k) for k in range(1, n_dp))

    def flags(live, m, source, index):
        return jnp.stack([jnp.asarray(v).astype(jnp.int32) for v in (live, m, f, source, index, 0, 0, 0)])

    state = {"token": None, "due": []}

    def chained(*arrays):
        due = tuple(v for n, v in state["due"] if n <= 0)
        state["due"] = [(n - 1, v) for n, v in state["due"] if n > 0]
        if state["token"] is not None:
            due = due + (state["token"],)
        if not due:
            return arrays
        out = lax.optimization_barrier(arrays + due)
        return out[: len(arrays)]

    shifts = [1] + list(range(n_dp - 1, 1, -1))
    queue = []

    def send_one(hold):
        if queue:
            store, k, payload, sections = queue.pop(0)
            block, _ = lax.optimization_barrier((payload(), state["token"]))
            store[k] = shifted(block, sections, k)
            state["due"].append((hold, store[k]))

    def enqueue(payload, sections):
        store = {}
        queue.extend((store, k, payload, sections) for k in shifts)
        return store

    fbufs, bbufs = None, None
    frecv = inputs[0]
    brecv = inputs[0]
    last = n_sec - 1
    edge = jnp.where(sec == 0, inputs, cotangent)
    far_edge = enqueue(lambda: edge, (0, last))

    def forward(t):
        nonlocal fbufs, frecv
        (x,) = chained(frecv)
        y, fbufs = fwd_slot(dims, scalars(t - sec, sec == 0), upo, dno, inputs, x, weights, fbufs, micro, held)
        state["token"] = y
        pairs = [(s, s + 1) for s in range(last) if 0 <= t - s < micro]
        if pairs:
            frecv = lax.ppermute(y, "section", pairs)

    def backward(t):
        nonlocal bbufs, brecv
        (g,) = chained(brecv)
        out, bbufs = bwd_slot(dims, scalars(t - (last - sec), sec == last), dno, grouped, cotangent, g,
                              weights, fbufs[3], fbufs[1], bbufs, micro, held)
        state["token"] = out
        pairs = [(last - s, last - s - 1) for s in range(last) if 0 <= t - s < micro]
        if pairs:
            brecv = lax.ppermute(out, "section", pairs)

    def forward_far(m, live, sources, source, index):
        nonlocal fbufs
        (sc,) = chained(flags(live, m, source, index))
        hidb, slpb, nrmb, xb, lowf = fbufs
        hidb, slpb, nrmb, lowf, state["token"] = fwd_far(dims, sc, upo, sources, weights, (hidb, slpb, nrmb, lowf), half)
        fbufs = (hidb, slpb, nrmb, xb, lowf)

    slots = micro + last
    half = micro // 2
    early, late = slice(0, half), slice(half, micro)
    inner, outer = list(range(1, n_sec)), list(range(last))

    def triple(store):
        return tuple(store[k] for k in range(1, n_dp))

    for t in range(slots):
        if t == slots - 1:
            forward_far(0, sec == 0, [triple(far_edge)], 0, 0)
        forward(t)
        if t < last:
            send_one(3)
        if t == slots - 1:
            x_late = enqueue(lambda: fbufs[3][late], inner)
        if t > last + 1:
            send_one(1)
        if t >= last:
            backward(t - last)
        if t == last + 1:
            x_early = enqueue(lambda: fbufs[3][early], inner)
        if t > last:
            send_one(1)
        if t == slots - 1:
            send_one(1)

    for t in range(slots - last, slots):
        backward(t)
        if t == slots - 3:
            g_early = enqueue(lambda: bbufs[1][early, 0:rows], outer)
        if t == slots - 1:
            g_late = enqueue(lambda: bbufs[1][late, 0:rows], outer)
        hold = 2 if t >= slots - 2 else 1
        send_one(hold)
        if t != slots - 2:
            send_one(hold)
        else:
            forward_far(0, sec > 0, [triple(x_early)], 0, 0)
    gpb, gb, lowb, gain_rows = bbufs

    def far_backward(m):
        nonlocal gpb, gb, lowb
        sources = [triple(g_early if m < half else g_late), triple(far_edge)]
        (sc,) = chained(flags(True, m, jnp.where(sec == last, 1, 0), jnp.where(sec == last, m, m % half)))
        gpb, gb, lowb, state["token"] = bwd_far(dims, sc, dno, sources, weights, fbufs[1], (gpb, gb, lowb), half)
        send_one(1)

    forward_far(half, True, [triple(x_late), triple(far_edge)], jnp.where(sec == 0, 1, 0), jnp.where(sec == 0, half, 0))
    send_one(1)
    far_backward(0)
    while queue:
        send_one(2)
    gain = jnp.sum(gain_rows, axis=(0, 1))[None]
    for other in to_dp(gain, range(n_sec)):
        gain = gain + other
    far_backward(half)
    hidb, slpb, nrmb, _, lowf = fbufs
    sc = scalars(zero, sec == 0)

    def over_fsdp(pieces, ahead=()):
        if parts == 2:
            got = lax.ppermute(pieces[1], "fsdp", swap)
            got = lax.optimization_barrier((got, *ahead))[0]
            return (pieces[0].astype(F32) + got.astype(F32))[None]
        return lax.psum_scatter(pieces[0], "fsdp", scatter_dimension=0, tiled=False).astype(F32)[None]

    dn_g, dn_small = weight_grads(dims, False, sc, dno, hidb, gb, lowb, lowf)
    up_g, up_small = weight_grads(dims, True, sc, grouped, gpb, nrmb, lowf, lowb, gain)
    dn, dns = over_fsdp(dn_g), over_fsdp(dn_small)
    up, ups = over_fsdp(up_g, (dn,)), over_fsdp(up_small)
    mw, hw = dims.mh * BLK, dims.hh * BLK
    return (
        ups[:, 0, mw + hw :],
        up,
        dn,
        ups[:, :, 0:mw],
        ups[:, :, mw : mw + hw],
        dns[:, :, mw : mw + hw],
        dns[:, :, 0:mw],
    )


def solution(mesh):
    placed = (
        P(None, ("fsdp", "dp"), None),
        P(None, ("fsdp", "dp"), None),
        P("section", "fsdp"),
        P("section", "fsdp", None, None),
        P("section", "fsdp", None, None),
        P("section", None, "fsdp"),
        P("section", None, "fsdp"),
        P("section", None, "fsdp"),
        P("section", None, "fsdp"),
        P("section", None),
        P("section", None),
    )
    return jax.shard_map(
        shards,
        mesh=mesh,
        in_specs=placed,
        out_specs=(
            P("section", "fsdp"),
            P("section", "fsdp", None, None),
            P("section", "fsdp", None, None),
            P("section", None, "fsdp"),
            P("section", None, "fsdp"),
            P("section", None, "fsdp"),
            P("section", None, "fsdp"),
        ),
        check_vma=False,
    )
```
